32 devices in a mesh: lat: 4 (over z), lon: 8 (over y, x, core).
Axes of the slice: x: 2, y: 2, z: 4, core: 2. Of those that a mesh axis runs over, the one named last changes fastest.
Arguments:
- basis: bfloat16 [131072, 128], P(('lat', 'lon'))
- order: int32 [131072], P(('lat', 'lon')), may hold values from 0 to 4095, as said below
- land: int32 [128, 1024], P('lat', 'lon'), may hold values 0 or 1
- conduct: float32 [128, 1024], P('lat', 'lon'), may hold values from 0.6 to 1
Outputs:
- variance: float32 [128, 1024], P('lat', 'lon')
The draws below stay inside these ranges and needn't reach their ends.
Inputs may be any that keep to these rules, and one draw needn't show every extreme that they name: `order`: each aligned block of 4096 entries starting at a multiple of 4096 holds every number from 0 to 4095 once.
All inputs are finite; a program needn't handle non-finite values. No bound on the sum of `land` on one device may be relied on, other than what follows from the above.
Results may differ from the reference program's by a relative error of at most 0.00053.
Values may be sent and summed in bfloat16 or wider, within the bound.
No kernel may reach another device: no remote copies, remote signals or barrier semaphores. Data moves between devices by JAX's collectives and lax.ppermute only.
A program may use at most 64 MiB of HBM per device.

```python
import jax
import jax.numpy as jnp
from jax import lax

K = 128
TILE_LAT = 32
TILE_LON = 128
SWEEPS = 10
ROWS = 4096
CELLS = 131072
NLAT = 128
NLON = 1024
N_LAT = 4
N_LON = 8


def draw_basis(key, part):
    key = jax.random.fold_in(key, 11)
    key_one, key_two = jax.random.split(key, 2)
    position = jnp.arange(CELLS, dtype=jnp.float32) / CELLS
    column_scale = jnp.exp(jnp.log(30.0) * jnp.arange(K, dtype=jnp.float32) / (K - 1))
    values = jax.random.normal(key_one, (CELLS, K), jnp.float32)
    rough = jax.random.uniform(key_two, (CELLS, 1), jnp.float32, 0.5, 1.5)
    scale = jnp.exp(jnp.log(3.0) * position)[:, None] * rough
    return (values * scale * column_scale[None, :]).astype(jnp.bfloat16)


def draw_order(key, part):
    key = jax.random.fold_in(key, 23)
    keys = jax.random.split(key, CELLS // ROWS)
    dealt = jax.vmap(lambda single: jax.random.permutation(single, ROWS))(keys)
    return dealt.reshape(CELLS).astype(jnp.int32)


def draw_conduct(key, part):
    key = jax.random.fold_in(key, 37)
    values = jnp.exp(jax.random.uniform(key, (NLAT, NLON), jnp.float32, jnp.log(0.6), 0.0))
    return values.astype(jnp.float32)


def with_ends(entries, stream_key, least, high):
    place = [jax.random.randint(jax.random.fold_in(stream_key, axis), (), 0, length) for axis, length in enumerate(entries.shape)]
    longest = entries.shape.index(max(entries.shape))
    next_to = place[:longest] + [(place[longest] + 1) % entries.shape[longest]] + place[longest + 1:]
    return entries.at[tuple(place)].set(least).at[tuple(next_to)].set(high)


def setup_inputs(seed: int = 0) -> dict:
    arg_keys = jax.random.split(jax.random.key(seed), 5)
    basis = draw_basis(jax.random.fold_in(arg_keys[4], 71), 0)
    order = draw_order(jax.random.fold_in(arg_keys[4], 71), 0)
    land = with_ends((jax.random.randint(arg_keys[2], (NLAT, NLON), 0, 20) < 19).astype(jnp.int32), jax.random.fold_in(arg_keys[2], 1), 0, 1)
    conduct = draw_conduct(jax.random.fold_in(arg_keys[4], 71), 0)
    return dict(basis=basis, order=order, land=land, conduct=conduct)


def rotate_rows(rows_in, gram):
    lower = jnp.linalg.cholesky(gram)
    inverse = jax.scipy.linalg.solve_triangular(lower, jnp.eye(gram.shape[0], dtype=jnp.float32), lower=True)
    return jnp.dot(rows_in.astype(jnp.float32), inverse.T.astype(jnp.float32), precision=lax.Precision.HIGHEST, preferred_element_type=jnp.float32).astype(jnp.bfloat16)

def sweep_plane(plane, coef_here, coef_north, coef_south, coef_east, coef_west):
    padded = jnp.pad(plane, ((1, 1), (0, 0)))
    total = plane + 0.124 * (coef_here + coef_north) * (padded[:-2] - plane)
    total = total + 0.124 * (coef_here + coef_south) * (padded[2:] - plane)
    total = total + 0.124 * (coef_here + coef_west) * (jnp.roll(plane, 1, 1) - plane)
    total = total + 0.124 * (coef_here + coef_east) * (jnp.roll(plane, -1, 1) - plane)
    return total

def reference(basis, order, land, conduct):
    blocks = N_LAT * N_LON
    width = basis.shape[1]
    gram = lax.dot_general(basis.astype(jnp.float32), basis.astype(jnp.float32), (((0,), (0,)), ((), ())), preferred_element_type=jnp.float32)
    rotated = rotate_rows(basis, gram)
    stacked = rotated.reshape(blocks, ROWS, width)
    picks = order.reshape(blocks, ROWS).astype(jnp.int32)
    ordered = jnp.take_along_axis(stacked, picks[:, :, None], axis=1)
    share = ROWS // blocks
    dealt = ordered.reshape(blocks, blocks, share, width).transpose(1, 0, 2, 3)
    tiles = dealt.reshape(N_LAT, N_LON, TILE_LAT, TILE_LON, width).transpose(0, 2, 1, 3, 4)
    columns = tiles.reshape(NLAT, NLON, width).transpose(2, 0, 1)
    coefficient = conduct * (0.35 + 0.65 * land.astype(jnp.float32))
    coef_pad = jnp.pad(coefficient, ((1, 1), (0, 0)))
    coef_north = coef_pad[:-2]
    coef_south = coef_pad[2:]
    coef_east = jnp.roll(coefficient, -1, 1)
    coef_west = jnp.roll(coefficient, 1, 1)

    def per_column(total_sq, column):
        plane = column.astype(jnp.float32)
        for step in range(SWEEPS):
            plane = sweep_plane(plane, coefficient, coef_north, coef_south, coef_east, coef_west)
            total_sq = total_sq + plane * plane
        return (total_sq, None)
    total_sq, unused = lax.scan(per_column, jnp.zeros((NLAT, NLON), jnp.float32), columns)
    return total_sq * (CELLS / (width * SWEEPS))
```

```python
import functools

import jax
import jax.numpy as jnp
from jax import lax
from jax.experimental import pallas as pl
from jax.experimental.pallas import tpu as pltpu
from jax.sharding import PartitionSpec as P

SWEEPS = 10
HALO = SWEEPS
LANES = 128
ONE_HOT = 1024
CHUNK = 256
GROUP = 16
STRIP = 64
SIDE = 3 * HALO
VMEM_BYTES = 56 * 1024 * 1024

bf16, f32, i32 = jnp.bfloat16, jnp.float32, jnp.int32


def iota(shape, dim):
    return lax.broadcasted_iota(i32, shape, dim)


def dot(a, b):
    return jnp.dot(a, b, preferred_element_type=f32)


def deal_kernel(basis_ref, order_ref, out_ref, turned):
    rows, width = basis_ref.shape
    parts = rows // ONE_HOT
    for q in range(parts):
        turned[q * width : (q + 1) * width, :] = basis_ref[
            q * ONE_HOT : (q + 1) * ONE_HOT, :
        ].T

    def step(c, carry):
        order = order_ref[pl.ds(c, 1), :]
        within = order % ONE_HOT
        part = order // ONE_HOT
        hot = (iota((ONE_HOT, CHUNK), 0) == within).astype(f32).astype(bf16)
        found = dot(turned[...], hot)
        picked = found[:width]
        for q in range(1, parts):
            picked = jnp.where(part == q, found[q * width : (q + 1) * width], picked)
        picked = picked.astype(bf16)
        for h in range(CHUNK // LANES):
            out_ref[c * (CHUNK // LANES) + h] = picked[:, h * LANES : (h + 1) * LANES]
        return carry

    lax.fori_loop(0, rows // CHUNK, step, 0)


def deal(basis, order):
    rows, width = basis.shape
    return pl.pallas_call(
        deal_kernel,
        out_shape=jax.ShapeDtypeStruct((rows // LANES, width, LANES), bf16),
        scratch_shapes=[pltpu.VMEM((rows // ONE_HOT * width, ONE_HOT), bf16)],
        compiler_params=pltpu.CompilerParams(vmem_limit_bytes=VMEM_BYTES),
        name="deal",
    )(basis, order.reshape(rows // CHUNK, CHUNK))


def rotate_kernel(rows_ref, inverse_ref, field_ref, edge_ref):
    tall, width, lanes = rows_ref.shape
    whole = inverse_ref[...]
    high = whole.astype(bf16)
    rest = whole - high.astype(f32)
    mid = rest.astype(bf16)
    low = (rest - mid.astype(f32)).astype(bf16)
    split = jnp.concatenate([high, mid, low], axis=0)
    for r in range(tall):
        parts = dot(split, rows_ref[r])
        turned = parts[:width] + (parts[width : 2 * width] + parts[2 * width :])
        field_ref[r] = turned.astype(bf16)
    groups = width // GROUP
    column = iota((lanes, 2 * LANES), 0)
    place = iota((lanes, 2 * LANES), 1)
    side, group, offset = place // LANES, (place % LANES) // GROUP, place % GROUP
    wanted = jnp.where(side == 0, offset, lanes - HALO + offset)
    keep = (offset < HALO) & (column == wanted)
    packed = jnp.zeros((tall * GROUP, 2 * LANES), f32)
    for g in range(groups):
        select = (keep & (group == g)).astype(f32).astype(bf16)
        piece = field_ref[:, g * GROUP : (g + 1) * GROUP, :].reshape(tall * GROUP, lanes)
        packed = packed + dot(piece, select)
    packed = packed.astype(bf16)
    edge_ref[0] = packed[:, :LANES].reshape(tall, GROUP, LANES)
    edge_ref[1] = packed[:, LANES:].reshape(tall, GROUP, LANES)


def rotate(rows, inverse):
    tall, width, lanes = rows.shape
    return pl.pallas_call(
        rotate_kernel,
        out_shape=(
            jax.ShapeDtypeStruct(rows.shape, bf16),
            jax.ShapeDtypeStruct((2, tall, GROUP, LANES), bf16),
        ),
        compiler_params=pltpu.CompilerParams(vmem_limit_bytes=VMEM_BYTES),
        name="rotate",
    )(rows, inverse)


def sweep_kernel(
    scale,
    ends_ref,
    north_ref,
    own_ref,
    south_ref,
    left_n_ref,
    left_ref,
    left_s_ref,
    right_n_ref,
    right_ref,
    right_s_ref,
    coef_ref,
    out_ref,
    u_ref,
    across_ref,
    down_ref,
    sum_ref,
):
    tall, width, lanes = own_ref.shape
    rows = tall + 2 * HALO
    main_groups = width // 8
    strip_groups = width // 2 // 8
    chunk = strip_groups
    half = width // 2

    for kind in range(2):
        coef = coef_ref[kind]
        across = 0.124 * (coef + pltpu.roll(coef, lanes - 1, 1))
        below = jnp.concatenate([coef[1:], coef[:1]], axis=0)
        down = 0.124 * (coef + below)
        across_ref[kind] = jnp.broadcast_to(across[:, None, :], (rows, 8, lanes))
        down_ref[kind] = jnp.broadcast_to(down[:, None, :], (rows, 8, lanes))
    sum_ref[...] = jnp.zeros_like(sum_ref)

    source = iota((2 * lanes, lanes), 0)
    place = iota((2 * lanes, lanes), 1)
    group, m = place // STRIP, place % STRIP
    from_half, column = source // lanes, source % lanes
    left_part = (m >= HALO) & (m < SIDE) & (column == m - HALO)
    right_part = (m >= SIDE) & (m < 2 * SIDE - HALO) & (column == m - SIDE + lanes - 2 * HALO)
    inner = ((group == from_half) & (left_part | right_part)).astype(f32).astype(bf16)
    halves = half // GROUP
    outers = []
    for gg in range(halves):
        slot = (group * halves + gg) * GROUP
        left_halo = (from_half == 0) & (m < HALO) & (column == slot + m)
        right_halo = (
            (from_half == 1)
            & (m >= 2 * SIDE - HALO)
            & (m < 2 * SIDE)
            & (column == slot + m - (2 * SIDE - HALO))
        )
        outers.append((left_halo | right_halo).astype(f32).astype(bf16))

    def fill(row, field, left, right):
        u_ref[row, :main_groups] = field.astype(f32).reshape(main_groups, 8, lanes)
        strip = dot(jnp.concatenate([field[:half], field[half:]], axis=1), inner)
        edge = jnp.concatenate([left, right], axis=1)
        outer = jnp.concatenate([dot(edge, o) for o in outers], axis=0)
        u_ref[row, main_groups:] = (strip + outer).reshape(strip_groups, 8, lanes)

    def fill_north(r, carry):
        fill(r, north_ref[r], left_n_ref[r], right_n_ref[r])
        fill(r + HALO + tall, south_ref[r], left_s_ref[r], right_s_ref[r])
        return carry

    def fill_own(r, carry):
        fill(r + HALO, own_ref[r], left_ref[r], right_ref[r])
        return carry

    lax.fori_loop(0, HALO, fill_north, 0)
    lax.fori_loop(0, tall, fill_own, 0)

    def sweep(s, carry):
        first = s + 1
        for c in range((main_groups + strip_groups) // chunk):
            kind = (c * chunk) // main_groups
            part = pl.ds(c * chunk, chunk)
            start = u_ref[first, part]
            above = down_ref[kind, first - 1] * (start - u_ref[first - 1, part])

            def one(row, here, above):
                below = u_ref[row + 1, part]
                under = down_ref[kind, row] * (below - here)
                east = pltpu.roll(here, lanes - 1, 2)
                flux = across_ref[kind, row] * (east - here)
                new = here + (under - above) + (flux - pltpu.roll(flux, 1, 2))
                u_ref[row, part] = new
                sum_ref[c, row] += jnp.sum(new * new, axis=0)
                return below, under

            def pair(p, state):
                row = first + 2 * p
                state = one(row, *state)
                return one(row + 1, *state)

            lax.fori_loop(0, (rows - 2 * first) // 2, pair, (start, above))

        @pl.when(ends_ref[0] == 1)
        def _():
            u_ref[HALO - 1] = jnp.zeros(u_ref.shape[1:], f32)

        @pl.when(ends_ref[1] == 1)
        def _():
            u_ref[HALO + tall] = jnp.zeros(u_ref.shape[1:], f32)

        return carry

    lax.fori_loop(0, SWEEPS, sweep, 0)

    inside = pl.ds(HALO, tall)
    middle = jnp.sum(sum_ref[0, inside] + sum_ref[1, inside], axis=1)
    strip = jnp.sum(sum_ref[2, inside], axis=1)
    strip = strip + pltpu.roll(strip, STRIP, 1)
    at = iota((tall, lanes), 1)
    left = pltpu.roll(strip, lanes - HALO, 1)
    right = pltpu.roll(strip, lanes - (2 * SIDE - HALO), 1)
    total = jnp.where(at < HALO, left, jnp.where(at >= lanes - HALO, right, middle))
    out_ref[...] = total * scale


def sweeps(scale, ends, fields, coef):
    own = fields[1]
    tall, width, lanes = own.shape
    rows = tall + 2 * HALO
    groups = (width + width // 2) // 8
    vmem = pl.BlockSpec(memory_space=pltpu.VMEM)
    return pl.pallas_call(
        functools.partial(sweep_kernel, scale),
        out_shape=jax.ShapeDtypeStruct((tall, lanes), f32),
        in_specs=[pl.BlockSpec(memory_space=pltpu.SMEM)] + [vmem] * (len(fields) + 1),
        out_specs=vmem,
        scratch_shapes=[
            pltpu.VMEM((rows, groups, 8, lanes), f32),
            pltpu.VMEM((2, rows, 8, lanes), f32),
            pltpu.VMEM((2, rows, 8, lanes), f32),
            pltpu.VMEM((3, rows, 8, lanes), f32),
        ],
        compiler_params=pltpu.CompilerParams(vmem_limit_bytes=VMEM_BYTES),
        name="sweeps",
    )(ends, *fields, coef)


def from_before(x, axis, closed):
    count = lax.axis_size(axis)
    return lax.ppermute(
        x, axis, [(i, (i + 1) % count) for i in range(count if closed else count - 1)]
    )


def from_after(x, axis, closed):
    count = lax.axis_size(axis)
    return lax.ppermute(
        x, axis, [((i + 1) % count, i) for i in range(count if closed else count - 1)]
    )


def summed(partial, axes, count):
    rows, width = partial.shape
    share = rows // count
    pieces = lax.all_to_all(partial, axes, split_axis=0, concat_axis=0, tiled=True)
    mine = jnp.sum(pieces.reshape(count, share, width), axis=0)
    copies = jnp.broadcast_to(mine[None], (count, share, width)).reshape(rows, width)
    return lax.all_to_all(copies, axes, split_axis=0, concat_axis=0, tiled=True)


def per_device(basis, order, land, conduct):
    axes = ("lat", "lon")
    rows_here, width = basis.shape
    tall, wide = land.shape
    count = lax.axis_size("lat") * lax.axis_size("lon")
    cells = rows_here * count
    share = rows_here // count

    partial = lax.dot_general(
        basis, basis, (((0,), (0,)), ((), ())), preferred_element_type=f32
    )
    gram = summed(partial, axes, count)

    dealt = deal(basis, order)
    split = LANES // share
    outgoing = dealt.reshape(-1, width, split, share).transpose(0, 2, 1, 3)
    outgoing = outgoing.reshape(count, width, share)
    arrived = lax.all_to_all(outgoing, axes, split_axis=0, concat_axis=0, tiled=True)
    raw = arrived.reshape(tall, wide // share, width, share).transpose(0, 2, 1, 3)
    raw = raw.reshape(tall, width, wide)

    lower = jnp.linalg.cholesky(gram)
    inverse = jax.scipy.linalg.solve_triangular(lower, jnp.eye(width, dtype=f32), lower=True)
    field, edges = rotate(raw, inverse)

    north = from_before(field[-HALO:], "lat", False)
    south = from_after(field[:HALO], "lat", False)
    left = from_before(edges[1], "lon", True)
    right = from_after(edges[0], "lon", True)
    left_n = from_before(left[-HALO:], "lat", False)
    left_s = from_after(left[:HALO], "lat", False)
    right_n = from_before(right[-HALO:], "lat", False)
    right_s = from_after(right[:HALO], "lat", False)

    coef = conduct * (0.35 + 0.65 * land.astype(f32))
    coef = jnp.concatenate(
        [from_before(coef[:, -HALO:], "lon", True), coef, from_after(coef[:, :HALO], "lon", True)],
        axis=1,
    )
    coef = jnp.concatenate(
        [from_before(coef[-HALO:], "lat", False), coef, from_after(coef[:HALO], "lat", False)],
        axis=0,
    )
    strip = jnp.concatenate([coef[:, :SIDE], coef[:, -SIDE:]], axis=1)
    strip = jnp.pad(strip, ((0, 0), (0, STRIP - 2 * SIDE)))
    coef = jnp.stack([coef[:, HALO:-HALO], jnp.concatenate([strip, strip], axis=1)])

    at = lax.axis_index("lat")
    ends = jnp.stack([at == 0, at == lax.axis_size("lat") - 1]).astype(i32)
    fields = (north, field, south, left_n, left, left_s, right_n, right, right_s)
    return sweeps(cells / (width * SWEEPS), ends, fields, coef)


def solution(mesh):
    in_specs = (P(("lat", "lon"), None), P(("lat", "lon")), P("lat", "lon"), P("lat", "lon"))
    out_specs = P("lat", "lon")
    return jax.shard_map(
        per_device, mesh=mesh, in_specs=in_specs, out_specs=out_specs, check_vma=False
    )
```

```python
import functools

import jax
import jax.numpy as jnp
from jax import lax
from jax.experimental import pallas as pl
from jax.experimental.pallas import tpu as pltpu
from jax.sharding import PartitionSpec as P

SWEEPS = 10
HALO = SWEEPS
LANES = 128
SUB = 8
ONE_HOT = 1024
BLOCK = 4
VMEM_BYTES = 56 * 1024 * 1024

bf16, f32, i32 = jnp.bfloat16, jnp.float32, jnp.int32


def iota(shape, dim):
    return lax.broadcasted_iota(i32, shape, dim)


def dot(a, b):
    return jnp.dot(a, b, preferred_element_type=f32)


def split3(x):
    high = x.astype(bf16)
    rest = x - high.astype(f32)
    mid = rest.astype(bf16)
    low = (rest - mid.astype(f32)).astype(bf16)
    return high, mid, low


def slots(wide):
    return -(-(wide + 2 * HALO) // SUB) * SUB


def circle(own, right, left, axis):
    wide = own.shape[axis]
    count = slots(wide)
    gap = list(own.shape)
    gap[axis] = count - wide - 2 * HALO
    around = jnp.concatenate([own, right, jnp.zeros(gap, own.dtype), left], axis=axis)
    shape = around.shape
    around = around.reshape(shape[:axis] + (SUB, count // SUB) + shape[axis + 1 :])
    return jnp.swapaxes(around, axis, axis + 1).reshape(shape)


def deal_kernel(basis_ref, order_ref, out_ref, hot_ref):
    rows, width = basis_ref.shape
    parts = rows // ONE_HOT
    blocks = order_ref.shape[0]
    lane = iota((LANES, LANES), 1)

    def mark(c, carry):
        order = jnp.broadcast_to(order_ref[pl.ds(c, 1), :], (LANES, LANES)).T
        within = order % ONE_HOT
        for b in range(ONE_HOT // LANES):
            hot = (within == lane + b * LANES).astype(f32).astype(bf16)
            hot_ref[pl.ds(c * LANES, LANES), b * LANES : (b + 1) * LANES] = hot
        return carry

    lax.fori_loop(0, blocks, mark, 0)
    stacked = jnp.concatenate(
        [basis_ref[q * ONE_HOT : (q + 1) * ONE_HOT, :] for q in range(parts)], axis=1
    )
    per_step = 2

    def pick(c, carry):
        found = dot(hot_ref[pl.ds(c * per_step * LANES, per_step * LANES), :], stacked)
        for h in range(per_step):
            at = c * per_step + h
            part = jnp.broadcast_to(order_ref[pl.ds(at, 1), :], (LANES, LANES)).T // ONE_HOT
            here = found[h * LANES : (h + 1) * LANES]
            picked = here[:, :width]
            for q in range(1, parts):
                picked = jnp.where(part == q, here[:, q * width : (q + 1) * width], picked)
            out_ref[pl.ds(at * LANES, LANES), :] = picked.astype(bf16)
        return carry

    lax.fori_loop(0, blocks // per_step, pick, 0)


def deal(basis, order):
    rows, width = basis.shape
    total = order.size
    return pl.pallas_call(
        deal_kernel,
        out_shape=jax.ShapeDtypeStruct((total, width), bf16),
        scratch_shapes=[pltpu.VMEM((total, ONE_HOT), bf16)],
        compiler_params=pltpu.CompilerParams(vmem_limit_bytes=VMEM_BYTES),
        name="deal",
    )(basis, order.reshape(total // LANES, LANES))


def sweep_kernel(
    scale, ends_ref, north_ref, own_ref, south_ref, inverse_ref, coef_ref, out_ref,
    first_ref, second_ref, across_ref, down_ref, sum_ref,
):
    tall = own_ref.shape[0]
    rows, groups = first_ref.shape[:2]
    lanes = first_ref.shape[3]
    places = groups * SUB

    spread = second_ref
    turned = coef_ref[...].T
    depth = turned.shape[1]
    pieces = jnp.concatenate(split3(turned[:places]), axis=1)
    per_step = 4

    def put(c, carry):
        row = iota((3 * depth, per_step * lanes), 0) % depth
        wanted = c * per_step + iota((3 * depth, per_step * lanes), 1) // lanes
        values = dot(pieces, (row == wanted).astype(f32).astype(bf16))
        for h in range(per_step):
            spread[c * per_step + h] = values[:, h * lanes : (h + 1) * lanes].reshape(
                groups, SUB, lanes
            )
        return carry

    lax.fori_loop(0, rows // per_step, put, 0)

    def weigh(r, carry):
        for g in range(groups):
            here = spread[r, g]
            east = spread[r, g + 1] if g + 1 < groups else pltpu.roll(spread[r, 0], SUB - 1, 0)
            across_ref[r, g] = 0.124 * (here + east)
            down_ref[r, g] = 0.124 * (here + spread[r + 1, g])
        return carry

    lax.fori_loop(0, rows - 1, weigh, 0)
    sum_ref[...] = jnp.zeros_like(sum_ref)

    turn = jnp.concatenate(split3(inverse_ref[...].T), axis=1)

    def rotate(source, start, take, offset):
        raw = source[pl.ds(start, take)].astype(f32).reshape(take * places, lanes).astype(bf16)
        parts = dot(raw, turn)
        field = parts[:, :lanes] + (parts[:, lanes : 2 * lanes] + parts[:, 2 * lanes :])
        field = field.astype(bf16).astype(f32)
        first_ref[pl.ds(start + offset, take)] = field.reshape(take, groups, SUB, lanes)

    def rotate_own(c, carry):
        rotate(own_ref, c * 4, 4, HALO)
        return carry

    def rotate_halo(c, carry):
        rotate(north_ref, c * 2, 2, 0)
        rotate(south_ref, c * 2, 2, HALO + tall)
        return carry

    lax.fori_loop(0, tall // 4, rotate_own, 0)
    lax.fori_loop(0, HALO // 2, rotate_halo, 0)

    def update(src, dst, row, take, kept):
        last = groups - 1
        west = []
        closing = []
        for r in range(take):
            here = src[row + r, last]
            east = pltpu.roll(src[row + r, 0], SUB - 1, 0)
            flux = across_ref[row + r, last] * (east - here)
            closing.append(flux)
            west.append(pltpu.roll(flux, 1, 0))
        here = [src[row + r, 0] for r in range(take)]
        for g in range(groups):
            above = down_ref[row - 1, g] * (here[0] - src[row - 1, g])
            following = []
            for r in range(take):
                below = here[r + 1] if r + 1 < take else src[row + take, g]
                under = down_ref[row + r, g] * (below - here[r])
                if g < last:
                    east = src[row + r, g + 1]
                    following.append(east)
                    flux = across_ref[row + r, g] * (east - here[r])
                else:
                    flux = closing[r]
                new = here[r] + ((under - above) + (flux - west[r]))
                dst[row + r, g] = new
                if kept:
                    sum_ref[row + r - HALO, g] += new * new
                above = under
                west[r] = flux
            here = following

    def sweep(s, src, dst):
        def inside(c, carry):
            update(src, dst, HALO + c * BLOCK, BLOCK, True)
            return carry

        def outside(r, carry):
            update(src, dst, r, 1, False)
            update(src, dst, rows - 1 - r, 1, False)
            return carry

        lax.fori_loop(0, tall // BLOCK, inside, 0)
        lax.fori_loop(s + 1, HALO, outside, 0)

        @pl.when(ends_ref[0] == 1)
        def _():
            dst[HALO - 1] = jnp.zeros(dst.shape[1:], f32)

        @pl.when(ends_ref[1] == 1)
        def _():
            dst[HALO + tall] = jnp.zeros(dst.shape[1:], f32)

    def two(t, carry):
        sweep(2 * t, first_ref, second_ref)
        sweep(2 * t + 1, second_ref, first_ref)
        return carry

    lax.fori_loop(0, SWEEPS // 2, two, 0)

    lane = iota((SUB, lanes), 1)

    def gather(r, totals):
        kept = []
        for g in range(groups):
            total = jnp.sum(sum_ref[r, g], axis=1, keepdims=True)
            kept.append(jnp.where(lane == r, total, totals[g]))
        return tuple(kept)

    totals = lax.fori_loop(
        0, tall, gather, tuple(jnp.zeros((SUB, lanes), f32) for _ in range(groups))
    )
    totals = jnp.concatenate(totals, axis=0).T[:tall]
    slot = iota((places, out_ref.shape[1]), 0)
    column = iota((places, out_ref.shape[1]), 1)
    back = (column == (slot % SUB) * groups + slot // SUB).astype(f32).astype(bf16)
    high, mid, low = split3(totals)
    out_ref[...] = (dot(high, back) + (dot(mid, back) + dot(low, back))) * scale


def sweeps(scale, ends, fields, inverse, coef, wide):
    own = fields[1]
    tall, places, lanes = own.shape
    rows = tall + 2 * HALO
    coef = jnp.pad(coef, ((0, 64 - rows), (0, 2 * LANES - places)))
    vmem = pl.BlockSpec(memory_space=pltpu.VMEM)
    grid_rows = (rows, places // SUB, SUB, lanes)
    return pl.pallas_call(
        functools.partial(sweep_kernel, scale),
        out_shape=jax.ShapeDtypeStruct((tall, wide), f32),
        in_specs=[pl.BlockSpec(memory_space=pltpu.SMEM)] + [vmem] * (len(fields) + 2),
        out_specs=vmem,
        scratch_shapes=[
            pltpu.VMEM(grid_rows, f32),
            pltpu.VMEM(grid_rows, f32),
            pltpu.VMEM(grid_rows, f32),
            pltpu.VMEM(grid_rows, f32),
            pltpu.VMEM((tall,) + grid_rows[1:], f32),
        ],
        compiler_params=pltpu.CompilerParams(vmem_limit_bytes=VMEM_BYTES),
        name="sweeps",
    )(ends, *fields, inverse, coef)


def from_before(x, axis, closed):
    count = lax.axis_size(axis)
    return lax.ppermute(
        x, axis, [(i, (i + 1) % count) for i in range(count if closed else count - 1)]
    )


def from_after(x, axis, closed):
    count = lax.axis_size(axis)
    return lax.ppermute(
        x, axis, [((i + 1) % count, i) for i in range(count if closed else count - 1)]
    )


def summed(partial, axes, count):
    rows, width = partial.shape
    share = rows // count
    pieces = lax.all_to_all(partial, axes, split_axis=0, concat_axis=0, tiled=True)
    mine = jnp.sum(pieces.reshape(count, share, width), axis=0)
    copies = jnp.broadcast_to(mine[None], (count, share, width)).reshape(rows, width)
    return lax.all_to_all(copies, axes, split_axis=0, concat_axis=0, tiled=True)


def dealt_rows(basis, order, tall, wide, axes, count):
    width = basis.shape[1]
    share = order.size // count
    if share == wide:
        order = order.reshape(lax.axis_size("lat"), lax.axis_size("lon"), wide)
        right = jnp.roll(order, -1, axis=1)[:, :, :HALO]
        left = jnp.roll(order, 1, axis=1)[:, :, -HALO:]
        moving = deal(basis, circle(order, right, left, 2))
        arrived = lax.all_to_all(moving, axes, split_axis=0, concat_axis=0, tiled=True)
        return arrived.reshape(tall, slots(wide), width)
    arrived = lax.all_to_all(basis[order], axes, split_axis=0, concat_axis=0, tiled=True)
    own = arrived.reshape(tall, wide, width)
    left = from_before(own[:, -HALO:], "lon", True)
    right = from_after(own[:, :HALO], "lon", True)
    return circle(own, right, left, 1)


def per_device(basis, order, land, conduct):
    axes = ("lat", "lon")
    rows_here, width = basis.shape
    tall, wide = land.shape
    count = lax.axis_size("lat") * lax.axis_size("lon")
    cells = rows_here * count

    partial = lax.dot_general(
        basis, basis, (((0,), (0,)), ((), ())), preferred_element_type=f32
    )
    gram = summed(partial, axes, count)
    raw = dealt_rows(basis, order, tall, wide, axes, count)
    north = from_before(raw[-HALO:], "lat", False)
    south = from_after(raw[:HALO], "lat", False)

    lower = jnp.linalg.cholesky(gram)
    inverse = jax.scipy.linalg.solve_triangular(lower, jnp.eye(width, dtype=f32), lower=True)

    coef = conduct * (0.35 + 0.65 * land.astype(f32))
    coef = circle(
        coef,
        from_after(coef[:, :HALO], "lon", True),
        from_before(coef[:, -HALO:], "lon", True),
        1,
    )
    coef = jnp.concatenate(
        [from_before(coef[-HALO:], "lat", False), coef, from_after(coef[:HALO], "lat", False)],
        axis=0,
    )
    at = lax.axis_index("lat")
    ends = jnp.stack([at == 0, at == lax.axis_size("lat") - 1]).astype(i32)
    scale = cells / (width * SWEEPS)
    return sweeps(scale, ends, (north, raw, south), inverse, coef, wide)


def solution(mesh):
    in_specs = (P(("lat", "lon"), None), P(("lat", "lon")), P("lat", "lon"), P("lat", "lon"))
    out_specs = P("lat", "lon")
    return jax.shard_map(
        per_device, mesh=mesh, in_specs=in_specs, out_specs=out_specs, check_vma=False
    )
```

```python
import functools

import jax
import jax.numpy as jnp
from jax import lax
from jax.experimental import pallas as pl
from jax.experimental.pallas import tpu as pltpu
from jax.sharding import PartitionSpec as P

SWEEPS = 10
HALO = SWEEPS
LANES = 128
SUB = 8
ONE_HOT = 1024
BLOCK = 4
VMEM_BYTES = 56 * 1024 * 1024

bf16, f32, i32 = jnp.bfloat16, jnp.float32, jnp.int32


def iota(shape, dim):
    return lax.broadcasted_iota(i32, shape, dim)


def dot(a, b):
    return jnp.dot(a, b, preferred_element_type=f32)


def split3(x):
    high = x.astype(bf16)
    rest = x - high.astype(f32)
    mid = rest.astype(bf16)
    low = (rest - mid.astype(f32)).astype(bf16)
    return high, mid, low


def slots(wide):
    return -(-(wide + 2 * HALO) // SUB) * SUB


def circle(own, right, left, axis):
    wide = own.shape[axis]
    count = slots(wide)
    gap = list(own.shape)
    gap[axis] = count - wide - 2 * HALO
    around = jnp.concatenate([own, right, jnp.zeros(gap, own.dtype), left], axis=axis)
    shape = around.shape
    around = around.reshape(shape[:axis] + (SUB, count // SUB) + shape[axis + 1 :])
    return jnp.swapaxes(around, axis, axis + 1).reshape(shape)


def deal_kernel(basis_ref, order_ref, out_ref):
    rows, width = basis_ref.shape
    parts = rows // ONE_HOT
    blocks = order_ref.shape[0]
    lane = iota((LANES, LANES), 1)
    stacked = jnp.concatenate(
        [basis_ref[q * ONE_HOT : (q + 1) * ONE_HOT, :] for q in range(parts)], axis=1
    )

    def pick(start, take):
        marks, part = [], []
        for h in range(take):
            order = jnp.broadcast_to(order_ref[pl.ds(start + h, 1), :], (LANES, LANES)).T
            within = order & (ONE_HOT - 1)
            part.append(order - within)
            marks.append(
                jnp.concatenate(
                    [
                        (within == lane + b * LANES).astype(f32).astype(bf16)
                        for b in range(ONE_HOT // LANES)
                    ],
                    axis=1,
                )
            )
        found = dot(jnp.concatenate(marks, axis=0), stacked)
        for h in range(take):
            here = found[h * LANES : (h + 1) * LANES]
            picked = here[:, :width]
            for q in range(1, parts):
                chosen = part[h] == q * ONE_HOT
                picked = jnp.where(chosen, here[:, q * width : (q + 1) * width], picked)
            out_ref[pl.ds((start + h) * LANES, LANES), :] = picked.astype(bf16)

    take = 4

    def step(c, carry):
        pick(c * take, take)
        return carry

    lax.fori_loop(0, blocks // take, step, 0)
    if blocks % take:
        pick(blocks - blocks % take, blocks % take)


def deal(basis, order):
    rows, width = basis.shape
    total = order.size
    return pl.pallas_call(
        deal_kernel,
        out_shape=jax.ShapeDtypeStruct((total, width), bf16),
        compiler_params=pltpu.CompilerParams(vmem_limit_bytes=VMEM_BYTES),
        cost_estimate=pl.CostEstimate(
            flops=2 * total * rows * width, bytes_accessed=4 * total * width, transcendentals=0
        ),
        name="deal",
    )(basis, order.reshape(total // LANES, LANES))


def inverse_kernel(gram_ref, out_ref):
    size = gram_ref.shape[0]
    tiles = [gram_ref[t * SUB : (t + 1) * SUB, :] for t in range(size // SUB)]
    lane = iota((SUB, size), 1)
    sub = iota((SUB, size), 0)
    pivots = [jnp.zeros((SUB, size), f32) for _ in tiles]
    for j in range(size):
        top, at = j // SUB, j % SUB
        is_lane = lane == j
        row = jnp.broadcast_to(tiles[top][at : at + 1, :], (SUB, size))
        columns = [
            jnp.broadcast_to(tiles[t][:, j : j + 1], (SUB, size)) for t in range(top, len(tiles))
        ]
        pivot = jnp.broadcast_to(columns[0][at : at + 1, :], (SUB, size))
        scaled = jnp.where(is_lane, 1.0, row) * (1.0 / pivot)
        pivots[top] = jnp.where(sub == at, pivot, pivots[top])
        for t in range(top, len(tiles)):
            rest = jnp.where(is_lane, 0.0, tiles[t]) - columns[t - top] * scaled
            if t == top:
                rest = jnp.where(sub > at, rest, jnp.where(is_lane & (sub == at), 1.0, tiles[t]))
            tiles[t] = rest
    for t in range(len(tiles)):
        kept = jnp.where(lane <= sub + t * SUB, tiles[t], 0.0)
        out_ref[t * SUB : (t + 1) * SUB, :] = kept * (1.0 / jnp.sqrt(pivots[t]))


def factor_inverse(gram):
    size = gram.shape[0]
    return pl.pallas_call(
        inverse_kernel,
        out_shape=jax.ShapeDtypeStruct(gram.shape, f32),
        compiler_params=pltpu.CompilerParams(vmem_limit_bytes=VMEM_BYTES),
        cost_estimate=pl.CostEstimate(
            flops=4 * size**4, bytes_accessed=8 * size * size, transcendentals=0
        ),
        name="factor_inverse",
    )(gram)


def sweep_kernel(
    scale, ends_ref, north_ref, own_ref, south_ref, inverse_ref, coef_ref, out_ref,
    first_ref, second_ref, across_ref, down_ref, sum_ref,
):
    tall = own_ref.shape[0]
    rows, groups = first_ref.shape[:2]
    lanes = first_ref.shape[3]
    places = groups * SUB

    spread = second_ref
    turned = coef_ref[...].T
    depth = turned.shape[1]
    pieces = jnp.concatenate(split3(turned[:places]), axis=1)
    per_step = 4

    def put(c, carry):
        row = iota((3 * depth, per_step * lanes), 0) % depth
        wanted = c * per_step + iota((3 * depth, per_step * lanes), 1) // lanes
        values = dot(pieces, (row == wanted).astype(f32).astype(bf16))
        for h in range(per_step):
            spread[c * per_step + h] = values[:, h * lanes : (h + 1) * lanes].reshape(
                groups, SUB, lanes
            )
        return carry

    lax.fori_loop(0, rows // per_step, put, 0)

    def weigh(r, carry):
        for g in range(groups):
            here = spread[r, g]
            east = spread[r, g + 1] if g + 1 < groups else pltpu.roll(spread[r, 0], SUB - 1, 0)
            across_ref[r, g] = 0.124 * (here + east)
            down_ref[r, g] = 0.124 * (here + spread[r + 1, g])
        return carry

    lax.fori_loop(0, rows - 1, weigh, 0)
    sum_ref[...] = jnp.zeros_like(sum_ref)

    turn = jnp.concatenate(split3(inverse_ref[...].T), axis=1)

    def rotate(source, start, take, offset):
        raw = source[pl.ds(start, take)].astype(f32).reshape(take * places, lanes).astype(bf16)
        parts = dot(raw, turn)
        field = parts[:, :lanes] + (parts[:, lanes : 2 * lanes] + parts[:, 2 * lanes :])
        field = field.astype(bf16).astype(f32)
        first_ref[pl.ds(start + offset, take)] = field.reshape(take, groups, SUB, lanes)

    def rotate_own(c, carry):
        rotate(own_ref, c * 4, 4, HALO)
        return carry

    def rotate_halo(c, carry):
        rotate(north_ref, c * 2, 2, 0)
        rotate(south_ref, c * 2, 2, HALO + tall)
        return carry

    lax.fori_loop(0, tall // 4, rotate_own, 0)
    lax.fori_loop(0, HALO // 2, rotate_halo, 0)

    def update(src, dst, row, take, kept):
        last = groups - 1
        west = []
        closing = []
        for r in range(take):
            here = src[row + r, last]
            east = pltpu.roll(src[row + r, 0], SUB - 1, 0)
            flux = across_ref[row + r, last] * (east - here)
            closing.append(flux)
            west.append(pltpu.roll(flux, 1, 0))
        here = [src[row + r, 0] for r in range(take)]
        for g in range(groups):
            above = down_ref[row - 1, g] * (here[0] - src[row - 1, g])
            following = []
            for r in range(take):
                below = here[r + 1] if r + 1 < take else src[row + take, g]
                under = down_ref[row + r, g] * (below - here[r])
                if g < last:
                    east = src[row + r, g + 1]
                    following.append(east)
                    flux = across_ref[row + r, g] * (east - here[r])
                else:
                    flux = closing[r]
                new = here[r] + ((under - above) + (flux - west[r]))
                dst[row + r, g] = new
                if kept:
                    sum_ref[row + r - HALO, g] += new * new
                above = under
                west[r] = flux
            here = following

    def sweep(s, src, dst):
        def inside(c, carry):
            update(src, dst, HALO + c * BLOCK, BLOCK, True)
            return carry

        def outside(r, carry):
            update(src, dst, r, 1, False)
            update(src, dst, rows - 1 - r, 1, False)
            return carry

        lax.fori_loop(0, tall // BLOCK, inside, 0)
        lax.fori_loop(s + 1, HALO, outside, 0)

        @pl.when(ends_ref[0] == 1)
        def _():
            dst[HALO - 1] = jnp.zeros(dst.shape[1:], f32)

        @pl.when(ends_ref[1] == 1)
        def _():
            dst[HALO + tall] = jnp.zeros(dst.shape[1:], f32)

    def two(t, carry):
        sweep(2 * t, first_ref, second_ref)
        sweep(2 * t + 1, second_ref, first_ref)
        return carry

    lax.fori_loop(0, SWEEPS // 2, two, 0)

    lane = iota((SUB, lanes), 1)

    def gather(r, totals):
        kept = []
        for g in range(groups):
            total = jnp.sum(sum_ref[r, g], axis=1, keepdims=True)
            kept.append(jnp.where(lane == r, total, totals[g]))
        return tuple(kept)

    totals = lax.fori_loop(
        0, tall, gather, tuple(jnp.zeros((SUB, lanes), f32) for _ in range(groups))
    )
    totals = jnp.concatenate(totals, axis=0).T[:tall]
    slot = iota((places, out_ref.shape[1]), 0)
    column = iota((places, out_ref.shape[1]), 1)
    back = (column == (slot % SUB) * groups + slot // SUB).astype(f32).astype(bf16)
    high, mid, low = split3(totals)
    out_ref[...] = (dot(high, back) + (dot(mid, back) + dot(low, back))) * scale


def sweeps(scale, ends, fields, inverse, coef, wide):
    own = fields[1]
    tall, places, lanes = own.shape
    rows = tall + 2 * HALO
    coef = jnp.pad(coef, ((0, 64 - rows), (0, 2 * LANES - places)))
    vmem = pl.BlockSpec(memory_space=pltpu.VMEM)
    grid_rows = (rows, places // SUB, SUB, lanes)
    return pl.pallas_call(
        functools.partial(sweep_kernel, scale),
        out_shape=jax.ShapeDtypeStruct((tall, wide), f32),
        in_specs=[pl.BlockSpec(memory_space=pltpu.SMEM)] + [vmem] * (len(fields) + 2),
        out_specs=vmem,
        scratch_shapes=[
            pltpu.VMEM(grid_rows, f32),
            pltpu.VMEM(grid_rows, f32),
            pltpu.VMEM(grid_rows, f32),
            pltpu.VMEM(grid_rows, f32),
            pltpu.VMEM((tall,) + grid_rows[1:], f32),
        ],
        compiler_params=pltpu.CompilerParams(vmem_limit_bytes=VMEM_BYTES),
        name="sweeps",
    )(ends, *fields, inverse, coef)


def from_before(x, axis, closed):
    count = lax.axis_size(axis)
    return lax.ppermute(
        x, axis, [(i, (i + 1) % count) for i in range(count if closed else count - 1)]
    )


def from_after(x, axis, closed):
    count = lax.axis_size(axis)
    return lax.ppermute(
        x, axis, [((i + 1) % count, i) for i in range(count if closed else count - 1)]
    )


def dealt_rows(basis, order, tall, wide, axes, count):
    width = basis.shape[1]
    share = order.size // count
    if share == wide:
        order = order.reshape(lax.axis_size("lat"), lax.axis_size("lon"), wide)
        right = jnp.roll(order, -1, axis=1)[:, :, :HALO]
        left = jnp.roll(order, 1, axis=1)[:, :, -HALO:]
        moving = deal(basis, circle(order, right, left, 2))
        return moving, lambda arrived: arrived.reshape(tall, slots(wide), width)

    def last_step(arrived):
        own = arrived.reshape(tall, wide, width)
        left = from_before(own[:, -HALO:], "lon", True)
        right = from_after(own[:, :HALO], "lon", True)
        return circle(own, right, left, 1)

    return basis[order], last_step


def per_device(basis, order, land, conduct):
    axes = ("lat", "lon")
    rows_here, width = basis.shape
    tall, wide = land.shape
    count = lax.axis_size("lat") * lax.axis_size("lon")
    cells = rows_here * count
    share = width // count
    tied = lax.optimization_barrier

    def exchange(x):
        return lax.all_to_all(x, axes, split_axis=0, concat_axis=0, tiled=True)

    moving, last_step = dealt_rows(basis, order, tall, wide, axes, count)
    moving, basis = tied((moving, basis))
    raw = last_step(exchange(moving))

    partial = lax.dot_general(
        basis, basis, (((0,), (0,)), ((), ())), preferred_element_type=f32
    )
    coef = conduct * (0.35 + 0.65 * land.astype(f32))
    partial, coef = tied((partial, coef))
    pieces = exchange(partial)
    coef = circle(
        coef,
        from_after(coef[:, :HALO], "lon", True),
        from_before(coef[:, -HALO:], "lon", True),
        1,
    )
    pieces, coef = tied((pieces, coef))
    mine = jnp.sum(pieces.reshape(count, share, width), axis=0)
    copies = jnp.broadcast_to(mine[None], (count, share, width)).reshape(width, width)
    gram = exchange(copies)
    coef = jnp.concatenate(
        [from_before(coef[-HALO:], "lat", False), coef, from_after(coef[:HALO], "lat", False)],
        axis=0,
    )
    gram, coef, raw = tied((gram, coef, raw))

    north = from_before(raw[-HALO:], "lat", False)
    south = from_after(raw[:HALO], "lat", False)
    inverse = factor_inverse(gram)

    at = lax.axis_index("lat")
    ends = jnp.stack([at == 0, at == lax.axis_size("lat") - 1]).astype(i32)
    scale = cells / (width * SWEEPS)
    return sweeps(scale, ends, (north, raw, south), inverse, coef, wide)


def solution(mesh):
    in_specs = (P(("lat", "lon"), None), P(("lat", "lon")), P("lat", "lon"), P("lat", "lon"))
    out_specs = P("lat", "lon")
    return jax.shard_map(
        per_device, mesh=mesh, in_specs=in_specs, out_specs=out_specs, check_vma=False
    )
```

```python
import functools

import jax
import jax.numpy as jnp
from jax import lax
from jax.experimental import pallas as pl
from jax.experimental.pallas import tpu as pltpu
from jax.sharding import PartitionSpec as P

SWEEPS = 10
HALO = SWEEPS
LANES = 128
SUB = 8
ONE_HOT = 1024
BLOCK = 4
VMEM_BYTES = 56 * 1024 * 1024

bf16, f32, i32 = jnp.bfloat16, jnp.float32, jnp.int32


def iota(shape, dim):
    return lax.broadcasted_iota(i32, shape, dim)


def dot(a, b):
    return jnp.dot(a, b, preferred_element_type=f32)


def split3(x):
    high = x.astype(bf16)
    rest = x - high.astype(f32)
    mid = rest.astype(bf16)
    low = (rest - mid.astype(f32)).astype(bf16)
    return high, mid, low


def slots(wide):
    return -(-(wide + 2 * HALO) // SUB) * SUB


def circle(own, right, left, axis):
    wide = own.shape[axis]
    count = slots(wide)
    gap = list(own.shape)
    gap[axis] = count - wide - 2 * HALO
    around = jnp.concatenate([own, right, jnp.zeros(gap, own.dtype), left], axis=axis)
    shape = around.shape
    around = around.reshape(shape[:axis] + (SUB, count // SUB) + shape[axis + 1 :])
    return jnp.swapaxes(around, axis, axis + 1).reshape(shape)


def deal_kernel(tiles_lon, basis_ref, order_ref, out_ref, slot_ref):
    rows, width = basis_ref.shape
    parts = rows // ONE_HOT
    tiles, places, _ = out_ref.shape
    wide = order_ref.shape[1]
    groups = places // SUB
    lane = iota((LANES, LANES), 1)
    stacked = jnp.concatenate(
        [basis_ref[q * ONE_HOT : (q + 1) * ONE_HOT, :] for q in range(parts)], axis=1
    )

    order = order_ref[...]
    at = iota(order.shape, 0) % tiles_lon
    after = jnp.where(
        at == tiles_lon - 1, pltpu.roll(order, tiles_lon - 1, 0), pltpu.roll(order, tiles - 1, 0)
    )
    before = jnp.where(
        at == 0, pltpu.roll(order, tiles - tiles_lon + 1, 0), pltpu.roll(order, 1, 0)
    )
    padded = slot_ref.shape[1]
    column = iota((wide, padded), 0)
    slot = iota((wide, padded), 1)
    place = jnp.where(slot < places, (slot % SUB) * groups + slot // SUB, -1)
    low = jnp.zeros((tiles, padded), f32)
    high = low
    for source, hit in (
        (order, (place < wide) & (column == place)),
        (after, (place < wide + HALO) & (column == place - wide)),
        (before, (place >= places - HALO) & (column == place - places + wide)),
    ):
        hot = hit.astype(f32).astype(bf16)
        low = low + dot((source & 63).astype(f32).astype(bf16), hot)
        high = high + dot((source >> 6).astype(f32).astype(bf16), hot)
    slot_ref[...] = (high * 64.0 + low).astype(i32)

    take = 4

    def step(c, carry):
        marks, part = [], []
        for h in range(take):
            order = slot_ref[pl.ds(c * take + h, 1), :]
            order = jnp.broadcast_to(order, (LANES, padded)).T[:places]
            within = order & (ONE_HOT - 1)
            part.append(order - within)
            lane = iota((places, LANES), 1)
            marks.append(
                jnp.concatenate(
                    [
                        (within == lane + b * LANES).astype(f32)
                        for b in range(ONE_HOT // LANES)
                    ],
                    axis=1,
                )
            )
        found = dot(jnp.concatenate(marks, axis=0).astype(bf16), stacked)
        for h in range(take):
            here = found[h * places : (h + 1) * places]
            picked = here[:, :width]
            for q in range(1, parts):
                chosen = part[h] == q * ONE_HOT
                picked = jnp.where(chosen, here[:, q * width : (q + 1) * width], picked)
            out_ref[c * take + h] = picked.astype(bf16)
        return carry

    lax.fori_loop(0, tiles // take, step, 0)


def deal(basis, order, tiles_lon, wide):
    rows, width = basis.shape
    tiles = rows // wide
    places = slots(wide)
    return pl.pallas_call(
        functools.partial(deal_kernel, tiles_lon),
        out_shape=jax.ShapeDtypeStruct((tiles, places, width), bf16),
        scratch_shapes=[pltpu.VMEM((tiles, -(-places // LANES) * LANES), i32)],
        compiler_params=pltpu.CompilerParams(vmem_limit_bytes=VMEM_BYTES),
        cost_estimate=pl.CostEstimate(
            flops=2 * tiles * places * rows * width, bytes_accessed=4 * rows * width, transcendentals=0
        ),
        name="deal",
    )(basis, order.reshape(tiles, wide))


def inverse_kernel(gram_ref, out_ref):
    size = gram_ref.shape[0]
    count = size // SUB
    shape = (SUB, size)
    tiles = [gram_ref[t * SUB : (t + 1) * SUB, :] for t in range(count)]
    lane = iota(shape, 1)
    sub = iota(shape, 0)
    for top in range(count):
        first = top * SUB
        inside = (lane >= first) & (lane < first + SUB)
        columns = [
            [jnp.broadcast_to(tiles[t][:, first + c : first + c + 1], shape) for t in range(top, count)]
            for c in range(SUB)
        ]
        core = {
            (r, c): jnp.broadcast_to(columns[c][0][r : r + 1, :], shape)
            for r in range(SUB)
            for c in range(r, SUB)
        }
        lines = [
            jnp.where(
                inside,
                jnp.where(lane == first + c, 1.0, 0.0),
                jnp.broadcast_to(tiles[top][c : c + 1, :], shape),
            )
            for c in range(SUB)
        ]
        scales = []
        for c in range(SUB):
            inverse = 1.0 / core[c, c]
            scales.append(inverse)
            for d in range(c + 1, SUB):
                factor = core[c, d] * inverse
                for e in range(d, SUB):
                    core[d, e] = core[d, e] - factor * core[c, e]
                lines[d] = lines[d] - factor * lines[c]
                for t in range(1, count - top):
                    columns[d][t] = columns[d][t] - factor * columns[c][t]
        for t in range(1, count - top):
            rest = jnp.where(inside, 0.0, tiles[top + t])
            for c in range(SUB):
                rest = rest - columns[c][t] * (scales[c] * lines[c])
            tiles[top + t] = rest
        merged = lines[0]
        pivot = core[0, 0]
        for c in range(1, SUB):
            merged = jnp.where(sub == c, lines[c], merged)
            pivot = jnp.where(sub == c, core[c, c], pivot)
        kept = jnp.where(lane <= sub + first, merged, 0.0)
        out_ref[first : first + SUB, :] = kept * (1.0 / jnp.sqrt(pivot))


def factor_inverse(gram):
    size = gram.shape[0]
    return pl.pallas_call(
        inverse_kernel,
        out_shape=jax.ShapeDtypeStruct(gram.shape, f32),
        compiler_params=pltpu.CompilerParams(vmem_limit_bytes=VMEM_BYTES),
        cost_estimate=pl.CostEstimate(
            flops=40 * size**4, bytes_accessed=8 * size * size, transcendentals=0
        ),
        name="factor_inverse",
    )(gram)


def weight_kernel(coef_ref, across_ref, down_ref, spread):
    rows, groups, _, lanes = spread.shape
    places = groups * SUB
    turned = coef_ref[...].T
    depth = turned.shape[1]
    pieces = jnp.concatenate(split3(turned[:places]), axis=1)
    per_step = 4

    def put(c, carry):
        row = iota((3 * depth, per_step * lanes), 0) % depth
        wanted = c * per_step + iota((3 * depth, per_step * lanes), 1) // lanes
        values = dot(pieces, (row == wanted).astype(f32).astype(bf16))
        for h in range(per_step):
            spread[c * per_step + h] = values[:, h * lanes : (h + 1) * lanes].reshape(
                groups, SUB, lanes
            )
        return carry

    lax.fori_loop(0, rows // per_step, put, 0)

    def weigh(r, carry):
        for g in range(groups):
            here = spread[r, g]
            east = spread[r, g + 1] if g + 1 < groups else pltpu.roll(spread[r, 0], SUB - 1, 0)
            across_ref[r, g] = 0.124 * (here + east)
            down_ref[r, g] = 0.124 * (here + spread[r + 1, g])
        return carry

    lax.fori_loop(0, rows - 1, weigh, 0)
    across_ref[rows - 1] = jnp.zeros((groups, SUB, lanes), f32)
    down_ref[rows - 1] = jnp.zeros((groups, SUB, lanes), f32)


def weights(coef, lanes):
    rows, places = coef.shape
    coef = jnp.pad(coef, ((0, -rows % 64), (0, -places % LANES)))
    shape = (rows, places // SUB, SUB, lanes)
    return pl.pallas_call(
        weight_kernel,
        out_shape=(jax.ShapeDtypeStruct(shape, f32),) * 2,
        scratch_shapes=[pltpu.VMEM(shape, f32)],
        compiler_params=pltpu.CompilerParams(vmem_limit_bytes=VMEM_BYTES),
        cost_estimate=pl.CostEstimate(
            flops=rows * places * lanes * 100, bytes_accessed=8 * rows * places * lanes, transcendentals=0
        ),
        name="weights",
    )(coef)


def rotation(inverse):
    return jnp.concatenate(split3(inverse.T), axis=1)


def rotated(raw, turn):
    take, places, lanes = raw.shape
    raw = raw.astype(f32).reshape(take * places, lanes).astype(bf16)
    parts = dot(raw, turn)
    field = parts[:, :lanes] + (parts[:, lanes : 2 * lanes] + parts[:, 2 * lanes :])
    return field.astype(bf16).astype(f32).reshape(take, places, lanes)


def rotate_kernel(raw_ref, inverse_ref, out_ref):
    turn = rotation(inverse_ref[...])
    take = 8

    def step(c, carry):
        rows = pl.ds(c * take, take)
        out_ref[rows] = rotated(raw_ref[rows], turn).astype(bf16)
        return carry

    lax.fori_loop(0, raw_ref.shape[0] // take, step, 0)


def rotate(raw, inverse):
    return pl.pallas_call(
        rotate_kernel,
        out_shape=jax.ShapeDtypeStruct(raw.shape, bf16),
        compiler_params=pltpu.CompilerParams(vmem_limit_bytes=VMEM_BYTES),
        cost_estimate=pl.CostEstimate(
            flops=raw.size * 2000, bytes_accessed=4 * raw.size, transcendentals=0
        ),
        name="rotate",
    )(raw, inverse)


def sweep_kernel(
    scale, ends_ref, north_ref, own_ref, south_ref, inverse_ref, across_hbm, down_hbm, out_ref,
    first_ref, second_ref, across_ref, down_ref, sum_ref, sems,
):
    tall = own_ref.shape[0]
    rows, groups = first_ref.shape[:2]
    lanes = first_ref.shape[3]
    places = groups * SUB
    fetches = [
        pltpu.make_async_copy(across_hbm, across_ref, sems.at[0]),
        pltpu.make_async_copy(down_hbm, down_ref, sems.at[1]),
    ]
    for fetch in fetches:
        fetch.start()
    sum_ref[...] = jnp.zeros_like(sum_ref)
    turn = rotation(inverse_ref[...])

    def fill_halo(c, carry):
        take = 5
        for source, offset in ((north_ref, 0), (south_ref, HALO + tall)):
            field = rotated(source[pl.ds(c * take, take)], turn)
            first_ref[pl.ds(offset + c * take, take)] = field.reshape(take, groups, SUB, lanes)
        return carry

    def fill_own(c, carry):
        take = 4
        field = own_ref[pl.ds(c * take, take)].astype(f32)
        first_ref[pl.ds(HALO + c * take, take)] = field.reshape(take, groups, SUB, lanes)
        return carry

    lax.fori_loop(0, HALO // 5, fill_halo, 0)
    lax.fori_loop(0, tall // 4, fill_own, 0)
    for fetch in fetches:
        fetch.wait()

    def update(src, dst, row, take, kept):
        last = groups - 1
        west = []
        closing = []
        for r in range(take):
            here = src[row + r, last]
            east = pltpu.roll(src[row + r, 0], SUB - 1, 0)
            flux = across_ref[row + r, last] * (east - here)
            closing.append(flux)
            west.append(pltpu.roll(flux, 1, 0))
        here = [src[row + r, 0] for r in range(take)]
        for g in range(groups):
            above = down_ref[row - 1, g] * (here[0] - src[row - 1, g])
            following = []
            for r in range(take):
                below = here[r + 1] if r + 1 < take else src[row + take, g]
                under = down_ref[row + r, g] * (below - here[r])
                if g < last:
                    east = src[row + r, g + 1]
                    following.append(east)
                    flux = across_ref[row + r, g] * (east - here[r])
                else:
                    flux = closing[r]
                new = here[r] + ((under - above) + (flux - west[r]))
                dst[row + r, g] = new
                if kept:
                    sum_ref[row + r - HALO, g] += new * new
                above = under
                west[r] = flux
            here = following

    def sweep(s, src, dst):
        def inside(c, carry):
            update(src, dst, HALO + c * BLOCK, BLOCK, True)
            return carry

        def outside(r, carry):
            update(src, dst, r, 1, False)
            update(src, dst, rows - 1 - r, 1, False)
            return carry

        lax.fori_loop(0, tall // BLOCK, inside, 0)
        lax.fori_loop(s + 1, HALO, outside, 0)

        @pl.when(ends_ref[0] == 1)
        def _():
            dst[HALO - 1] = jnp.zeros(dst.shape[1:], f32)

        @pl.when(ends_ref[1] == 1)
        def _():
            dst[HALO + tall] = jnp.zeros(dst.shape[1:], f32)

    def two(t, carry):
        sweep(2 * t, first_ref, second_ref)
        sweep(2 * t + 1, second_ref, first_ref)
        return carry

    lax.fori_loop(0, SWEEPS // 2, two, 0)

    lane = iota((SUB, lanes), 1)

    def gather(c, totals):
        totals = list(totals)
        for r in [c * 2, c * 2 + 1]:
            for g in range(groups):
                total = jnp.sum(sum_ref[r, g], axis=1, keepdims=True)
                totals[g] = jnp.where(lane == r, total, totals[g])
        return tuple(totals)

    totals = lax.fori_loop(
        0, tall // 2, gather, tuple(jnp.zeros((SUB, lanes), f32) for _ in range(groups))
    )
    totals = jnp.concatenate(totals, axis=0).T[:tall]
    slot = iota((places, out_ref.shape[1]), 0)
    column = iota((places, out_ref.shape[1]), 1)
    back = (column == (slot % SUB) * groups + slot // SUB).astype(f32).astype(bf16)
    high, mid, low = split3(totals)
    out_ref[...] = (dot(high, back) + (dot(mid, back) + dot(low, back))) * scale


def sweeps(scale, ends, fields, inverse, across_down, wide):
    own = fields[1]
    tall, places, lanes = own.shape
    rows = tall + 2 * HALO
    vmem = pl.BlockSpec(memory_space=pltpu.VMEM)
    far = pl.BlockSpec(memory_space=pl.ANY)
    grid_rows = (rows, places // SUB, SUB, lanes)
    return pl.pallas_call(
        functools.partial(sweep_kernel, scale),
        out_shape=jax.ShapeDtypeStruct((tall, wide), f32),
        in_specs=[pl.BlockSpec(memory_space=pltpu.SMEM)] + [vmem] * (len(fields) + 1) + [far] * 2,
        out_specs=vmem,
        scratch_shapes=[
            pltpu.VMEM(grid_rows, f32),
            pltpu.VMEM(grid_rows, f32),
            pltpu.VMEM(grid_rows, f32),
            pltpu.VMEM(grid_rows, f32),
            pltpu.VMEM((tall,) + grid_rows[1:], f32),
            pltpu.SemaphoreType.DMA((2,)),
        ],
        compiler_params=pltpu.CompilerParams(vmem_limit_bytes=VMEM_BYTES),
        name="sweeps",
    )(ends, *fields, inverse, *across_down)


def from_before(x, axis, closed):
    count = lax.axis_size(axis)
    return lax.ppermute(
        x, axis, [(i, (i + 1) % count) for i in range(count if closed else count - 1)]
    )


def from_after(x, axis, closed):
    count = lax.axis_size(axis)
    return lax.ppermute(
        x, axis, [((i + 1) % count, i) for i in range(count if closed else count - 1)]
    )


def summed(x):
    def partner(axis, bits):
        return lax.ppermute(x, axis, [(i, i ^ bits) for i in range(lax.axis_size(axis))])

    for axis in ("lon", "lat"):
        step, count = 1, lax.axis_size(axis)
        while step < count:
            if step * 4 <= count:
                one, two, three = (partner(axis, step * k) for k in (1, 2, 3))
                x = (x + one) + (two + three)
                step *= 4
            else:
                x = x + partner(axis, step)
                step *= 2
    return x


def dealt_rows(basis, order, tall, wide, axes, count):
    width = basis.shape[1]
    share = order.size // count
    if share == wide:
        moving = deal(basis, order, lax.axis_size("lon"), wide)
        return moving, lambda arrived: arrived

    def last_step(arrived):
        own = arrived.reshape(tall, wide, width)
        left = from_before(own[:, -HALO:], "lon", True)
        right = from_after(own[:, :HALO], "lon", True)
        return circle(own, right, left, 1)

    return basis[order], last_step


def per_device(basis, order, land, conduct):
    axes = ("lat", "lon")
    rows_here, width = basis.shape
    tall, wide = land.shape
    count = lax.axis_size("lat") * lax.axis_size("lon")
    cells = rows_here * count
    tied = lax.optimization_barrier

    moving, last_step = dealt_rows(basis, order, tall, wide, axes, count)
    moving, basis = tied((moving, basis))
    raw = last_step(lax.all_to_all(moving, axes, split_axis=0, concat_axis=0, tiled=True))

    partial = lax.dot_general(
        basis, basis, (((0,), (0,)), ((), ())), preferred_element_type=f32
    )
    coef = conduct * (0.35 + 0.65 * land.astype(f32))
    partial, coef = tied((partial, coef))
    gram = summed(partial)
    coef = circle(
        coef,
        from_after(coef[:, :HALO], "lon", True),
        from_before(coef[:, -HALO:], "lon", True),
        1,
    )
    coef = jnp.concatenate(
        [from_before(coef[-HALO:], "lat", False), coef, from_after(coef[:HALO], "lat", False)],
        axis=0,
    )
    across_down = weights(coef, width)
    inverse = factor_inverse(gram)

    north = from_before(raw[-HALO:], "lat", False)
    south = from_after(raw[:HALO], "lat", False)
    own = rotate(raw, inverse)

    at = lax.axis_index("lat")
    ends = jnp.stack([at == 0, at == lax.axis_size("lat") - 1]).astype(i32)
    scale = cells / (width * SWEEPS)
    return sweeps(scale, ends, (north, own, south), inverse, across_down, wide)


def solution(mesh):
    in_specs = (P(("lat", "lon"), None), P(("lat", "lon")), P("lat", "lon"), P("lat", "lon"))
    out_specs = P("lat", "lon")
    return jax.shard_map(
        per_device, mesh=mesh, in_specs=in_specs, out_specs=out_specs, check_vma=False
    )
```

```python
import functools

import jax
import jax.numpy as jnp
from jax import lax
from jax.experimental import pallas as pl
from jax.experimental.pallas import tpu as pltpu
from jax.sharding import PartitionSpec as P

SWEEPS = 10
HALO = SWEEPS
LANES = 128
SUB = 8
ONE_HOT = 1024
BLOCK = 4
VMEM_BYTES = 56 * 1024 * 1024

bf16, f32, i32 = jnp.bfloat16, jnp.float32, jnp.int32


def iota(shape, dim):
    return lax.broadcasted_iota(i32, shape, dim)


def dot(a, b):
    return jnp.dot(a, b, preferred_element_type=f32)


def split3(x):
    high = x.astype(bf16)
    rest = x - high.astype(f32)
    mid = rest.astype(bf16)
    low = (rest - mid.astype(f32)).astype(bf16)
    return high, mid, low


def slots(wide):
    return -(-(wide + 2 * HALO) // SUB) * SUB


def circle(own, right, left, axis):
    wide = own.shape[axis]
    count = slots(wide)
    gap = list(own.shape)
    gap[axis] = count - wide - 2 * HALO
    around = jnp.concatenate([own, right, jnp.zeros(gap, own.dtype), left], axis=axis)
    shape = around.shape
    around = around.reshape(shape[:axis] + (SUB, count // SUB) + shape[axis + 1 :])
    return jnp.swapaxes(around, axis, axis + 1).reshape(shape)


def deal_kernel(tiles_lon, basis_ref, order_ref, out_ref, slot_ref):
    rows, width = basis_ref.shape
    parts = rows // ONE_HOT
    tiles, places, _ = out_ref.shape
    wide = order_ref.shape[1]
    groups = places // SUB
    lane = iota((LANES, LANES), 1)
    stacked = jnp.concatenate(
        [basis_ref[q * ONE_HOT : (q + 1) * ONE_HOT, :] for q in range(parts)], axis=1
    )

    order = order_ref[...]
    at = iota(order.shape, 0) % tiles_lon
    after = jnp.where(
        at == tiles_lon - 1, pltpu.roll(order, tiles_lon - 1, 0), pltpu.roll(order, tiles - 1, 0)
    )
    before = jnp.where(
        at == 0, pltpu.roll(order, tiles - tiles_lon + 1, 0), pltpu.roll(order, 1, 0)
    )
    padded = slot_ref.shape[1]
    column = iota((wide, padded), 0)
    slot = iota((wide, padded), 1)
    place = jnp.where(slot < places, (slot % SUB) * groups + slot // SUB, -1)
    low = jnp.zeros((tiles, padded), f32)
    high = low
    for source, hit in (
        (order, (place < wide) & (column == place)),
        (after, (place < wide + HALO) & (column == place - wide)),
        (before, (place >= places - HALO) & (column == place - places + wide)),
    ):
        hot = hit.astype(f32).astype(bf16)
        low = low + dot((source & 63).astype(f32).astype(bf16), hot)
        high = high + dot((source >> 6).astype(f32).astype(bf16), hot)
    slot_ref[...] = (high * 64.0 + low).astype(i32)

    take = 4

    def step(c, carry):
        marks, part = [], []
        for h in range(take):
            order = slot_ref[pl.ds(c * take + h, 1), :]
            order = jnp.broadcast_to(order, (LANES, padded)).T[:places]
            within = order & (ONE_HOT - 1)
            part.append(order - within)
            lane = iota((places, LANES), 1)
            marks.append(
                jnp.concatenate(
                    [
                        (within == lane + b * LANES).astype(f32)
                        for b in range(ONE_HOT // LANES)
                    ],
                    axis=1,
                )
            )
        found = dot(jnp.concatenate(marks, axis=0).astype(bf16), stacked)
        for h in range(take):
            here = found[h * places : (h + 1) * places]
            picked = here[:, :width]
            for q in range(1, parts):
                chosen = part[h] == q * ONE_HOT
                picked = jnp.where(chosen, here[:, q * width : (q + 1) * width], picked)
            out_ref[c * take + h] = picked.astype(bf16)
        return carry

    lax.fori_loop(0, tiles // take, step, 0)


def deal(basis, order, tiles_lon, wide):
    rows, width = basis.shape
    tiles = rows // wide
    places = slots(wide)
    return pl.pallas_call(
        functools.partial(deal_kernel, tiles_lon),
        out_shape=jax.ShapeDtypeStruct((tiles, places, width), bf16),
        scratch_shapes=[pltpu.VMEM((tiles, -(-places // LANES) * LANES), i32)],
        compiler_params=pltpu.CompilerParams(vmem_limit_bytes=VMEM_BYTES),
        cost_estimate=pl.CostEstimate(
            flops=2 * tiles * places * rows * width, bytes_accessed=4 * rows * width, transcendentals=0
        ),
        name="deal",
    )(basis, order.reshape(tiles, wide))


def inverse_kernel(gram_ref, out_ref):
    size = gram_ref.shape[0]
    count = size // SUB
    shape = (SUB, size)
    tiles = [gram_ref[t * SUB : (t + 1) * SUB, :] for t in range(count)]
    lane = iota(shape, 1)
    sub = iota(shape, 0)
    for top in range(count):
        first = top * SUB
        inside = (lane >= first) & (lane < first + SUB)
        columns = [
            [jnp.broadcast_to(tiles[t][:, first + c : first + c + 1], shape) for t in range(top, count)]
            for c in range(SUB)
        ]
        core = {
            (r, c): jnp.broadcast_to(columns[c][0][r : r + 1, :], shape)
            for r in range(SUB)
            for c in range(r, SUB)
        }
        lines = [
            jnp.where(
                inside,
                jnp.where(lane == first + c, 1.0, 0.0),
                jnp.broadcast_to(tiles[top][c : c + 1, :], shape),
            )
            for c in range(SUB)
        ]
        scales = []
        for c in range(SUB):
            inverse = 1.0 / core[c, c]
            scales.append(inverse)
            for d in range(c + 1, SUB):
                factor = core[c, d] * inverse
                for e in range(d, SUB):
                    core[d, e] = core[d, e] - factor * core[c, e]
                lines[d] = lines[d] - factor * lines[c]
                for t in range(1, count - top):
                    columns[d][t] = columns[d][t] - factor * columns[c][t]
        for t in range(1, count - top):
            rest = jnp.where(inside, 0.0, tiles[top + t])
            for c in range(SUB):
                rest = rest - columns[c][t] * (scales[c] * lines[c])
            tiles[top + t] = rest
        merged = lines[0]
        pivot = core[0, 0]
        for c in range(1, SUB):
            merged = jnp.where(sub == c, lines[c], merged)
            pivot = jnp.where(sub == c, core[c, c], pivot)
        kept = jnp.where(lane <= sub + first, merged, 0.0)
        out_ref[first : first + SUB, :] = kept * (1.0 / jnp.sqrt(pivot))


def factor_inverse(gram):
    size = gram.shape[0]
    return pl.pallas_call(
        inverse_kernel,
        out_shape=jax.ShapeDtypeStruct(gram.shape, f32),
        compiler_params=pltpu.CompilerParams(vmem_limit_bytes=VMEM_BYTES),
        cost_estimate=pl.CostEstimate(
            flops=40 * size**4, bytes_accessed=8 * size * size, transcendentals=0
        ),
        name="factor_inverse",
    )(gram)


def weight_kernel(coef_ref, across_ref, down_ref, spread):
    rows, groups, _, lanes = spread.shape
    places = groups * SUB
    turned = coef_ref[...].T
    depth = turned.shape[1]
    pieces = jnp.concatenate(split3(turned[:places]), axis=1)
    per_step = rows // 4
    offset = iota((3 * depth, per_step * lanes), 0) & (depth - 1)
    offset = offset - (iota((3 * depth, per_step * lanes), 1) // lanes)

    def put(c, carry):
        values = dot(pieces, (offset == c * per_step).astype(f32).astype(bf16))
        for h in range(per_step):
            spread[c * per_step + h] = values[:, h * lanes : (h + 1) * lanes].reshape(
                groups, SUB, lanes
            )
        return carry

    lax.fori_loop(0, 4, put, 0)

    def weigh(r, carry):
        for g in range(groups):
            here = spread[r, g]
            east = spread[r, g + 1] if g + 1 < groups else pltpu.roll(spread[r, 0], SUB - 1, 0)
            across_ref[r, g] = 0.124 * (here + east)
            down_ref[r, g] = 0.124 * (here + spread[r + 1, g])
        return carry

    lax.fori_loop(0, rows - 1, weigh, 0)
    across_ref[rows - 1] = jnp.zeros((groups, SUB, lanes), f32)
    down_ref[rows - 1] = jnp.zeros((groups, SUB, lanes), f32)


def weights(coef, lanes):
    rows, places = coef.shape
    coef = jnp.pad(coef, ((0, -rows % 64), (0, -places % LANES)))
    shape = (rows, places // SUB, SUB, lanes)
    return pl.pallas_call(
        weight_kernel,
        out_shape=(jax.ShapeDtypeStruct(shape, f32),) * 2,
        scratch_shapes=[pltpu.VMEM(shape, f32)],
        compiler_params=pltpu.CompilerParams(vmem_limit_bytes=VMEM_BYTES),
        cost_estimate=pl.CostEstimate(
            flops=rows * places * lanes * 100, bytes_accessed=8 * rows * places * lanes, transcendentals=0
        ),
        name="weights",
    )(coef)


def rotation(inverse):
    return jnp.concatenate(split3(inverse.T), axis=1)


def rotated(raw, turn):
    take, places, lanes = raw.shape
    raw = raw.astype(f32).reshape(take * places, lanes).astype(bf16)
    parts = dot(raw, turn)
    field = parts[:, :lanes] + (parts[:, lanes : 2 * lanes] + parts[:, 2 * lanes :])
    return field.astype(bf16).astype(f32).reshape(take, places, lanes)


def update(src, dst, across, down, sums, row, take):
    groups = src.shape[1]
    last = groups - 1
    span = range(take)
    start = [src[row + r, 0] for r in span]
    closing = [
        across[row + r, last] * (pltpu.roll(start[r], SUB - 1, 0) - src[row + r, last])
        for r in span
    ]
    wrapped = [pltpu.roll(flux, 1, 0) for flux in closing]

    def vertical(g, here):
        above = down[row - 1, g] * (here[0] - src[row - 1, g])
        change = []
        for r in span:
            below = here[r + 1] if r + 1 < take else src[row + take, g]
            under = down[row + r, g] * (below - here[r])
            change.append(under - above)
            above = under
        return change

    def finish(r, g, new):
        dst[row + r, g] = new
        sums[row + r, g] += new * new

    here = [src[row + r, 1] for r in span]
    west = [across[row + r, 0] * (here[r] - start[r]) for r in span]
    change = vertical(0, start)
    pending = [start[r] + (change[r] + west[r]) for r in span]
    for g in range(1, groups):
        if g < last:
            following = [src[row + r, g + 1] for r in span]
            flux = [across[row + r, g] * (following[r] - here[r]) for r in span]
        else:
            following, flux = None, closing
        change = vertical(g, here)
        for r in span:
            finish(r, g, here[r] + (change[r] + (flux[r] - west[r])))
        here, west = following, flux
    for r in span:
        finish(r, 0, pending[r] - wrapped[r])


def summed_lanes(sums, rows, totals):
    lane = iota(totals[0].shape, 1)
    for row, to in rows:
        for g in range(len(totals)):
            total = jnp.sum(sums[row, g], axis=1, keepdims=True)
            totals[g] = totals[g] + jnp.where(lane == to, total, 0.0)
    return totals


def inner_kernel(
    own_ref, inverse_ref, across_hbm, down_hbm, first_ref, second_ref, total_ref,
    across_ref, down_ref, sum_ref, sems,
):
    tall, groups, _, lanes = first_ref.shape
    inside = pl.ds(HALO, tall)
    fetches = [
        pltpu.make_async_copy(across_hbm.at[inside], across_ref, sems.at[0]),
        pltpu.make_async_copy(down_hbm.at[inside], down_ref, sems.at[1]),
    ]
    for fetch in fetches:
        fetch.start()
    turn = rotation(inverse_ref[...])
    take = 8

    def fill(c, carry):
        field = rotated(own_ref[pl.ds(c * take, take)], turn)
        first_ref[pl.ds(c * take, take)] = field.reshape(take, groups, SUB, lanes)
        return carry

    lax.fori_loop(0, tall // take, fill, 0)
    sum_ref[...] = jnp.zeros_like(sum_ref)
    second_ref[0] = jnp.zeros(second_ref.shape[1:], f32)
    second_ref[tall - 1] = jnp.zeros(second_ref.shape[1:], f32)
    for fetch in fetches:
        fetch.wait()

    def sweep(s, src, dst, odd_pair):
        count = tall - 2 - 2 * s

        def step(c, carry):
            update(src, dst, across_ref, down_ref, sum_ref, s + 1 + c * BLOCK, BLOCK)
            return carry

        lax.fori_loop(0, count // BLOCK, step, 0)
        if odd_pair:
            update(src, dst, across_ref, down_ref, sum_ref, s + count - 1, 2)

    def two(t, carry):
        sweep(2 * t, first_ref, second_ref, (tall - 2) % BLOCK == 2)
        sweep(2 * t + 1, second_ref, first_ref, (tall - 4) % BLOCK == 2)
        return carry

    lax.fori_loop(0, SWEEPS // 2, two, 0)

    def gather(c, totals):
        rows = [(c * 2 + h, c * 2 + h) for h in range(2)]
        return tuple(summed_lanes(sum_ref, rows, list(totals)))

    zeros = tuple(jnp.zeros((SUB, lanes), f32) for _ in range(groups))
    totals = lax.fori_loop(0, tall // 2, gather, zeros)
    total_ref[...] = jnp.concatenate(totals, axis=0)


def inner_sweeps(own, inverse, across_down):
    tall, places, lanes = own.shape
    vmem = pl.BlockSpec(memory_space=pltpu.VMEM)
    far = pl.BlockSpec(memory_space=pl.ANY)
    shape = (tall, places // SUB, SUB, lanes)
    return pl.pallas_call(
        inner_kernel,
        out_shape=(
            jax.ShapeDtypeStruct(shape, f32),
            jax.ShapeDtypeStruct(shape, f32),
            jax.ShapeDtypeStruct((places, lanes), f32),
        ),
        in_specs=[vmem, vmem, far, far],
        out_specs=(vmem, vmem, vmem),
        scratch_shapes=[
            pltpu.VMEM(shape, f32),
            pltpu.VMEM(shape, f32),
            pltpu.VMEM(shape, f32),
            pltpu.SemaphoreType.DMA((2,)),
        ],
        compiler_params=pltpu.CompilerParams(vmem_limit_bytes=VMEM_BYTES),
        cost_estimate=pl.CostEstimate(
            flops=12 * 10**9, bytes_accessed=8 * own.size, transcendentals=0
        ),
        name="inner_sweeps",
    )(own, inverse, *across_down)


def outer_kernel(
    scale, ends_ref, north_ref, south_ref, inverse_ref, inner_ref, first_hbm, second_hbm,
    across_hbm, down_hbm, out_ref, first_ref, second_ref, across_ref, down_ref, sum_ref, sems,
):
    rows, groups, _, lanes = first_ref.shape
    tall = rows - 2 * HALO
    places = groups * SUB
    near = HALO + 1
    fetches = []
    for k, (source, target) in enumerate(((first_hbm, first_ref), (second_hbm, second_ref))):
        for side, row in enumerate((0, tall - near)):
            fetches.append(
                pltpu.make_async_copy(
                    source.at[pl.ds(row, near)],
                    target.at[pl.ds(HALO + row, near)],
                    sems.at[2 * k + side],
                )
            )
    wide_part = 2 * HALO + 1
    for k, (source, target) in enumerate(((across_hbm, across_ref), (down_hbm, down_ref))):
        for side, row in enumerate((0, rows - wide_part)):
            part = pl.ds(row, wide_part)
            fetches.append(
                pltpu.make_async_copy(source.at[part], target.at[part], sems.at[4 + 2 * k + side])
            )
    for fetch in fetches:
        fetch.start()
    sum_ref[...] = jnp.zeros_like(sum_ref)
    turn = rotation(inverse_ref[...])
    take = 5

    def fill(c, carry):
        for source, offset in ((north_ref, 0), (south_ref, HALO + tall)):
            field = rotated(source[pl.ds(c * take, take)], turn)
            first_ref[pl.ds(offset + c * take, take)] = field.reshape(take, groups, SUB, lanes)
        return carry

    lax.fori_loop(0, HALO // take, fill, 0)
    for fetch in fetches:
        fetch.wait()

    def sweep(s, src, dst):
        def step(c, carry):
            bottom = c // 2
            row = jnp.where(bottom == 0, s + 1, rows - 1 - HALO - s) + (c % 2) * take
            update(src, dst, across_ref, down_ref, sum_ref, row, take)
            return carry

        lax.fori_loop(0, 4, step, 0)

        @pl.when(ends_ref[0] == 1)
        def _():
            dst[HALO - 1] = jnp.zeros(dst.shape[1:], f32)

        @pl.when(ends_ref[1] == 1)
        def _():
            dst[HALO + tall] = jnp.zeros(dst.shape[1:], f32)

    def two(t, carry):
        sweep(2 * t, first_ref, second_ref)
        sweep(2 * t + 1, second_ref, first_ref)
        return carry

    lax.fori_loop(0, SWEEPS // 2, two, 0)

    def gather(c, totals):
        pairs = [(HALO + c, c), (tall + c, tall - HALO + c)]
        return tuple(summed_lanes(sum_ref, pairs, list(totals)))

    totals = tuple(inner_ref[g * SUB : (g + 1) * SUB, :] for g in range(groups))
    totals = lax.fori_loop(0, HALO, gather, totals)
    totals = jnp.concatenate(totals, axis=0).T[:tall]
    slot = iota((places, out_ref.shape[1]), 0)
    column = iota((places, out_ref.shape[1]), 1)
    back = (column == (slot % SUB) * groups + slot // SUB).astype(f32).astype(bf16)
    high, mid, low = split3(totals)
    out_ref[...] = (dot(high, back) + (dot(mid, back) + dot(low, back))) * scale


def outer_sweeps(scale, ends, north, south, inverse, inner, across_down, wide):
    first, second, total = inner
    tall, groups, _, lanes = first.shape
    shape = (tall + 2 * HALO, groups, SUB, lanes)
    vmem = pl.BlockSpec(memory_space=pltpu.VMEM)
    far = pl.BlockSpec(memory_space=pl.ANY)
    return pl.pallas_call(
        functools.partial(outer_kernel, scale),
        out_shape=jax.ShapeDtypeStruct((tall, wide), f32),
        in_specs=[pl.BlockSpec(memory_space=pltpu.SMEM)] + [vmem] * 4 + [far] * 4,
        out_specs=vmem,
        scratch_shapes=[pltpu.VMEM(shape, f32)] * 5 + [pltpu.SemaphoreType.DMA((8,))],
        compiler_params=pltpu.CompilerParams(vmem_limit_bytes=VMEM_BYTES),
        name="outer_sweeps",
    )(ends, north, south, inverse, total, first, second, *across_down)


def from_before(x, axis, closed):
    count = lax.axis_size(axis)
    return lax.ppermute(
        x, axis, [(i, (i + 1) % count) for i in range(count if closed else count - 1)]
    )


def from_after(x, axis, closed):
    count = lax.axis_size(axis)
    return lax.ppermute(
        x, axis, [((i + 1) % count, i) for i in range(count if closed else count - 1)]
    )


def summed(x, extra, axis):
    size = x.shape[0]
    count = lax.axis_size(axis)

    def ahead(values, step):
        return lax.ppermute(values, axis, [((i + step) % count, i) for i in range(count)])

    sent = jnp.concatenate([x, extra], axis=0)
    after, before, second = ahead(sent, 1), ahead(sent, count - 1), ahead(x, 2)
    x = (x + before[:size]) + (after[:size] + second)
    step = 4
    while step < count:
        x = x + ahead(x, step)
        step *= 2
    return x, before[size:], after[size:]


def dealt_rows(basis, order, tall, wide, axes, count):
    width = basis.shape[1]
    share = order.size // count
    if share == wide:
        moving = deal(basis, order, lax.axis_size("lon"), wide)
        return moving, lambda arrived: arrived

    def last_step(arrived):
        own = arrived.reshape(tall, wide, width)
        left = from_before(own[:, -HALO:], "lon", True)
        right = from_after(own[:, :HALO], "lon", True)
        return circle(own, right, left, 1)

    return basis[order], last_step


def per_device(basis, order, land, conduct):
    axes = ("lat", "lon")
    rows_here, width = basis.shape
    tall, wide = land.shape
    count = lax.axis_size("lat") * lax.axis_size("lon")
    cells = rows_here * count
    tied = lax.optimization_barrier
    at = lax.axis_index("lat")
    top, bottom = at == 0, at == lax.axis_size("lat") - 1

    moving, last_step = dealt_rows(basis, order, tall, wide, axes, count)
    moving, basis = tied((moving, basis))
    raw = last_step(lax.all_to_all(moving, axes, split_axis=0, concat_axis=0, tiled=True))

    partial = lax.dot_general(
        basis, basis, (((0,), (0,)), ((), ())), preferred_element_type=f32
    )
    coef = conduct * (0.35 + 0.65 * land.astype(f32))
    edges = jnp.concatenate([coef[:, :HALO], coef[:, -HALO:]], axis=1).T
    edges = jnp.pad(edges, ((0, 4), (0, width - tall)))
    partial, before, after = summed(partial, edges, "lon")
    coef = circle(coef, after[:HALO, :tall].T, before[HALO : 2 * HALO, :tall].T, 1)
    ends = jnp.concatenate([coef[:HALO], coef[-HALO:]], axis=0)
    rest = coef.shape[1] - width
    edges = jnp.concatenate(
        [ends[:, :width], jnp.pad(ends[:, width:], ((0, 0), (0, width - rest)))], axis=0
    )
    gram, before, after = summed(partial, edges, "lat")
    before = jnp.concatenate([before[: 2 * HALO], before[2 * HALO :, :rest]], axis=1)[HALO:]
    after = jnp.concatenate([after[: 2 * HALO], after[2 * HALO :, :rest]], axis=1)[:HALO]
    coef = jnp.concatenate(
        [jnp.where(top, 0.0, before), coef, jnp.where(bottom, 0.0, after)], axis=0
    )
    inverse = factor_inverse(gram)
    across_down = weights(coef, width)
    raw, inverse = tied((raw, inverse))

    north = from_before(raw[-HALO:], "lat", False)
    south = from_after(raw[:HALO], "lat", False)
    inner = inner_sweeps(raw, inverse, across_down)
    ends = jnp.stack([top, bottom]).astype(i32)
    scale = cells / (width * SWEEPS)
    return outer_sweeps(scale, ends, north, south, inverse, inner, across_down, wide)


def solution(mesh):
    in_specs = (P(("lat", "lon"), None), P(("lat", "lon")), P("lat", "lon"), P("lat", "lon"))
    out_specs = P("lat", "lon")
    return jax.shard_map(
        per_device, mesh=mesh, in_specs=in_specs, out_specs=out_specs, check_vma=False
    )
```

```python
import functools

import jax
import jax.numpy as jnp
from jax import lax
from jax.experimental import pallas as pl
from jax.experimental.pallas import tpu as pltpu
from jax.sharding import PartitionSpec as P

SWEEPS = 10
HALO = SWEEPS
LANES = 128
SUB = 8
ONE_HOT = 1024
TILES = 4
BLOCK = 4
VMEM_BYTES = 56 * 1024 * 1024

bf16, f32, i32 = jnp.bfloat16, jnp.float32, jnp.int32


def iota(shape, dim):
    return lax.broadcasted_iota(i32, shape, dim)


def dot(a, b):
    return jnp.dot(a, b, preferred_element_type=f32)


def split3(x):
    high = x.astype(bf16)
    rest = x - high.astype(f32)
    mid = rest.astype(bf16)
    low = (rest - mid.astype(f32)).astype(bf16)
    return high, mid, low


def slots(wide):
    return -(-(wide + 2 * HALO) // SUB) * SUB


def circle(own, right, left, axis):
    wide = own.shape[axis]
    count = slots(wide)
    gap = list(own.shape)
    gap[axis] = count - wide - 2 * HALO
    around = jnp.concatenate([own, right, jnp.zeros(gap, own.dtype), left], axis=axis)
    shape = around.shape
    around = around.reshape(shape[:axis] + (SUB, count // SUB) + shape[axis + 1 :])
    return jnp.swapaxes(around, axis, axis + 1).reshape(shape)


def deal_kernel(tiles_lon, first, count, basis_ref, order_ref, *refs):
    out_ref, slot_ref, ready_ref, sems = refs[-4:]
    rows, width = basis_ref.shape
    parts = rows // ONE_HOT
    tiles, places, _ = out_ref.shape
    wide = order_ref.shape[1]
    groups = places // SUB
    stacked = jnp.concatenate(
        [basis_ref[q * ONE_HOT : (q + 1) * ONE_HOT, :] for q in range(parts)], axis=1
    )

    order = order_ref[...]
    at = iota(order.shape, 0) % tiles_lon
    after = jnp.where(
        at == tiles_lon - 1, pltpu.roll(order, tiles_lon - 1, 0), pltpu.roll(order, tiles - 1, 0)
    )
    before = jnp.where(
        at == 0, pltpu.roll(order, tiles - tiles_lon + 1, 0), pltpu.roll(order, 1, 0)
    )
    padded = slot_ref.shape[1]
    column = iota((wide, padded), 0)
    slot = iota((wide, padded), 1)
    place = jnp.where(slot < places, (slot % SUB) * groups + slot // SUB, -1)
    low = jnp.zeros((tiles, padded), f32)
    high = low
    for source, hit in (
        (order, (place < wide) & (column == place)),
        (after, (place < wide + HALO) & (column == place - wide)),
        (before, (place >= places - HALO) & (column == place - places + wide)),
    ):
        hot = hit.astype(f32).astype(bf16)
        low = low + dot((source & 63).astype(f32).astype(bf16), hot)
        high = high + dot((source >> 6).astype(f32).astype(bf16), hot)
    slot_ref[...] = (high * 64.0 + low).astype(i32)

    take = TILES
    steps = count // take

    def leave(c):
        return pltpu.make_async_copy(
            ready_ref.at[pl.ds(c * take, take)],
            out_ref.at[pl.ds(first + c * take, take)],
            sems.at[c],
        )

    lane = iota((take * places, LANES), 1)
    for c in range(steps):
        wanted = []
        for h in range(take):
            order = slot_ref[first + c * take + h : first + c * take + h + 1, :]
            wanted.append(jnp.broadcast_to(order, (LANES, padded)).T[:places])
        wanted = jnp.concatenate(wanted, axis=0)
        within = wanted & (ONE_HOT - 1)
        part = wanted - within
        marks = [
            (within == lane + b * LANES).astype(f32).astype(bf16)
            for b in range(ONE_HOT // LANES)
        ]
        found = dot(jnp.concatenate(marks, axis=1), stacked)
        picked = found[:, :width]
        for q in range(1, parts):
            picked = jnp.where(
                part == q * ONE_HOT, found[:, q * width : (q + 1) * width], picked
            )
        for h in range(take):
            ready_ref[c * take + h] = picked[h * places : (h + 1) * places].astype(bf16)
        leave(c).start()
    for c in range(steps):
        leave(c).wait()


def deal(basis, order, tiles_lon, wide, first, count, so_far):
    rows, width = basis.shape
    tiles = rows // wide
    places = slots(wide)
    vmem = pl.BlockSpec(memory_space=pltpu.VMEM)
    far = pl.BlockSpec(memory_space=pl.ANY)
    before = [] if so_far is None else [so_far]
    return pl.pallas_call(
        functools.partial(deal_kernel, tiles_lon, first, count),
        out_shape=jax.ShapeDtypeStruct((tiles, places, width), bf16),
        in_specs=[vmem, vmem] + [far] * len(before),
        out_specs=far,
        input_output_aliases={2: 0} if before else {},
        scratch_shapes=[
            pltpu.VMEM((tiles, -(-places // LANES) * LANES), i32),
            pltpu.VMEM((count, places, width), bf16),
            pltpu.SemaphoreType.DMA((count // TILES,)),
        ],
        compiler_params=pltpu.CompilerParams(vmem_limit_bytes=VMEM_BYTES),
        cost_estimate=pl.CostEstimate(
            flops=2 * count * places * rows * width,
            bytes_accessed=4 * rows * width,
            transcendentals=0,
        ),
        name=f"deal_{first}",
    )(basis, order.reshape(tiles, wide), *before)


def inverse_kernel(gram_ref, out_ref):
    size = gram_ref.shape[0]
    count = size // SUB
    shape = (SUB, size)
    tiles = [gram_ref[t * SUB : (t + 1) * SUB, :] for t in range(count)]
    lane = iota(shape, 1)
    sub = iota(shape, 0)
    for top in range(count):
        first = top * SUB
        inside = (lane >= first) & (lane < first + SUB)
        columns = [
            [jnp.broadcast_to(tiles[t][:, first + c : first + c + 1], shape) for t in range(top, count)]
            for c in range(SUB)
        ]
        core = {
            (r, c): jnp.broadcast_to(columns[c][0][r : r + 1, :], shape)
            for r in range(SUB)
            for c in range(r, SUB)
        }
        lines = [
            jnp.where(
                inside,
                jnp.where(lane == first + c, 1.0, 0.0),
                jnp.broadcast_to(tiles[top][c : c + 1, :], shape),
            )
            for c in range(SUB)
        ]
        scales = []
        for c in range(SUB):
            inverse = 1.0 / core[c, c]
            scales.append(inverse)
            for d in range(c + 1, SUB):
                factor = core[c, d] * inverse
                for e in range(d, SUB):
                    core[d, e] = core[d, e] - factor * core[c, e]
                lines[d] = lines[d] - factor * lines[c]
                for t in range(1, count - top):
                    columns[d][t] = columns[d][t] - factor * columns[c][t]
        for t in range(1, count - top):
            rest = jnp.where(inside, 0.0, tiles[top + t])
            for c in range(SUB):
                rest = rest - columns[c][t] * (scales[c] * lines[c])
            tiles[top + t] = rest
        merged = lines[0]
        pivot = core[0, 0]
        for c in range(1, SUB):
            merged = jnp.where(sub == c, lines[c], merged)
            pivot = jnp.where(sub == c, core[c, c], pivot)
        kept = jnp.where(lane <= sub + first, merged, 0.0)
        out_ref[first : first + SUB, :] = kept * (1.0 / jnp.sqrt(pivot))


def factor_inverse(gram):
    size = gram.shape[0]
    return pl.pallas_call(
        inverse_kernel,
        out_shape=jax.ShapeDtypeStruct(gram.shape, f32),
        compiler_params=pltpu.CompilerParams(vmem_limit_bytes=VMEM_BYTES),
        cost_estimate=pl.CostEstimate(
            flops=40 * size**4, bytes_accessed=8 * size * size, transcendentals=0
        ),
        name="factor_inverse",
    )(gram)


def weight_kernel(coef_ref, across_ref, down_ref, spread):
    rows, groups, _, lanes = spread.shape
    places = groups * SUB
    turned = coef_ref[...].T
    depth = turned.shape[1]
    pieces = jnp.concatenate(split3(turned[:places]), axis=1)
    per_step = rows // 4
    offset = iota((3 * depth, per_step * lanes), 0) & (depth - 1)
    offset = offset - (iota((3 * depth, per_step * lanes), 1) // lanes)

    def put(c, carry):
        values = dot(pieces, (offset == c * per_step).astype(f32).astype(bf16))
        for h in range(per_step):
            spread[c * per_step + h] = values[:, h * lanes : (h + 1) * lanes].reshape(
                groups, SUB, lanes
            )
        return carry

    lax.fori_loop(0, 4, put, 0)

    def weigh(r, carry):
        for g in range(groups):
            here = spread[r, g]
            east = spread[r, g + 1] if g + 1 < groups else pltpu.roll(spread[r, 0], SUB - 1, 0)
            across_ref[r, g] = 0.124 * (here + east)
            down_ref[r, g] = 0.124 * (here + spread[r + 1, g])
        return carry

    lax.fori_loop(0, rows - 1, weigh, 0)
    across_ref[rows - 1] = jnp.zeros((groups, SUB, lanes), f32)
    down_ref[rows - 1] = jnp.zeros((groups, SUB, lanes), f32)


def weights(coef, lanes):
    rows, places = coef.shape
    coef = jnp.pad(coef, ((0, -rows % 64), (0, -places % LANES)))
    shape = (rows, places // SUB, SUB, lanes)
    return pl.pallas_call(
        weight_kernel,
        out_shape=(jax.ShapeDtypeStruct(shape, f32),) * 2,
        scratch_shapes=[pltpu.VMEM(shape, f32)],
        compiler_params=pltpu.CompilerParams(vmem_limit_bytes=VMEM_BYTES),
        cost_estimate=pl.CostEstimate(
            flops=rows * places * lanes * 100, bytes_accessed=8 * rows * places * lanes, transcendentals=0
        ),
        name="weights",
    )(coef)


def rotation(inverse):
    high, mid, low = split3(inverse.T)
    return jnp.concatenate(
        [jnp.concatenate([high, low], axis=1), jnp.concatenate([mid, jnp.zeros_like(mid)], axis=1)],
        axis=0,
    )


def rotated(raw, turn):
    lanes = raw.shape[1]
    parts = dot(jnp.concatenate([raw, raw], axis=1), turn)
    return (parts[:, :lanes] + parts[:, lanes:]).astype(bf16).astype(f32)


def update(src, dst, across, down, sums, row, take):
    groups = src.shape[1]
    last = groups - 1
    span = range(take)
    start = [src[row + r, 0] for r in span]
    closing = [
        across[row + r, last] * (pltpu.roll(start[r], SUB - 1, 0) - src[row + r, last])
        for r in span
    ]
    wrapped = [pltpu.roll(flux, 1, 0) for flux in closing]

    def vertical(g, here):
        above = down[row - 1, g] * (here[0] - src[row - 1, g])
        change = []
        for r in span:
            below = here[r + 1] if r + 1 < take else src[row + take, g]
            under = down[row + r, g] * (below - here[r])
            change.append(under - above)
            above = under
        return change

    def finish(r, g, new):
        dst[row + r, g] = new
        sums[row + r, g] += new * new

    here = [src[row + r, 1] for r in span]
    west = [across[row + r, 0] * (here[r] - start[r]) for r in span]
    change = vertical(0, start)
    pending = [start[r] + (change[r] + west[r]) for r in span]
    for g in range(1, groups):
        if g < last:
            following = [src[row + r, g + 1] for r in span]
            flux = [across[row + r, g] * (following[r] - here[r]) for r in span]
        else:
            following, flux = None, closing
        change = vertical(g, here)
        for r in span:
            finish(r, g, here[r] + (change[r] + (flux[r] - west[r])))
        here, west = following, flux
    for r in span:
        finish(r, 0, pending[r] - wrapped[r])


def summed_lanes(sums, rows, totals):
    lane = iota(totals[0].shape, 1)
    for row, to in rows:
        for g in range(len(totals)):
            total = jnp.sum(sums[row, g], axis=1, keepdims=True)
            totals[g] = totals[g] + jnp.where(lane == to, total, 0.0)
    return totals


def inner_kernel(
    own_ref, inverse_ref, across_hbm, down_hbm, first_ref, second_ref, total_ref,
    across_ref, down_ref, sum_ref, sems,
):
    tall, groups, _, lanes = first_ref.shape
    inside = pl.ds(HALO, tall)
    fetches = [
        pltpu.make_async_copy(across_hbm.at[inside], across_ref, sems.at[0]),
        pltpu.make_async_copy(down_hbm.at[inside], down_ref, sems.at[1]),
    ]
    for fetch in fetches:
        fetch.start()
    turn = rotation(inverse_ref[...])
    take = 4
    cells = take * groups * SUB

    def fill(c, carry):
        field = rotated(own_ref[pl.ds(pl.multiple_of(c * cells, 16), cells), :], turn)
        first_ref[pl.ds(c * take, take)] = field.reshape(take, groups, SUB, lanes)
        return carry

    lax.fori_loop(0, tall // take, fill, 0)
    sum_ref[...] = jnp.zeros_like(sum_ref)
    second_ref[0] = jnp.zeros(second_ref.shape[1:], f32)
    second_ref[tall - 1] = jnp.zeros(second_ref.shape[1:], f32)
    for fetch in fetches:
        fetch.wait()

    def sweep(s, src, dst, odd_pair):
        count = tall - 2 - 2 * s

        def step(c, carry):
            update(src, dst, across_ref, down_ref, sum_ref, s + 1 + c * BLOCK, BLOCK)
            return carry

        lax.fori_loop(0, count // BLOCK, step, 0)
        if odd_pair:
            update(src, dst, across_ref, down_ref, sum_ref, s + count - 1, 2)

    def two(t, carry):
        sweep(2 * t, first_ref, second_ref, (tall - 2) % BLOCK == 2)
        sweep(2 * t + 1, second_ref, first_ref, (tall - 4) % BLOCK == 2)
        return carry

    lax.fori_loop(0, SWEEPS // 2, two, 0)

    def gather(c, totals):
        rows = [(c * 4 + h, c * 4 + h) for h in range(4)]
        return tuple(summed_lanes(sum_ref, rows, list(totals)))

    zeros = tuple(jnp.zeros((SUB, lanes), f32) for _ in range(groups))
    totals = lax.fori_loop(0, tall // 4, gather, zeros)
    total_ref[...] = jnp.concatenate(totals, axis=0)


def inner_sweeps(own, inverse, across_down):
    tall, places, lanes = own.shape
    own = own.reshape(tall * places, lanes)
    vmem = pl.BlockSpec(memory_space=pltpu.VMEM)
    far = pl.BlockSpec(memory_space=pl.ANY)
    shape = (tall, places // SUB, SUB, lanes)
    return pl.pallas_call(
        inner_kernel,
        out_shape=(
            jax.ShapeDtypeStruct(shape, f32),
            jax.ShapeDtypeStruct(shape, f32),
            jax.ShapeDtypeStruct((places, lanes), f32),
        ),
        in_specs=[vmem, vmem, far, far],
        out_specs=(vmem, vmem, vmem),
        scratch_shapes=[
            pltpu.VMEM(shape, f32),
            pltpu.VMEM(shape, f32),
            pltpu.VMEM(shape, f32),
            pltpu.SemaphoreType.DMA((2,)),
        ],
        compiler_params=pltpu.CompilerParams(vmem_limit_bytes=VMEM_BYTES),
        cost_estimate=pl.CostEstimate(
            flops=12 * 10**9, bytes_accessed=8 * own.size, transcendentals=0
        ),
        name="inner_sweeps",
    )(own, inverse, *across_down)


def outer_kernel(
    scale, ends_ref, north_ref, south_ref, inverse_ref, inner_ref, first_hbm, second_hbm,
    across_hbm, down_hbm, out_ref, first_ref, second_ref, across_ref, down_ref, sum_ref, sems,
):
    rows, groups, _, lanes = first_ref.shape
    tall = rows - 2 * HALO
    places = groups * SUB
    near = HALO + 1
    fetches = []
    for k, (source, target) in enumerate(((first_hbm, first_ref), (second_hbm, second_ref))):
        for side, row in enumerate((0, tall - near)):
            fetches.append(
                pltpu.make_async_copy(
                    source.at[pl.ds(row, near)],
                    target.at[pl.ds(HALO + row, near)],
                    sems.at[2 * k + side],
                )
            )
    wide_part = 2 * HALO + 1
    for k, (source, target) in enumerate(((across_hbm, across_ref), (down_hbm, down_ref))):
        for side, row in enumerate((0, rows - wide_part)):
            part = pl.ds(row, wide_part)
            fetches.append(
                pltpu.make_async_copy(source.at[part], target.at[part], sems.at[4 + 2 * k + side])
            )
    for fetch in fetches:
        fetch.start()
    sum_ref[...] = jnp.zeros_like(sum_ref)
    turn = rotation(inverse_ref[...])
    take = 2
    cells = take * places

    def fill(c, carry):
        for source, offset in ((north_ref, 0), (south_ref, HALO + tall)):
            field = rotated(source[pl.ds(pl.multiple_of(c * cells, 16), cells), :], turn)
            first_ref[pl.ds(offset + c * take, take)] = field.reshape(take, groups, SUB, lanes)
        return carry

    lax.fori_loop(0, HALO // take, fill, 0)
    take = HALO // 2
    for fetch in fetches:
        fetch.wait()

    def sweep(s, src, dst):
        def step(c, carry):
            bottom = c // 2
            row = jnp.where(bottom == 0, s + 1, rows - 1 - HALO - s) + (c % 2) * take
            update(src, dst, across_ref, down_ref, sum_ref, row, take)
            return carry

        lax.fori_loop(0, 4, step, 0)

        @pl.when(ends_ref[0] == 1)
        def _():
            dst[HALO - 1] = jnp.zeros(dst.shape[1:], f32)

        @pl.when(ends_ref[1] == 1)
        def _():
            dst[HALO + tall] = jnp.zeros(dst.shape[1:], f32)

    def two(t, carry):
        sweep(2 * t, first_ref, second_ref)
        sweep(2 * t + 1, second_ref, first_ref)
        return carry

    lax.fori_loop(0, SWEEPS // 2, two, 0)

    def gather(c, totals):
        pairs = []
        for row in (2 * c, 2 * c + 1):
            pairs += [(HALO + row, row), (tall + row, tall - HALO + row)]
        return tuple(summed_lanes(sum_ref, pairs, list(totals)))

    totals = tuple(inner_ref[g * SUB : (g + 1) * SUB, :] for g in range(groups))
    totals = lax.fori_loop(0, HALO // 2, gather, totals)
    totals = jnp.concatenate(totals, axis=0).T[:tall]
    slot = iota((places, out_ref.shape[1]), 0)
    column = iota((places, out_ref.shape[1]), 1)
    back = (column == (slot % SUB) * groups + slot // SUB).astype(f32).astype(bf16)
    high, mid, low = split3(totals)
    out_ref[...] = (dot(high, back) + (dot(mid, back) + dot(low, back))) * scale


def outer_sweeps(scale, ends, north, south, inverse, inner, across_down, wide):
    first, second, total = inner
    tall, groups, _, lanes = first.shape
    shape = (tall + 2 * HALO, groups, SUB, lanes)
    north, south = (x.reshape(-1, lanes) for x in (north, south))
    vmem = pl.BlockSpec(memory_space=pltpu.VMEM)
    far = pl.BlockSpec(memory_space=pl.ANY)
    return pl.pallas_call(
        functools.partial(outer_kernel, scale),
        out_shape=jax.ShapeDtypeStruct((tall, wide), f32),
        in_specs=[pl.BlockSpec(memory_space=pltpu.SMEM)] + [vmem] * 4 + [far] * 4,
        out_specs=vmem,
        scratch_shapes=[pltpu.VMEM(shape, f32)] * 5 + [pltpu.SemaphoreType.DMA((8,))],
        compiler_params=pltpu.CompilerParams(vmem_limit_bytes=VMEM_BYTES),
        name="outer_sweeps",
    )(ends, north, south, inverse, total, first, second, *across_down)


def from_before(x, axis, closed):
    count = lax.axis_size(axis)
    return lax.ppermute(
        x, axis, [(i, (i + 1) % count) for i in range(count if closed else count - 1)]
    )


def from_after(x, axis, closed):
    count = lax.axis_size(axis)
    return lax.ppermute(
        x, axis, [((i + 1) % count, i) for i in range(count if closed else count - 1)]
    )


def ahead(values, axis, step):
    count = lax.axis_size(axis)
    return lax.ppermute(values, axis, [((i + step) % count, i) for i in range(count)])


def neighbours(x, extra, axis):
    size = x.shape[0]
    sent = jnp.concatenate([x, extra], axis=0)
    after, before, second = ahead(sent, axis, 1), ahead(sent, axis, -1), ahead(x, axis, 2)
    x = (x + before[:size]) + (after[:size] + second)
    return x, before[size:], after[size:]


def rest_of_ring(x, axis):
    step = 4
    while step < lax.axis_size(axis):
        x = x + ahead(x, axis, step)
        step *= 2
    return x


def per_device(basis, order, land, conduct):
    axes = ("lat", "lon")
    rows_here, width = basis.shape
    tall, wide = land.shape
    count = lax.axis_size("lat") * lax.axis_size("lon")
    cells = rows_here * count
    tied = lax.optimization_barrier
    at = lax.axis_index("lat")
    top, bottom = at == 0, at == lax.axis_size("lat") - 1
    whole_rows = rows_here // count == wide

    def dealt(part, so_far):
        if not whole_rows:
            return basis[order] if so_far is None else so_far
        bounds = [0, 3 * tall // 8, 5 * tall // 8, tall]
        return deal(
            basis, order, lax.axis_size("lon"), wide, bounds[part],
            bounds[part + 1] - bounds[part], so_far,
        )

    partial = lax.dot_general(
        basis, basis, (((0,), (0,)), ((), ())), preferred_element_type=f32
    )
    coef = conduct * (0.35 + 0.65 * land.astype(f32))
    edges = jnp.pad(
        jnp.concatenate([coef[:, :HALO], coef[:, -HALO:]], axis=1),
        ((0, 0), (0, width - 2 * HALO)),
    )
    partial, edges, basis = tied((partial, edges, basis))
    moving = dealt(0, None)
    partial, before, after = neighbours(partial, edges, "lon")
    partial, moving = tied((partial, moving))
    moving = dealt(1, moving)
    partial = rest_of_ring(partial, "lon")
    coef = circle(coef, after[:, :HALO], before[:, HALO : 2 * HALO], 1)
    ends = jnp.concatenate([coef[:HALO], coef[-HALO:]], axis=0)
    rest = coef.shape[1] - width
    edges = jnp.concatenate(
        [ends[:, :width], jnp.pad(ends[:, width:], ((0, 0), (0, width - rest)))], axis=0
    )
    partial, edges, moving = tied((partial, edges, moving))
    moving = dealt(2, moving)
    partial, before, after = neighbours(partial, edges, "lat")
    gram = rest_of_ring(partial, "lat")
    gram, before, after, moving = tied((gram, before, after, moving))

    raw = lax.all_to_all(moving, axes, split_axis=0, concat_axis=0, tiled=True)
    if not whole_rows:
        raw = raw.reshape(tall, wide, width)
        left = from_before(raw[:, -HALO:], "lon", True)
        right = from_after(raw[:, :HALO], "lon", True)
        raw = circle(raw, right, left, 1)

    before = jnp.concatenate([before[: 2 * HALO], before[2 * HALO :, :rest]], axis=1)[HALO:]
    after = jnp.concatenate([after[: 2 * HALO], after[2 * HALO :, :rest]], axis=1)[:HALO]
    coef = jnp.concatenate(
        [jnp.where(top, 0.0, before), coef, jnp.where(bottom, 0.0, after)], axis=0
    )
    inverse = factor_inverse(gram)
    across_down = weights(coef, width)
    ends = jnp.stack([top, bottom]).astype(i32)
    raw, inverse, across_down, ends = tied((raw, inverse, across_down, ends))

    north = from_before(raw[-HALO:], "lat", False)
    south = from_after(raw[:HALO], "lat", False)
    inner = inner_sweeps(raw, inverse, across_down)
    scale = cells / (width * SWEEPS)
    return outer_sweeps(scale, ends, north, south, inverse, inner, across_down, wide)


def solution(mesh):
    in_specs = (P(("lat", "lon"), None), P(("lat", "lon")), P("lat", "lon"), P("lat", "lon"))
    out_specs = P("lat", "lon")
    return jax.shard_map(
        per_device, mesh=mesh, in_specs=in_specs, out_specs=out_specs, check_vma=False
    )
```

```python
import functools

import jax
import jax.numpy as jnp
from jax import lax
from jax.experimental import pallas as pl
from jax.experimental.pallas import tpu as pltpu
from jax.sharding import PartitionSpec as P

SWEEPS = 10
HALO = SWEEPS
LANES = 128
SUB = 8
ONE_HOT = 1024
TILES = 4
BLOCK = 4
VMEM_BYTES = 56 * 1024 * 1024

bf16, f32, i32 = jnp.bfloat16, jnp.float32, jnp.int32


def iota(shape, dim):
    return lax.broadcasted_iota(i32, shape, dim)


def dot(a, b):
    return jnp.dot(a, b, preferred_element_type=f32)


def split3(x):
    high = x.astype(bf16)
    rest = x - high.astype(f32)
    mid = rest.astype(bf16)
    low = (rest - mid.astype(f32)).astype(bf16)
    return high, mid, low


def slots(wide):
    return -(-(wide + 2 * HALO) // SUB) * SUB


def circle(own, right, left, axis):
    wide = own.shape[axis]
    count = slots(wide)
    gap = list(own.shape)
    gap[axis] = count - wide - 2 * HALO
    around = jnp.concatenate([own, right, jnp.zeros(gap, own.dtype), left], axis=axis)
    shape = around.shape
    around = around.reshape(shape[:axis] + (SUB, count // SUB) + shape[axis + 1 :])
    return jnp.swapaxes(around, axis, axis + 1).reshape(shape)


def deal_kernel(tiles_lon, basis_ref, order_ref, out_ref, slot_ref, ready_ref, sems):
    rows, width = basis_ref.shape
    parts = rows // ONE_HOT
    tiles, places, _ = out_ref.shape
    wide = order_ref.shape[1]
    groups = places // SUB
    stacked = jnp.concatenate(
        [basis_ref[q * ONE_HOT : (q + 1) * ONE_HOT, :] for q in range(parts)], axis=1
    )

    order = order_ref[...]
    at = iota(order.shape, 0) % tiles_lon
    after = jnp.where(
        at == tiles_lon - 1, pltpu.roll(order, tiles_lon - 1, 0), pltpu.roll(order, tiles - 1, 0)
    )
    before = jnp.where(
        at == 0, pltpu.roll(order, tiles - tiles_lon + 1, 0), pltpu.roll(order, 1, 0)
    )
    padded = slot_ref.shape[1]
    column = iota((wide, padded), 0)
    slot = iota((wide, padded), 1)
    place = jnp.where(slot < places, (slot % SUB) * groups + slot // SUB, -1)
    low = jnp.zeros((tiles, padded), f32)
    high = low
    for source, hit in (
        (order, (place < wide) & (column == place)),
        (after, (place < wide + HALO) & (column == place - wide)),
        (before, (place >= places - HALO) & (column == place - places + wide)),
    ):
        hot = hit.astype(f32).astype(bf16)
        low = low + dot((source & 63).astype(f32).astype(bf16), hot)
        high = high + dot((source >> 6).astype(f32).astype(bf16), hot)
    slot_ref[...] = (high * 64.0 + low).astype(i32)

    take = TILES
    steps = tiles // take

    def leave(c):
        return pltpu.make_async_copy(
            ready_ref.at[pl.ds(c * take, take)],
            out_ref.at[pl.ds(c * take, take)],
            sems.at[c],
        )

    lane = iota((take * places, LANES), 1)

    def step(c, carry):
        wanted = []
        for h in range(take):
            order = slot_ref[pl.ds(c * take + h, 1), :]
            wanted.append(jnp.broadcast_to(order, (LANES, padded)).T[:places])
        wanted = jnp.concatenate(wanted, axis=0)
        within = wanted & (ONE_HOT - 1)
        part = wanted - within
        marks = [
            (within == lane + b * LANES).astype(f32).astype(bf16)
            for b in range(ONE_HOT // LANES)
        ]
        found = dot(jnp.concatenate(marks, axis=1), stacked)
        picked = found[:, :width]
        for q in range(1, parts):
            picked = jnp.where(
                part == q * ONE_HOT, found[:, q * width : (q + 1) * width], picked
            )
        for h in range(take):
            ready_ref[c * take + h] = picked[h * places : (h + 1) * places].astype(bf16)
        leave(c).start()
        return carry

    lax.fori_loop(0, steps, step, 0)
    for c in range(steps):
        leave(c).wait()


def deal(basis, order, tiles_lon, wide):
    rows, width = basis.shape
    tiles = rows // wide
    places = slots(wide)
    vmem = pl.BlockSpec(memory_space=pltpu.VMEM)
    return pl.pallas_call(
        functools.partial(deal_kernel, tiles_lon),
        out_shape=jax.ShapeDtypeStruct((tiles, places, width), bf16),
        in_specs=[vmem, vmem],
        out_specs=pl.BlockSpec(memory_space=pl.ANY),
        scratch_shapes=[
            pltpu.VMEM((tiles, -(-places // LANES) * LANES), i32),
            pltpu.VMEM((tiles, places, width), bf16),
            pltpu.SemaphoreType.DMA((tiles // TILES,)),
        ],
        compiler_params=pltpu.CompilerParams(vmem_limit_bytes=VMEM_BYTES),
        cost_estimate=pl.CostEstimate(
            flops=2 * tiles * places * rows * width,
            bytes_accessed=4 * rows * width,
            transcendentals=0,
        ),
        name="deal",
    )(basis, order.reshape(tiles, wide))


def inverse_kernel(gram_ref, out_ref):
    size = gram_ref.shape[0]
    count = size // SUB
    shape = (SUB, size)
    tiles = [gram_ref[t * SUB : (t + 1) * SUB, :] for t in range(count)]
    lane = iota(shape, 1)
    sub = iota(shape, 0)
    for top in range(count):
        first = top * SUB
        inside = (lane >= first) & (lane < first + SUB)
        columns = [
            [jnp.broadcast_to(tiles[t][:, first + c : first + c + 1], shape) for t in range(top, count)]
            for c in range(SUB)
        ]
        core = {
            (r, c): jnp.broadcast_to(columns[c][0][r : r + 1, :], shape)
            for r in range(SUB)
            for c in range(r, SUB)
        }
        lines = [
            jnp.where(
                inside,
                jnp.where(lane == first + c, 1.0, 0.0),
                jnp.broadcast_to(tiles[top][c : c + 1, :], shape),
            )
            for c in range(SUB)
        ]
        scales = []
        for c in range(SUB):
            inverse = 1.0 / core[c, c]
            scales.append(inverse)
            for d in range(c + 1, SUB):
                factor = core[c, d] * inverse
                for e in range(d, SUB):
                    core[d, e] = core[d, e] - factor * core[c, e]
                lines[d] = lines[d] - factor * lines[c]
                for t in range(1, count - top):
                    columns[d][t] = columns[d][t] - factor * columns[c][t]
        for t in range(1, count - top):
            rest = jnp.where(inside, 0.0, tiles[top + t])
            for c in range(SUB):
                rest = rest - columns[c][t] * (scales[c] * lines[c])
            tiles[top + t] = rest
        merged = lines[0]
        pivot = core[0, 0]
        for c in range(1, SUB):
            merged = jnp.where(sub == c, lines[c], merged)
            pivot = jnp.where(sub == c, core[c, c], pivot)
        kept = jnp.where(lane <= sub + first, merged, 0.0)
        out_ref[first : first + SUB, :] = kept * (1.0 / jnp.sqrt(pivot))


def factor_inverse(gram):
    size = gram.shape[0]
    return pl.pallas_call(
        inverse_kernel,
        out_shape=jax.ShapeDtypeStruct(gram.shape, f32),
        compiler_params=pltpu.CompilerParams(vmem_limit_bytes=VMEM_BYTES),
        cost_estimate=pl.CostEstimate(
            flops=40 * size**4, bytes_accessed=8 * size * size, transcendentals=0
        ),
        name="factor_inverse",
    )(gram)


def weight_kernel(coef_ref, across_ref, down_ref, spread):
    rows, groups, _, lanes = spread.shape
    places = groups * SUB
    turned = coef_ref[...].T
    depth = turned.shape[1]
    pieces = jnp.concatenate(split3(turned[:places]), axis=1)
    per_step = rows // 4
    offset = iota((3 * depth, per_step * lanes), 0) & (depth - 1)
    offset = offset - (iota((3 * depth, per_step * lanes), 1) // lanes)

    def put(c, carry):
        values = dot(pieces, (offset == c * per_step).astype(f32).astype(bf16))
        for h in range(per_step):
            spread[c * per_step + h] = values[:, h * lanes : (h + 1) * lanes].reshape(
                groups, SUB, lanes
            )
        return carry

    lax.fori_loop(0, 4, put, 0)

    def weigh(r, carry):
        for g in range(groups):
            here = spread[r, g]
            east = spread[r, g + 1] if g + 1 < groups else pltpu.roll(spread[r, 0], SUB - 1, 0)
            across_ref[r, g] = 0.124 * (here + east)
            down_ref[r, g] = 0.124 * (here + spread[r + 1, g])
        return carry

    lax.fori_loop(0, rows - 1, weigh, 0)
    across_ref[rows - 1] = jnp.zeros((groups, SUB, lanes), f32)
    down_ref[rows - 1] = jnp.zeros((groups, SUB, lanes), f32)


def weights(coef, lanes):
    rows, places = coef.shape
    coef = jnp.pad(coef, ((0, -rows % 64), (0, -places % LANES)))
    shape = (rows, places // SUB, SUB, lanes)
    return pl.pallas_call(
        weight_kernel,
        out_shape=(jax.ShapeDtypeStruct(shape, f32),) * 2,
        scratch_shapes=[pltpu.VMEM(shape, f32)],
        compiler_params=pltpu.CompilerParams(vmem_limit_bytes=VMEM_BYTES),
        cost_estimate=pl.CostEstimate(
            flops=rows * places * lanes * 100, bytes_accessed=8 * rows * places * lanes, transcendentals=0
        ),
        name="weights",
    )(coef)


def rotation(inverse):
    high, mid, low = split3(inverse.T)
    return jnp.concatenate(
        [jnp.concatenate([high, low], axis=1), jnp.concatenate([mid, jnp.zeros_like(mid)], axis=1)],
        axis=0,
    )


def rotated(raw, turn):
    lanes = raw.shape[1]
    parts = dot(jnp.concatenate([raw, raw], axis=1), turn)
    return (parts[:, :lanes] + parts[:, lanes:]).astype(bf16).astype(f32)


def update(src, dst, across, down, sums, row, take):
    groups = src.shape[1]
    last = groups - 1
    span = range(take)
    start = [src[row + r, 0] for r in span]
    closing = [
        across[row + r, last] * (pltpu.roll(start[r], SUB - 1, 0) - src[row + r, last])
        for r in span
    ]
    wrapped = [pltpu.roll(flux, 1, 0) for flux in closing]

    def vertical(g, here):
        above = down[row - 1, g] * (here[0] - src[row - 1, g])
        change = []
        for r in span:
            below = here[r + 1] if r + 1 < take else src[row + take, g]
            under = down[row + r, g] * (below - here[r])
            change.append(under - above)
            above = under
        return change

    def finish(r, g, new):
        dst[row + r, g] = new
        sums[row + r, g] += new * new

    here = [src[row + r, 1] for r in span]
    west = [across[row + r, 0] * (here[r] - start[r]) for r in span]
    change = vertical(0, start)
    pending = [start[r] + (change[r] + west[r]) for r in span]
    for g in range(1, groups):
        if g < last:
            following = [src[row + r, g + 1] for r in span]
            flux = [across[row + r, g] * (following[r] - here[r]) for r in span]
        else:
            following, flux = None, closing
        change = vertical(g, here)
        for r in span:
            finish(r, g, here[r] + (change[r] + (flux[r] - west[r])))
        here, west = following, flux
    for r in span:
        finish(r, 0, pending[r] - wrapped[r])


def summed_lanes(sums, rows, totals):
    lane = iota(totals[0].shape, 1)
    for row, to in rows:
        for g in range(len(totals)):
            total = jnp.sum(sums[row, g], axis=1, keepdims=True)
            totals[g] = totals[g] + jnp.where(lane == to, total, 0.0)
    return totals


def inner_kernel(
    own_ref, inverse_ref, across_hbm, down_hbm, first_hbm, second_hbm, total_ref,
    first_ref, second_ref, across_ref, down_ref, sum_ref, sems,
):
    tall, groups, _, lanes = first_ref.shape
    inside = pl.ds(HALO, tall)
    fetches = [
        pltpu.make_async_copy(across_hbm.at[inside], across_ref, sems.at[0]),
        pltpu.make_async_copy(down_hbm.at[inside], down_ref, sems.at[1]),
    ]
    for fetch in fetches:
        fetch.start()
    turn = rotation(inverse_ref[...])
    take = 4
    cells = take * groups * SUB

    def fill(c, carry):
        field = rotated(own_ref[pl.ds(pl.multiple_of(c * cells, 16), cells), :], turn)
        first_ref[pl.ds(c * take, take)] = field.reshape(take, groups, SUB, lanes)
        return carry

    lax.fori_loop(0, tall // take, fill, 0)
    sum_ref[...] = jnp.zeros_like(sum_ref)
    second_ref[0] = jnp.zeros(second_ref.shape[1:], f32)
    second_ref[tall - 1] = jnp.zeros(second_ref.shape[1:], f32)
    for fetch in fetches:
        fetch.wait()

    def sweep(s, src, dst, odd_pair):
        count = tall - 2 - 2 * s

        def step(c, carry):
            update(src, dst, across_ref, down_ref, sum_ref, s + 1 + c * BLOCK, BLOCK)
            return carry

        lax.fori_loop(0, count // BLOCK, step, 0)
        if odd_pair:
            update(src, dst, across_ref, down_ref, sum_ref, s + count - 1, 2)

    def two(t, carry):
        sweep(2 * t, first_ref, second_ref, (tall - 2) % BLOCK == 2)
        sweep(2 * t + 1, second_ref, first_ref, (tall - 4) % BLOCK == 2)
        return carry

    lax.fori_loop(0, SWEEPS // 2, two, 0)

    near = HALO + 1
    leaving = []
    for k, (source, target) in enumerate(((first_ref, first_hbm), (second_ref, second_hbm))):
        for side, row in enumerate((0, tall - near)):
            part = pl.ds(row, near)
            leaving.append(
                pltpu.make_async_copy(source.at[part], target.at[part], sems.at[2 + 2 * k + side])
            )
    for copy in leaving:
        copy.start()

    def gather(c, totals):
        rows = [(c * 4 + h, c * 4 + h) for h in range(4)]
        return tuple(summed_lanes(sum_ref, rows, list(totals)))

    zeros = tuple(jnp.zeros((SUB, lanes), f32) for _ in range(groups))
    totals = lax.fori_loop(0, tall // 4, gather, zeros)
    total_ref[...] = jnp.concatenate(totals, axis=0)
    for copy in leaving:
        copy.wait()


def inner_sweeps(own, inverse, across_down):
    tall, places, lanes = own.shape
    own = own.reshape(tall * places, lanes)
    vmem = pl.BlockSpec(memory_space=pltpu.VMEM)
    far = pl.BlockSpec(memory_space=pl.ANY)
    shape = (tall, places // SUB, SUB, lanes)
    return pl.pallas_call(
        inner_kernel,
        out_shape=(
            jax.ShapeDtypeStruct(shape, f32),
            jax.ShapeDtypeStruct(shape, f32),
            jax.ShapeDtypeStruct((places, lanes), f32),
        ),
        in_specs=[vmem, vmem, far, far],
        out_specs=(far, far, vmem),
        scratch_shapes=[pltpu.VMEM(shape, f32)] * 5 + [pltpu.SemaphoreType.DMA((6,))],
        compiler_params=pltpu.CompilerParams(vmem_limit_bytes=VMEM_BYTES),
        cost_estimate=pl.CostEstimate(
            flops=12 * 10**9, bytes_accessed=8 * own.size, transcendentals=0
        ),
        name="inner_sweeps",
    )(own, inverse, *across_down)


def outer_kernel(
    scale, ends_ref, north_ref, south_ref, inverse_ref, inner_ref, first_hbm, second_hbm,
    across_hbm, down_hbm, out_ref, first_ref, second_ref, across_ref, down_ref, sum_ref, sems,
):
    rows, groups, _, lanes = first_ref.shape
    tall = rows - 2 * HALO
    places = groups * SUB
    near = HALO + 1
    fetches = []
    for k, (source, target) in enumerate(((first_hbm, first_ref), (second_hbm, second_ref))):
        for side, row in enumerate((0, tall - near)):
            fetches.append(
                pltpu.make_async_copy(
                    source.at[pl.ds(row, near)],
                    target.at[pl.ds(HALO + row, near)],
                    sems.at[2 * k + side],
                )
            )
    wide_part = 2 * HALO + 1
    for k, (source, target) in enumerate(((across_hbm, across_ref), (down_hbm, down_ref))):
        for side, row in enumerate((0, rows - wide_part)):
            part = pl.ds(row, wide_part)
            fetches.append(
                pltpu.make_async_copy(source.at[part], target.at[part], sems.at[4 + 2 * k + side])
            )
    for fetch in fetches:
        fetch.start()
    sum_ref[...] = jnp.zeros_like(sum_ref)
    turn = rotation(inverse_ref[...])
    take = 2
    cells = take * places

    def fill(c, carry):
        for source, offset in ((north_ref, 0), (south_ref, HALO + tall)):
            field = rotated(source[pl.ds(pl.multiple_of(c * cells, 16), cells), :], turn)
            first_ref[pl.ds(offset + c * take, take)] = field.reshape(take, groups, SUB, lanes)
        return carry

    lax.fori_loop(0, HALO // take, fill, 0)
    take = HALO // 2
    for fetch in fetches:
        fetch.wait()

    def sweep(s, src, dst):
        def step(c, carry):
            bottom = c // 2
            row = jnp.where(bottom == 0, s + 1, rows - 1 - HALO - s) + (c % 2) * take
            update(src, dst, across_ref, down_ref, sum_ref, row, take)
            return carry

        lax.fori_loop(0, 4, step, 0)

        @pl.when(ends_ref[0] == 1)
        def _():
            dst[HALO - 1] = jnp.zeros(dst.shape[1:], f32)

        @pl.when(ends_ref[1] == 1)
        def _():
            dst[HALO + tall] = jnp.zeros(dst.shape[1:], f32)

    def two(t, carry):
        sweep(2 * t, first_ref, second_ref)
        sweep(2 * t + 1, second_ref, first_ref)
        return carry

    lax.fori_loop(0, SWEEPS // 2, two, 0)

    def gather(c, totals):
        pairs = []
        for row in (2 * c, 2 * c + 1):
            pairs += [(HALO + row, row), (tall + row, tall - HALO + row)]
        return tuple(summed_lanes(sum_ref, pairs, list(totals)))

    totals = tuple(inner_ref[g * SUB : (g + 1) * SUB, :] for g in range(groups))
    totals = lax.fori_loop(0, HALO // 2, gather, totals)
    totals = jnp.concatenate(totals, axis=0).T[:tall]
    slot = iota((places, out_ref.shape[1]), 0)
    column = iota((places, out_ref.shape[1]), 1)
    back = (column == (slot % SUB) * groups + slot // SUB).astype(f32).astype(bf16)
    high, mid, low = split3(totals)
    out_ref[...] = (dot(high, back) + (dot(mid, back) + dot(low, back))) * scale


def outer_sweeps(scale, ends, north, south, inverse, inner, across_down, wide):
    first, second, total = inner
    tall, groups, _, lanes = first.shape
    shape = (tall + 2 * HALO, groups, SUB, lanes)
    north, south = (x.reshape(-1, lanes) for x in (north, south))
    vmem = pl.BlockSpec(memory_space=pltpu.VMEM)
    far = pl.BlockSpec(memory_space=pl.ANY)
    return pl.pallas_call(
        functools.partial(outer_kernel, scale),
        out_shape=jax.ShapeDtypeStruct((tall, wide), f32),
        in_specs=[pl.BlockSpec(memory_space=pltpu.SMEM)] + [vmem] * 4 + [far] * 4,
        out_specs=vmem,
        scratch_shapes=[pltpu.VMEM(shape, f32)] * 5 + [pltpu.SemaphoreType.DMA((8,))],
        compiler_params=pltpu.CompilerParams(vmem_limit_bytes=VMEM_BYTES),
        name="outer_sweeps",
    )(ends, north, south, inverse, total, first, second, *across_down)


def from_before(x, axis, closed):
    count = lax.axis_size(axis)
    return lax.ppermute(
        x, axis, [(i, (i + 1) % count) for i in range(count if closed else count - 1)]
    )


def from_after(x, axis, closed):
    count = lax.axis_size(axis)
    return lax.ppermute(
        x, axis, [((i + 1) % count, i) for i in range(count if closed else count - 1)]
    )


def ahead(values, axis, step):
    count = lax.axis_size(axis)
    return lax.ppermute(values, axis, [((i + step) % count, i) for i in range(count)])


def neighbours(x, extra, axis):
    size = x.shape[0]
    sent = jnp.concatenate([x, extra], axis=0)
    after, before, second = ahead(sent, axis, 1), ahead(sent, axis, -1), ahead(x, axis, 2)
    x = (x + before[:size]) + (after[:size] + second)
    return x, before[size:], after[size:]


def rest_of_ring(x, axis):
    step = 4
    while step < lax.axis_size(axis):
        x = x + ahead(x, axis, step)
        step *= 2
    return x


def per_device(basis, order, land, conduct):
    axes = ("lat", "lon")
    rows_here, width = basis.shape
    tall, wide = land.shape
    count = lax.axis_size("lat") * lax.axis_size("lon")
    cells = rows_here * count
    tied = lax.optimization_barrier
    at = lax.axis_index("lat")
    top, bottom = at == 0, at == lax.axis_size("lat") - 1

    whole_rows = rows_here // count == wide
    moving = deal(basis, order, lax.axis_size("lon"), wide) if whole_rows else basis[order]
    moving, basis = tied((moving, basis))
    raw = lax.all_to_all(moving, axes, split_axis=0, concat_axis=0, tiled=True)
    if not whole_rows:
        raw = raw.reshape(tall, wide, width)
        left = from_before(raw[:, -HALO:], "lon", True)
        right = from_after(raw[:, :HALO], "lon", True)
        raw = circle(raw, right, left, 1)

    partial = lax.dot_general(
        basis, basis, (((0,), (0,)), ((), ())), preferred_element_type=f32
    )
    coef = conduct * (0.35 + 0.65 * land.astype(f32))
    edges = jnp.concatenate([coef[:HALO], coef[-HALO:]], axis=0)
    edges = jnp.pad(edges, ((0, 4), (0, width - wide)))
    partial, before, after = neighbours(partial, edges, "lat")
    partial = rest_of_ring(partial, "lat")
    before = jnp.where(top, 0.0, before[HALO : 2 * HALO, :wide])
    after = jnp.where(bottom, 0.0, after[:HALO, :wide])
    coef = jnp.concatenate([before, coef, after], axis=0)
    edges = jnp.concatenate([coef[:, :HALO], coef[:, -HALO:]], axis=1)
    edges = jnp.pad(edges, ((0, 4), (0, width - 2 * HALO)))
    partial, before, after = neighbours(partial, edges, "lon")
    rows = coef.shape[0]
    coef = circle(coef, after[:rows, :HALO], before[:rows, HALO : 2 * HALO], 1)
    gram = rest_of_ring(partial, "lon")
    inverse = factor_inverse(gram)
    across_down = weights(coef, width)
    ends = jnp.stack([top, bottom]).astype(i32)
    raw, inverse, across_down, ends = tied((raw, inverse, across_down, ends))

    north = from_before(raw[-HALO:], "lat", False)
    south = from_after(raw[:HALO], "lat", False)
    inner = inner_sweeps(raw, inverse, across_down)
    scale = cells / (width * SWEEPS)
    return outer_sweeps(scale, ends, north, south, inverse, inner, across_down, wide)


def solution(mesh):
    in_specs = (P(("lat", "lon"), None), P(("lat", "lon")), P("lat", "lon"), P("lat", "lon"))
    out_specs = P("lat", "lon")
    return jax.shard_map(
        per_device, mesh=mesh, in_specs=in_specs, out_specs=out_specs, check_vma=False
    )
```

```python
import functools

import jax
import jax.numpy as jnp
from jax import lax
from jax.experimental import pallas as pl
from jax.experimental.pallas import tpu as pltpu
from jax.sharding import PartitionSpec as P

SWEEPS = 10
HALO = SWEEPS
LANES = 128
SUB = 8
ONE_HOT = 1024
TILES = 4
BLOCK = 4
VMEM_BYTES = 56 * 1024 * 1024

bf16, f32, i32 = jnp.bfloat16, jnp.float32, jnp.int32


def iota(shape, dim):
    return lax.broadcasted_iota(i32, shape, dim)


def dot(a, b):
    return jnp.dot(a, b, preferred_element_type=f32)


def split3(x):
    high = x.astype(bf16)
    rest = x - high.astype(f32)
    mid = rest.astype(bf16)
    low = (rest - mid.astype(f32)).astype(bf16)
    return high, mid, low


def slots(wide):
    return -(-(wide + 2 * HALO) // SUB) * SUB


def circle(own, right, left, axis):
    wide = own.shape[axis]
    count = slots(wide)
    gap = list(own.shape)
    gap[axis] = count - wide - 2 * HALO
    around = jnp.concatenate([own, right, jnp.zeros(gap, own.dtype), left], axis=axis)
    shape = around.shape
    around = around.reshape(shape[:axis] + (SUB, count // SUB) + shape[axis + 1 :])
    return jnp.swapaxes(around, axis, axis + 1).reshape(shape)


def deal_kernel(tiles_lon, basis_ref, order_ref, out_ref, slot_ref, ready_ref, sems):
    rows, width = basis_ref.shape
    parts = rows // ONE_HOT
    tiles, places, _ = out_ref.shape
    wide = order_ref.shape[1]
    groups = places // SUB
    stacked = jnp.concatenate(
        [basis_ref[q * ONE_HOT : (q + 1) * ONE_HOT, :] for q in range(parts)], axis=1
    )

    order = order_ref[...]
    at = iota(order.shape, 0) % tiles_lon
    after = jnp.where(
        at == tiles_lon - 1, pltpu.roll(order, tiles_lon - 1, 0), pltpu.roll(order, tiles - 1, 0)
    )
    before = jnp.where(
        at == 0, pltpu.roll(order, tiles - tiles_lon + 1, 0), pltpu.roll(order, 1, 0)
    )
    padded = slot_ref.shape[1]
    column = iota((wide, padded), 0)
    slot = iota((wide, padded), 1)
    place = jnp.where(slot < places, (slot % SUB) * groups + slot // SUB, -1)
    sources, hits = [], []
    for source, hit in (
        (order, (place < wide) & (column == place)),
        (after, (place < wide + HALO) & (column == place - wide)),
        (before, (place >= places - HALO) & (column == place - places + wide)),
    ):
        hits.append(hit.astype(f32).astype(bf16))
        halves = jnp.concatenate([source & 63, source >> 6], axis=0)
        sources.append(halves.astype(f32).astype(bf16))
    halves = dot(jnp.concatenate(sources, axis=1), jnp.concatenate(hits, axis=0))
    slot_ref[...] = (halves[tiles:] * 64.0 + halves[:tiles]).astype(i32)

    take = TILES
    steps = tiles // take

    def leave(c):
        return pltpu.make_async_copy(
            ready_ref.at[pl.ds(c * take, take)],
            out_ref.at[pl.ds(c * take, take)],
            sems.at[c],
        )

    lane = iota((take * places, LANES), 1)

    for c in range(steps):
        wanted = []
        for h in range(take):
            order = slot_ref[c * take + h : c * take + h + 1, :]
            wanted.append(jnp.broadcast_to(order, (LANES, padded)).T[:places])
        wanted = jnp.concatenate(wanted, axis=0)
        within = wanted & (ONE_HOT - 1)
        part = wanted - within
        marks = [
            (within == lane + b * LANES).astype(f32).astype(bf16)
            for b in range(ONE_HOT // LANES)
        ]
        found = dot(jnp.concatenate(marks, axis=1), stacked)
        picked = found[:, :width]
        for q in range(1, parts):
            picked = jnp.where(
                part == q * ONE_HOT, found[:, q * width : (q + 1) * width], picked
            )
        for h in range(take):
            ready_ref[c * take + h] = picked[h * places : (h + 1) * places].astype(bf16)
        leave(c).start()
    for c in range(steps):
        leave(c).wait()


def deal(basis, order, tiles_lon, wide):
    rows, width = basis.shape
    tiles = rows // wide
    places = slots(wide)
    vmem = pl.BlockSpec(memory_space=pltpu.VMEM)
    return pl.pallas_call(
        functools.partial(deal_kernel, tiles_lon),
        out_shape=jax.ShapeDtypeStruct((tiles, places, width), bf16),
        in_specs=[vmem, vmem],
        out_specs=pl.BlockSpec(memory_space=pl.ANY),
        scratch_shapes=[
            pltpu.VMEM((tiles, -(-places // LANES) * LANES), i32),
            pltpu.VMEM((tiles, places, width), bf16),
            pltpu.SemaphoreType.DMA((tiles // TILES,)),
        ],
        compiler_params=pltpu.CompilerParams(vmem_limit_bytes=VMEM_BYTES),
        cost_estimate=pl.CostEstimate(
            flops=2 * tiles * places * rows * width,
            bytes_accessed=4 * rows * width,
            transcendentals=0,
        ),
        name="deal",
    )(basis, order.reshape(tiles, wide))


def inverse_kernel(gram_ref, out_ref):
    size = gram_ref.shape[0]
    count = size // SUB
    shape = (SUB, size)
    tiles = [gram_ref[t * SUB : (t + 1) * SUB, :] for t in range(count)]
    lane = iota(shape, 1)
    sub = iota(shape, 0)
    for top in range(count):
        first = top * SUB
        inside = (lane >= first) & (lane < first + SUB)
        columns = [
            [jnp.broadcast_to(tiles[t][:, first + c : first + c + 1], shape) for t in range(top, count)]
            for c in range(SUB)
        ]
        core = {
            (r, c): jnp.broadcast_to(columns[c][0][r : r + 1, :], shape)
            for r in range(SUB)
            for c in range(r, SUB)
        }
        lines = [
            jnp.where(
                inside,
                jnp.where(lane == first + c, 1.0, 0.0),
                jnp.broadcast_to(tiles[top][c : c + 1, :], shape),
            )
            for c in range(SUB)
        ]
        scales = []
        for c in range(SUB):
            inverse = 1.0 / core[c, c]
            scales.append(inverse)
            for d in range(c + 1, SUB):
                factor = core[c, d] * inverse
                for e in range(d, SUB):
                    core[d, e] = core[d, e] - factor * core[c, e]
                lines[d] = lines[d] - factor * lines[c]
                for t in range(1, count - top):
                    columns[d][t] = columns[d][t] - factor * columns[c][t]
        for t in range(1, count - top):
            rest = jnp.where(inside, 0.0, tiles[top + t])
            for c in range(SUB):
                rest = rest - columns[c][t] * (scales[c] * lines[c])
            tiles[top + t] = rest
        merged = lines[0]
        pivot = core[0, 0]
        for c in range(1, SUB):
            merged = jnp.where(sub == c, lines[c], merged)
            pivot = jnp.where(sub == c, core[c, c], pivot)
        kept = jnp.where(lane <= sub + first, merged, 0.0)
        out_ref[first : first + SUB, :] = kept * (1.0 / jnp.sqrt(pivot))


def factor_inverse(gram):
    size = gram.shape[0]
    return pl.pallas_call(
        inverse_kernel,
        out_shape=jax.ShapeDtypeStruct(gram.shape, f32),
        compiler_params=pltpu.CompilerParams(vmem_limit_bytes=VMEM_BYTES),
        cost_estimate=pl.CostEstimate(
            flops=40 * size**4, bytes_accessed=8 * size * size, transcendentals=0
        ),
        name="factor_inverse",
    )(gram)


def weight_kernel(coef_ref, across_ref, down_ref, spread):
    rows, groups, _, lanes = spread.shape
    places = groups * SUB
    turned = coef_ref[...].T
    depth = turned.shape[1]
    pieces = jnp.concatenate(split3(turned[:places]), axis=1)
    per_step = rows // 4
    offset = iota((3 * depth, per_step * lanes), 0) & (depth - 1)
    offset = offset - (iota((3 * depth, per_step * lanes), 1) // lanes)

    def put(c, carry):
        values = dot(pieces, (offset == c * per_step).astype(f32).astype(bf16))
        for h in range(per_step):
            spread[c * per_step + h] = values[:, h * lanes : (h + 1) * lanes].reshape(
                groups, SUB, lanes
            )
        return carry

    lax.fori_loop(0, 4, put, 0)

    def weigh(r, carry):
        for g in range(groups):
            here = spread[r, g]
            east = spread[r, g + 1] if g + 1 < groups else pltpu.roll(spread[r, 0], SUB - 1, 0)
            across_ref[r, g] = 0.124 * (here + east)
            down_ref[r, g] = 0.124 * (here + spread[r + 1, g])
        return carry

    lax.fori_loop(0, rows - 1, weigh, 0)
    across_ref[rows - 1] = jnp.zeros((groups, SUB, lanes), f32)
    down_ref[rows - 1] = jnp.zeros((groups, SUB, lanes), f32)


def weights(coef, lanes):
    rows, places = coef.shape
    coef = jnp.pad(coef, ((0, -rows % 64), (0, -places % LANES)))
    shape = (rows, places // SUB, SUB, lanes)
    return pl.pallas_call(
        weight_kernel,
        out_shape=(jax.ShapeDtypeStruct(shape, f32),) * 2,
        scratch_shapes=[pltpu.VMEM(shape, f32)],
        compiler_params=pltpu.CompilerParams(vmem_limit_bytes=VMEM_BYTES),
        cost_estimate=pl.CostEstimate(
            flops=rows * places * lanes * 100, bytes_accessed=8 * rows * places * lanes, transcendentals=0
        ),
        name="weights",
    )(coef)


def rotation(inverse):
    high, mid, low = split3(inverse.T)
    return jnp.concatenate(
        [jnp.concatenate([high, low], axis=1), jnp.concatenate([mid, jnp.zeros_like(mid)], axis=1)],
        axis=0,
    )


def rotated(raw, turn):
    lanes = raw.shape[1]
    parts = dot(jnp.concatenate([raw, raw], axis=1), turn)
    return (parts[:, :lanes] + parts[:, lanes:]).astype(bf16).astype(f32)


def update(src, dst, across, down, sums, row, take):
    groups = src.shape[1]
    last = groups - 1
    span = range(take)
    start = [src[row + r, 0] for r in span]
    closing = [
        across[row + r, last] * (pltpu.roll(start[r], SUB - 1, 0) - src[row + r, last])
        for r in span
    ]
    wrapped = [pltpu.roll(flux, 1, 0) for flux in closing]

    def vertical(g, here):
        above = down[row - 1, g] * (here[0] - src[row - 1, g])
        change = []
        for r in span:
            below = here[r + 1] if r + 1 < take else src[row + take, g]
            under = down[row + r, g] * (below - here[r])
            change.append(under - above)
            above = under
        return change

    def finish(r, g, new):
        dst[row + r, g] = new
        sums[row + r, g] += new * new

    here = [src[row + r, 1] for r in span]
    west = [across[row + r, 0] * (here[r] - start[r]) for r in span]
    change = vertical(0, start)
    pending = [start[r] + (change[r] + west[r]) for r in span]
    for g in range(1, groups):
        if g < last:
            following = [src[row + r, g + 1] for r in span]
            flux = [across[row + r, g] * (following[r] - here[r]) for r in span]
        else:
            following, flux = None, closing
        change = vertical(g, here)
        for r in span:
            finish(r, g, here[r] + (change[r] + (flux[r] - west[r])))
        here, west = following, flux
    for r in span:
        finish(r, 0, pending[r] - wrapped[r])


def summed_lanes(sums, rows, totals):
    lane = iota(totals[0].shape, 1)
    for row, to in rows:
        for g in range(len(totals)):
            total = jnp.sum(sums[row, g], axis=1, keepdims=True)
            totals[g] = totals[g] + jnp.where(lane == to, total, 0.0)
    return totals


def inner_kernel(
    own_ref, inverse_ref, across_hbm, down_hbm, first_hbm, second_hbm, total_ref,
    first_ref, second_ref, across_ref, down_ref, sum_ref, sems,
):
    tall, groups, _, lanes = first_ref.shape
    inside = pl.ds(HALO, tall)
    fetches = [
        pltpu.make_async_copy(across_hbm.at[inside], across_ref, sems.at[0]),
        pltpu.make_async_copy(down_hbm.at[inside], down_ref, sems.at[1]),
    ]
    for fetch in fetches:
        fetch.start()
    turn = rotation(inverse_ref[...])
    take = 4
    cells = take * groups * SUB

    def fill(c, carry):
        field = rotated(own_ref[pl.ds(pl.multiple_of(c * cells, 16), cells), :], turn)
        first_ref[pl.ds(c * take, take)] = field.reshape(take, groups, SUB, lanes)
        return carry

    lax.fori_loop(0, tall // take, fill, 0)
    sum_ref[...] = jnp.zeros_like(sum_ref)
    second_ref[0] = jnp.zeros(second_ref.shape[1:], f32)
    second_ref[tall - 1] = jnp.zeros(second_ref.shape[1:], f32)
    for fetch in fetches:
        fetch.wait()

    for s in range(SWEEPS):
        src, dst = (first_ref, second_ref) if s % 2 == 0 else (second_ref, first_ref)
        count = tall - 2 - 2 * s
        steps = count // (2 * BLOCK)

        def step(c, carry):
            for h in range(2):
                row = s + 1 + (2 * c + h) * BLOCK
                update(src, dst, across_ref, down_ref, sum_ref, row, BLOCK)
            return carry

        lax.fori_loop(0, steps, step, 0)
        done = steps * 2 * BLOCK
        while done < count:
            take = min(BLOCK, count - done)
            update(src, dst, across_ref, down_ref, sum_ref, s + 1 + done, take)
            done += take

    near = HALO + 1
    leaving = []
    for k, (source, target) in enumerate(((first_ref, first_hbm), (second_ref, second_hbm))):
        for side, row in enumerate((0, tall - near)):
            part = pl.ds(row, near)
            leaving.append(
                pltpu.make_async_copy(source.at[part], target.at[part], sems.at[2 + 2 * k + side])
            )
    for copy in leaving:
        copy.start()

    def gather(c, totals):
        rows = [(c * 4 + h, c * 4 + h) for h in range(4)]
        return tuple(summed_lanes(sum_ref, rows, list(totals)))

    zeros = tuple(jnp.zeros((SUB, lanes), f32) for _ in range(groups))
    totals = lax.fori_loop(0, tall // 4, gather, zeros)
    total_ref[...] = jnp.concatenate(totals, axis=0)
    for copy in leaving:
        copy.wait()


def inner_sweeps(own, inverse, across_down):
    tall, places, lanes = own.shape
    own = own.reshape(tall * places, lanes)
    vmem = pl.BlockSpec(memory_space=pltpu.VMEM)
    far = pl.BlockSpec(memory_space=pl.ANY)
    shape = (tall, places // SUB, SUB, lanes)
    return pl.pallas_call(
        inner_kernel,
        out_shape=(
            jax.ShapeDtypeStruct(shape, f32),
            jax.ShapeDtypeStruct(shape, f32),
            jax.ShapeDtypeStruct((places, lanes), f32),
        ),
        in_specs=[vmem, vmem, far, far],
        out_specs=(far, far, vmem),
        scratch_shapes=[pltpu.VMEM(shape, f32)] * 5 + [pltpu.SemaphoreType.DMA((6,))],
        compiler_params=pltpu.CompilerParams(vmem_limit_bytes=VMEM_BYTES),
        cost_estimate=pl.CostEstimate(
            flops=12 * 10**9, bytes_accessed=8 * own.size, transcendentals=0
        ),
        name="inner_sweeps",
    )(own, inverse, *across_down)


def outer_kernel(
    scale, ends_ref, inverse_ref, inner_ref, north_hbm, south_hbm, first_hbm, second_hbm,
    across_hbm, down_hbm, out_ref, first_ref, second_ref, across_ref, down_ref, sum_ref,
    north_ref, south_ref, sems,
):
    rows, groups, _, lanes = first_ref.shape
    tall = rows - 2 * HALO
    places = groups * SUB
    near = HALO + 1
    halos = [
        pltpu.make_async_copy(north_hbm, north_ref, sems.at[8]),
        pltpu.make_async_copy(south_hbm, south_ref, sems.at[9]),
    ]
    for halo in halos:
        halo.start()
    fetches = []
    for k, (source, target) in enumerate(((first_hbm, first_ref), (second_hbm, second_ref))):
        for side, row in enumerate((0, tall - near)):
            fetches.append(
                pltpu.make_async_copy(
                    source.at[pl.ds(row, near)],
                    target.at[pl.ds(HALO + row, near)],
                    sems.at[2 * k + side],
                )
            )
    wide_part = 2 * HALO + 1
    for k, (source, target) in enumerate(((across_hbm, across_ref), (down_hbm, down_ref))):
        for side, row in enumerate((0, rows - wide_part)):
            part = pl.ds(row, wide_part)
            fetches.append(
                pltpu.make_async_copy(source.at[part], target.at[part], sems.at[4 + 2 * k + side])
            )
    for fetch in fetches:
        fetch.start()
    sum_ref[...] = jnp.zeros_like(sum_ref)
    turn = rotation(inverse_ref[...])
    for halo in halos:
        halo.wait()
    take = 2
    cells = take * places

    def fill(c, carry):
        for source, offset in ((north_ref, 0), (south_ref, HALO + tall)):
            field = rotated(source[pl.ds(pl.multiple_of(c * cells, 16), cells), :], turn)
            first_ref[pl.ds(offset + c * take, take)] = field.reshape(take, groups, SUB, lanes)
        return carry

    lax.fori_loop(0, HALO // take, fill, 0)
    take = HALO // 2
    for fetch in fetches:
        fetch.wait()

    def sweep(s, src, dst):
        for start in (s + 1, rows - 1 - HALO - s):
            for c in range(HALO // take):
                update(src, dst, across_ref, down_ref, sum_ref, start + c * take, take)

        @pl.when(ends_ref[0] == 1)
        def _():
            dst[HALO - 1] = jnp.zeros(dst.shape[1:], f32)

        @pl.when(ends_ref[1] == 1)
        def _():
            dst[HALO + tall] = jnp.zeros(dst.shape[1:], f32)

    def two(t, carry):
        sweep(2 * t, first_ref, second_ref)
        sweep(2 * t + 1, second_ref, first_ref)
        return carry

    lax.fori_loop(0, SWEEPS // 2, two, 0)

    def gather(c, totals):
        pairs = []
        for row in (2 * c, 2 * c + 1):
            pairs += [(HALO + row, row), (tall + row, tall - HALO + row)]
        return tuple(summed_lanes(sum_ref, pairs, list(totals)))

    totals = tuple(inner_ref[g * SUB : (g + 1) * SUB, :] for g in range(groups))
    totals = lax.fori_loop(0, HALO // 2, gather, totals)
    totals = jnp.concatenate(totals, axis=0).T[:tall]
    slot = iota((places, out_ref.shape[1]), 0)
    column = iota((places, out_ref.shape[1]), 1)
    back = (column == (slot % SUB) * groups + slot // SUB).astype(f32).astype(bf16)
    high, mid, low = split3(totals)
    out_ref[...] = (dot(high, back) + (dot(mid, back) + dot(low, back))) * scale


def outer_sweeps(scale, ends, north, south, inverse, inner, across_down, wide):
    first, second, total = inner
    tall, groups, _, lanes = first.shape
    shape = (tall + 2 * HALO, groups, SUB, lanes)
    north, south = (x.reshape(-1, lanes) for x in (north, south))
    vmem = pl.BlockSpec(memory_space=pltpu.VMEM)
    far = pl.BlockSpec(memory_space=pl.ANY)
    return pl.pallas_call(
        functools.partial(outer_kernel, scale),
        out_shape=jax.ShapeDtypeStruct((tall, wide), f32),
        in_specs=[pl.BlockSpec(memory_space=pltpu.SMEM)] + [vmem] * 2 + [far] * 6,
        out_specs=vmem,
        scratch_shapes=[pltpu.VMEM(shape, f32)] * 5
        + [pltpu.VMEM(north.shape, bf16)] * 2
        + [pltpu.SemaphoreType.DMA((10,))],
        compiler_params=pltpu.CompilerParams(vmem_limit_bytes=VMEM_BYTES // 2),
        name="outer_sweeps",
    )(ends, inverse, total, north, south, first, second, *across_down)


def from_before(x, axis, closed):
    count = lax.axis_size(axis)
    return lax.ppermute(
        x, axis, [(i, (i + 1) % count) for i in range(count if closed else count - 1)]
    )


def from_after(x, axis, closed):
    count = lax.axis_size(axis)
    return lax.ppermute(
        x, axis, [((i + 1) % count, i) for i in range(count if closed else count - 1)]
    )


def ahead(values, axis, step):
    count = lax.axis_size(axis)
    return lax.ppermute(values, axis, [((i + step) % count, i) for i in range(count)])


def neighbours(x, extra, axis):
    size = x.shape[0]
    sent = jnp.concatenate([x, extra], axis=0)
    after, before, second = ahead(sent, axis, 1), ahead(sent, axis, -1), ahead(x, axis, 2)
    x = (x + before[:size]) + (after[:size] + second)
    return x, before[size:], after[size:]


def rest_of_ring(x, axis):
    step = 4
    while step < lax.axis_size(axis):
        x = x + ahead(x, axis, step)
        step *= 2
    return x


def per_device(basis, order, land, conduct):
    axes = ("lat", "lon")
    rows_here, width = basis.shape
    tall, wide = land.shape
    count = lax.axis_size("lat") * lax.axis_size("lon")
    cells = rows_here * count
    tied = lax.optimization_barrier
    at = lax.axis_index("lat")
    top, bottom = at == 0, at == lax.axis_size("lat") - 1

    whole_rows = rows_here // count == wide
    moving = deal(basis, order, lax.axis_size("lon"), wide) if whole_rows else basis[order]
    moving, basis, land, conduct = tied((moving, basis, land, conduct))
    raw = lax.all_to_all(moving, axes, split_axis=0, concat_axis=0, tiled=True)
    if not whole_rows:
        raw = raw.reshape(tall, wide, width)
        left = from_before(raw[:, -HALO:], "lon", True)
        right = from_after(raw[:, :HALO], "lon", True)
        raw = circle(raw, right, left, 1)

    partial = lax.dot_general(
        basis, basis, (((0,), (0,)), ((), ())), preferred_element_type=f32
    )
    coef = conduct * (0.35 + 0.65 * land.astype(f32))
    edges = jnp.concatenate([coef[:HALO], coef[-HALO:]], axis=0)
    edges = jnp.pad(edges, ((0, 4), (0, width - wide)))
    partial, before, after = neighbours(partial, edges, "lat")
    partial = rest_of_ring(partial, "lat")
    before = jnp.where(top, 0.0, before[HALO : 2 * HALO, :wide])
    after = jnp.where(bottom, 0.0, after[:HALO, :wide])
    coef = jnp.concatenate([before, coef, after], axis=0)
    edges = jnp.concatenate([coef[:, :HALO], coef[:, -HALO:]], axis=1)
    edges = jnp.pad(edges, ((0, 4), (0, width - 2 * HALO)))
    partial, before, after = neighbours(partial, edges, "lon")
    rows = coef.shape[0]
    coef = circle(coef, after[:rows, :HALO], before[:rows, HALO : 2 * HALO], 1)
    gram = rest_of_ring(partial, "lon")
    inverse = factor_inverse(gram)
    across_down = weights(coef, width)
    ends = jnp.stack([top, bottom]).astype(i32)
    raw, inverse, across_down, ends = tied((raw, inverse, across_down, ends))

    north = from_before(raw[-HALO:], "lat", False)
    south = from_after(raw[:HALO], "lat", False)
    inner = inner_sweeps(raw, inverse, across_down)
    scale = cells / (width * SWEEPS)
    return outer_sweeps(scale, ends, north, south, inverse, inner, across_down, wide)


def solution(mesh):
    in_specs = (P(("lat", "lon"), None), P(("lat", "lon")), P("lat", "lon"), P("lat", "lon"))
    out_specs = P("lat", "lon")
    return jax.shard_map(
        per_device, mesh=mesh, in_specs=in_specs, out_specs=out_specs, check_vma=False
    )
```

```python
import functools

import jax
import jax.numpy as jnp
from jax import lax
from jax.experimental import pallas as pl
from jax.experimental.pallas import tpu as pltpu
from jax.sharding import PartitionSpec as P

SWEEPS = 10
HALO = SWEEPS
LANES = 128
SUB = 8
ONE_HOT = 1024
TILES = 4
BLOCK = 4
VMEM_BYTES = 56 * 1024 * 1024

bf16, f32, i32 = jnp.bfloat16, jnp.float32, jnp.int32


def iota(shape, dim):
    return lax.broadcasted_iota(i32, shape, dim)


def dot(a, b):
    return jnp.dot(a, b, preferred_element_type=f32)


def split3(x):
    high = x.astype(bf16)
    rest = x - high.astype(f32)
    mid = rest.astype(bf16)
    low = (rest - mid.astype(f32)).astype(bf16)
    return high, mid, low


def slots(wide):
    return -(-(wide + 2 * HALO) // SUB) * SUB


def circle(own, right, left, axis):
    wide = own.shape[axis]
    count = slots(wide)
    gap = list(own.shape)
    gap[axis] = count - wide - 2 * HALO
    around = jnp.concatenate([own, right, jnp.zeros(gap, own.dtype), left], axis=axis)
    shape = around.shape
    around = around.reshape(shape[:axis] + (SUB, count // SUB) + shape[axis + 1 :])
    return jnp.swapaxes(around, axis, axis + 1).reshape(shape)


def deal_kernel(tiles_lon, basis_ref, order_ref, out_ref, slot_ref, ready_ref, sems):
    rows, width = basis_ref.shape
    parts = rows // ONE_HOT
    tiles, places, _ = out_ref.shape
    wide = order_ref.shape[1]
    groups = places // SUB
    stacked = jnp.concatenate(
        [basis_ref[q * ONE_HOT : (q + 1) * ONE_HOT, :] for q in range(parts)], axis=1
    )

    order = order_ref[...]
    at = iota(order.shape, 0) % tiles_lon
    after = jnp.where(
        at == tiles_lon - 1, pltpu.roll(order, tiles_lon - 1, 0), pltpu.roll(order, tiles - 1, 0)
    )
    before = jnp.where(
        at == 0, pltpu.roll(order, tiles - tiles_lon + 1, 0), pltpu.roll(order, 1, 0)
    )
    padded = slot_ref.shape[1]
    column = iota((wide, padded), 0)
    slot = iota((wide, padded), 1)
    place = jnp.where(slot < places, (slot % SUB) * groups + slot // SUB, -1)
    sources, hits = [], []
    for source, hit in (
        (order, (place < wide) & (column == place)),
        (after, (place < wide + HALO) & (column == place - wide)),
        (before, (place >= places - HALO) & (column == place - places + wide)),
    ):
        hits.append(hit.astype(f32).astype(bf16))
        halves = jnp.concatenate([source & 63, source >> 6], axis=0)
        sources.append(halves.astype(f32).astype(bf16))
    halves = dot(jnp.concatenate(sources, axis=1), jnp.concatenate(hits, axis=0))
    slot_ref[...] = (halves[tiles:] * 64.0 + halves[:tiles]).astype(i32)

    take = TILES
    steps = tiles // take

    def leave(c):
        return pltpu.make_async_copy(
            ready_ref.at[pl.ds(c * take, take)],
            out_ref.at[pl.ds(c * take, take)],
            sems.at[c],
        )

    lane = iota((take * places, LANES), 1)

    for c in range(steps):
        wanted = []
        for h in range(take):
            order = slot_ref[c * take + h : c * take + h + 1, :]
            wanted.append(jnp.broadcast_to(order, (LANES, padded)).T[:places])
        wanted = jnp.concatenate(wanted, axis=0)
        within = wanted & (ONE_HOT - 1)
        part = wanted - within
        marks = [
            (within == lane + b * LANES).astype(f32).astype(bf16)
            for b in range(ONE_HOT // LANES)
        ]
        found = dot(jnp.concatenate(marks, axis=1), stacked)
        picked = found[:, :width]
        for q in range(1, parts):
            picked = jnp.where(
                part == q * ONE_HOT, found[:, q * width : (q + 1) * width], picked
            )
        for h in range(take):
            ready_ref[c * take + h] = picked[h * places : (h + 1) * places].astype(bf16)
        leave(c).start()
    for c in range(steps):
        leave(c).wait()


def deal(basis, order, tiles_lon, wide):
    rows, width = basis.shape
    tiles = rows // wide
    places = slots(wide)
    vmem = pl.BlockSpec(memory_space=pltpu.VMEM)
    return pl.pallas_call(
        functools.partial(deal_kernel, tiles_lon),
        out_shape=jax.ShapeDtypeStruct((tiles, places, width), bf16),
        in_specs=[vmem, vmem],
        out_specs=pl.BlockSpec(memory_space=pl.ANY),
        scratch_shapes=[
            pltpu.VMEM((tiles, -(-places // LANES) * LANES), i32),
            pltpu.VMEM((tiles, places, width), bf16),
            pltpu.SemaphoreType.DMA((tiles // TILES,)),
        ],
        compiler_params=pltpu.CompilerParams(vmem_limit_bytes=VMEM_BYTES),
        cost_estimate=pl.CostEstimate(
            flops=2 * tiles * places * rows * width,
            bytes_accessed=4 * rows * width,
            transcendentals=0,
        ),
        name="deal",
    )(basis, order.reshape(tiles, wide))


def inverse_kernel(gram_ref, out_ref):
    size = gram_ref.shape[0]
    count = size // SUB
    shape = (SUB, size)
    tiles = [gram_ref[t * SUB : (t + 1) * SUB, :] for t in range(count)]
    lane = iota(shape, 1)
    sub = iota(shape, 0)
    for top in range(count):
        first = top * SUB
        inside = (lane >= first) & (lane < first + SUB)
        columns = [
            [jnp.broadcast_to(tiles[t][:, first + c : first + c + 1], shape) for t in range(top, count)]
            for c in range(SUB)
        ]
        core = {
            (r, c): jnp.broadcast_to(columns[c][0][r : r + 1, :], shape)
            for r in range(SUB)
            for c in range(r, SUB)
        }
        lines = [
            jnp.where(
                inside,
                jnp.where(lane == first + c, 1.0, 0.0),
                jnp.broadcast_to(tiles[top][c : c + 1, :], shape),
            )
            for c in range(SUB)
        ]
        scales = []
        for c in range(SUB):
            inverse = 1.0 / core[c, c]
            scales.append(inverse)
            for d in range(c + 1, SUB):
                factor = core[c, d] * inverse
                for e in range(d, SUB):
                    core[d, e] = core[d, e] - factor * core[c, e]
                lines[d] = lines[d] - factor * lines[c]
                for t in range(1, count - top):
                    columns[d][t] = columns[d][t] - factor * columns[c][t]
        for t in range(1, count - top):
            rest = jnp.where(inside, 0.0, tiles[top + t])
            for c in range(SUB):
                rest = rest - columns[c][t] * (scales[c] * lines[c])
            tiles[top + t] = rest
        merged = lines[0]
        pivot = core[0, 0]
        for c in range(1, SUB):
            merged = jnp.where(sub == c, lines[c], merged)
            pivot = jnp.where(sub == c, core[c, c], pivot)
        kept = jnp.where(lane <= sub + first, merged, 0.0)
        out_ref[first : first + SUB, :] = kept * (1.0 / jnp.sqrt(pivot))


def factor_inverse(gram):
    size = gram.shape[0]
    return pl.pallas_call(
        inverse_kernel,
        out_shape=jax.ShapeDtypeStruct(gram.shape, f32),
        compiler_params=pltpu.CompilerParams(vmem_limit_bytes=VMEM_BYTES),
        cost_estimate=pl.CostEstimate(
            flops=40 * size**4, bytes_accessed=8 * size * size, transcendentals=0
        ),
        name="factor_inverse",
    )(gram)


def weight_kernel(coef_ref, across_ref, down_ref, spread):
    rows, groups, _, lanes = spread.shape
    places = groups * SUB
    turned = coef_ref[...].T
    depth = turned.shape[1]
    pieces = jnp.concatenate(split3(turned[:places]), axis=1)
    per_step = rows // 4
    offset = iota((3 * depth, per_step * lanes), 0) & (depth - 1)
    offset = offset - (iota((3 * depth, per_step * lanes), 1) // lanes)

    def put(c, carry):
        values = dot(pieces, (offset == c * per_step).astype(f32).astype(bf16))
        for h in range(per_step):
            spread[c * per_step + h] = values[:, h * lanes : (h + 1) * lanes].reshape(
                groups, SUB, lanes
            )
        return carry

    lax.fori_loop(0, 4, put, 0)

    def weigh(r, carry):
        for g in range(groups):
            here = spread[r, g]
            east = spread[r, g + 1] if g + 1 < groups else pltpu.roll(spread[r, 0], SUB - 1, 0)
            across_ref[r, g] = 0.124 * (here + east)
            down_ref[r, g] = 0.124 * (here + spread[r + 1, g])
        return carry

    lax.fori_loop(0, rows - 1, weigh, 0)
    across_ref[rows - 1] = jnp.zeros((groups, SUB, lanes), f32)
    down_ref[rows - 1] = jnp.zeros((groups, SUB, lanes), f32)


def weights(coef, lanes):
    rows, places = coef.shape
    coef = jnp.pad(coef, ((0, -rows % 64), (0, -places % LANES)))
    shape = (rows, places // SUB, SUB, lanes)
    return pl.pallas_call(
        weight_kernel,
        out_shape=(jax.ShapeDtypeStruct(shape, f32),) * 2,
        scratch_shapes=[pltpu.VMEM(shape, f32)],
        compiler_params=pltpu.CompilerParams(vmem_limit_bytes=VMEM_BYTES),
        cost_estimate=pl.CostEstimate(
            flops=rows * places * lanes * 100, bytes_accessed=8 * rows * places * lanes, transcendentals=0
        ),
        name="weights",
    )(coef)


def rotation(inverse):
    high, mid, low = split3(inverse.T)
    return jnp.concatenate(
        [jnp.concatenate([high, low], axis=1), jnp.concatenate([mid, jnp.zeros_like(mid)], axis=1)],
        axis=0,
    )


def rotated(raw, turn):
    lanes = raw.shape[1]
    parts = dot(jnp.concatenate([raw, raw], axis=1), turn)
    return (parts[:, :lanes] + parts[:, lanes:]).astype(bf16).astype(f32)


def update(src, dst, across, down, sums, row, take):
    groups = src.shape[1]
    last = groups - 1
    span = range(take)
    start = [src[row + r, 0] for r in span]
    closing = [
        across[row + r, last] * (pltpu.roll(start[r], SUB - 1, 0) - src[row + r, last])
        for r in span
    ]
    wrapped = [pltpu.roll(flux, 1, 0) for flux in closing]

    def vertical(g, here):
        above = down[row - 1, g] * (here[0] - src[row - 1, g])
        change = []
        for r in span:
            below = here[r + 1] if r + 1 < take else src[row + take, g]
            under = down[row + r, g] * (below - here[r])
            change.append(under - above)
            above = under
        return change

    def finish(r, g, new):
        dst[row + r, g] = new
        sums[row + r, g] += new * new

    here = [src[row + r, 1] for r in span]
    west = [across[row + r, 0] * (here[r] - start[r]) for r in span]
    change = vertical(0, start)
    pending = [start[r] + (change[r] + west[r]) for r in span]
    for g in range(1, groups):
        if g < last:
            following = [src[row + r, g + 1] for r in span]
            flux = [across[row + r, g] * (following[r] - here[r]) for r in span]
        else:
            following, flux = None, closing
        change = vertical(g, here)
        for r in span:
            finish(r, g, here[r] + (change[r] + (flux[r] - west[r])))
        here, west = following, flux
    for r in span:
        finish(r, 0, pending[r] - wrapped[r])


def summed_lanes(sums, rows, totals):
    lane = iota(totals[0].shape, 1)
    for row, to in rows:
        for g in range(len(totals)):
            total = jnp.sum(sums[row, g], axis=1, keepdims=True)
            totals[g] = totals[g] + jnp.where(lane == to, total, 0.0)
    return totals


def inner_kernel(
    own_ref, inverse_ref, across_hbm, down_hbm, first_hbm, second_hbm, total_ref,
    first_ref, second_ref, across_ref, down_ref, sum_ref, sems,
):
    tall, groups, _, lanes = first_ref.shape
    inside = pl.ds(HALO, tall)
    fetches = [
        pltpu.make_async_copy(across_hbm.at[inside], across_ref, sems.at[0]),
        pltpu.make_async_copy(down_hbm.at[inside], down_ref, sems.at[1]),
    ]
    for fetch in fetches:
        fetch.start()
    turn = rotation(inverse_ref[...])
    take = 4
    cells = take * groups * SUB

    def fill(c, carry):
        field = rotated(own_ref[pl.ds(pl.multiple_of(c * cells, 16), cells), :], turn)
        first_ref[pl.ds(c * take, take)] = field.reshape(take, groups, SUB, lanes)
        return carry

    lax.fori_loop(0, tall // take, fill, 0)
    sum_ref[...] = jnp.zeros_like(sum_ref)
    second_ref[0] = jnp.zeros(second_ref.shape[1:], f32)
    second_ref[tall - 1] = jnp.zeros(second_ref.shape[1:], f32)
    for fetch in fetches:
        fetch.wait()

    def sweep(s, src, dst, odd_pair):
        count = tall - 2 - 2 * s

        def step(c, carry):
            update(src, dst, across_ref, down_ref, sum_ref, s + 1 + c * BLOCK, BLOCK)
            return carry

        lax.fori_loop(0, count // BLOCK, step, 0)
        if odd_pair:
            update(src, dst, across_ref, down_ref, sum_ref, s + count - 1, 2)

    def two(t, carry):
        sweep(2 * t, first_ref, second_ref, (tall - 2) % BLOCK == 2)
        sweep(2 * t + 1, second_ref, first_ref, (tall - 4) % BLOCK == 2)
        return carry

    lax.fori_loop(0, SWEEPS // 2, two, 0)

    near = HALO + 1
    leaving = []
    for k, (source, target) in enumerate(((first_ref, first_hbm), (second_ref, second_hbm))):
        for side, row in enumerate((0, tall - near)):
            part = pl.ds(row, near)
            leaving.append(
                pltpu.make_async_copy(source.at[part], target.at[part], sems.at[2 + 2 * k + side])
            )
    for copy in leaving:
        copy.start()

    def gather(c, totals):
        rows = [(c * 4 + h, c * 4 + h) for h in range(4)]
        return tuple(summed_lanes(sum_ref, rows, list(totals)))

    zeros = tuple(jnp.zeros((SUB, lanes), f32) for _ in range(groups))
    totals = lax.fori_loop(0, tall // 4, gather, zeros)
    total_ref[...] = jnp.concatenate(totals, axis=0)
    for copy in leaving:
        copy.wait()


def inner_sweeps(own, inverse, across_down):
    tall, places, lanes = own.shape
    own = own.reshape(tall * places, lanes)
    vmem = pl.BlockSpec(memory_space=pltpu.VMEM)
    far = pl.BlockSpec(memory_space=pl.ANY)
    shape = (tall, places // SUB, SUB, lanes)
    return pl.pallas_call(
        inner_kernel,
        out_shape=(
            jax.ShapeDtypeStruct(shape, f32),
            jax.ShapeDtypeStruct(shape, f32),
            jax.ShapeDtypeStruct((places, lanes), f32),
        ),
        in_specs=[vmem, vmem, far, far],
        out_specs=(far, far, vmem),
        scratch_shapes=[pltpu.VMEM(shape, f32)] * 5 + [pltpu.SemaphoreType.DMA((6,))],
        compiler_params=pltpu.CompilerParams(vmem_limit_bytes=VMEM_BYTES),
        cost_estimate=pl.CostEstimate(
            flops=12 * 10**9, bytes_accessed=8 * own.size, transcendentals=0
        ),
        name="inner_sweeps",
    )(own, inverse, *across_down)


def outer_kernel(
    scale, ends_ref, inverse_ref, inner_ref, north_hbm, south_hbm, first_hbm, second_hbm,
    across_hbm, down_hbm, out_ref, first_ref, second_ref, across_ref, down_ref, sum_ref,
    north_ref, south_ref, sems,
):
    rows, groups, _, lanes = first_ref.shape
    tall = rows - 2 * HALO
    places = groups * SUB
    near = HALO + 1
    halos = [
        pltpu.make_async_copy(north_hbm, north_ref, sems.at[8]),
        pltpu.make_async_copy(south_hbm, south_ref, sems.at[9]),
    ]
    for halo in halos:
        halo.start()
    fetches = []
    for k, (source, target) in enumerate(((first_hbm, first_ref), (second_hbm, second_ref))):
        for side, row in enumerate((0, tall - near)):
            fetches.append(
                pltpu.make_async_copy(
                    source.at[pl.ds(row, near)],
                    target.at[pl.ds(HALO + row, near)],
                    sems.at[2 * k + side],
                )
            )
    wide_part = 2 * HALO + 1
    for k, (source, target) in enumerate(((across_hbm, across_ref), (down_hbm, down_ref))):
        for side, row in enumerate((0, rows - wide_part)):
            part = pl.ds(row, wide_part)
            fetches.append(
                pltpu.make_async_copy(source.at[part], target.at[part], sems.at[4 + 2 * k + side])
            )
    for fetch in fetches:
        fetch.start()
    sum_ref[...] = jnp.zeros_like(sum_ref)
    turn = rotation(inverse_ref[...])
    for halo in halos:
        halo.wait()
    take = 2
    cells = take * places

    def fill(c, carry):
        for source, offset in ((north_ref, 0), (south_ref, HALO + tall)):
            field = rotated(source[pl.ds(pl.multiple_of(c * cells, 16), cells), :], turn)
            first_ref[pl.ds(offset + c * take, take)] = field.reshape(take, groups, SUB, lanes)
        return carry

    lax.fori_loop(0, HALO // take, fill, 0)
    take = HALO // 2
    for fetch in fetches:
        fetch.wait()

    def sweep(s, src, dst):
        def step(c, carry):
            bottom = c // 2
            row = jnp.where(bottom == 0, s + 1, rows - 1 - HALO - s) + (c % 2) * take
            update(src, dst, across_ref, down_ref, sum_ref, row, take)
            return carry

        lax.fori_loop(0, 4, step, 0)

        @pl.when(ends_ref[0] == 1)
        def _():
            dst[HALO - 1] = jnp.zeros(dst.shape[1:], f32)

        @pl.when(ends_ref[1] == 1)
        def _():
            dst[HALO + tall] = jnp.zeros(dst.shape[1:], f32)

    def two(t, carry):
        sweep(2 * t, first_ref, second_ref)
        sweep(2 * t + 1, second_ref, first_ref)
        return carry

    lax.fori_loop(0, SWEEPS // 2, two, 0)

    def gather(c, totals):
        pairs = []
        for row in (2 * c, 2 * c + 1):
            pairs += [(HALO + row, row), (tall + row, tall - HALO + row)]
        return tuple(summed_lanes(sum_ref, pairs, list(totals)))

    totals = tuple(inner_ref[g * SUB : (g + 1) * SUB, :] for g in range(groups))
    totals = lax.fori_loop(0, HALO // 2, gather, totals)
    totals = jnp.concatenate(totals, axis=0).T[:tall]
    slot = iota((places, out_ref.shape[1]), 0)
    column = iota((places, out_ref.shape[1]), 1)
    back = (column == (slot % SUB) * groups + slot // SUB).astype(f32).astype(bf16)
    high, mid, low = split3(totals)
    out_ref[...] = (dot(high, back) + (dot(mid, back) + dot(low, back))) * scale


def outer_sweeps(scale, ends, north, south, inverse, inner, across_down, wide):
    first, second, total = inner
    tall, groups, _, lanes = first.shape
    shape = (tall + 2 * HALO, groups, SUB, lanes)
    north, south = (x.reshape(-1, lanes) for x in (north, south))
    vmem = pl.BlockSpec(memory_space=pltpu.VMEM)
    far = pl.BlockSpec(memory_space=pl.ANY)
    return pl.pallas_call(
        functools.partial(outer_kernel, scale),
        out_shape=jax.ShapeDtypeStruct((tall, wide), f32),
        in_specs=[pl.BlockSpec(memory_space=pltpu.SMEM)] + [vmem] * 2 + [far] * 6,
        out_specs=vmem,
        scratch_shapes=[pltpu.VMEM(shape, f32)] * 5
        + [pltpu.VMEM(north.shape, bf16)] * 2
        + [pltpu.SemaphoreType.DMA((10,))],
        compiler_params=pltpu.CompilerParams(vmem_limit_bytes=VMEM_BYTES),
        name="outer_sweeps",
    )(ends, inverse, total, north, south, first, second, *across_down)


def from_before(x, axis, closed):
    count = lax.axis_size(axis)
    return lax.ppermute(
        x, axis, [(i, (i + 1) % count) for i in range(count if closed else count - 1)]
    )


def from_after(x, axis, closed):
    count = lax.axis_size(axis)
    return lax.ppermute(
        x, axis, [((i + 1) % count, i) for i in range(count if closed else count - 1)]
    )


def ahead(values, axis, step):
    count = lax.axis_size(axis)
    return lax.ppermute(values, axis, [((i + step) % count, i) for i in range(count)])


def neighbours(x, extra, axis):
    size = x.shape[0]
    sent = jnp.concatenate([x, extra], axis=0)
    after, before, second = ahead(sent, axis, 1), ahead(sent, axis, -1), ahead(x, axis, 2)
    x = (x + before[:size]) + (after[:size] + second)
    return x, before[size:], after[size:]


def rest_of_ring(x, axis):
    step = 4
    while step < lax.axis_size(axis):
        x = x + ahead(x, axis, step)
        step *= 2
    return x


def per_device(basis, order, land, conduct):
    axes = ("lat", "lon")
    rows_here, width = basis.shape
    tall, wide = land.shape
    count = lax.axis_size("lat") * lax.axis_size("lon")
    cells = rows_here * count
    tied = lax.optimization_barrier
    at = lax.axis_index("lat")
    top, bottom = at == 0, at == lax.axis_size("lat") - 1

    whole_rows = rows_here // count == wide
    moving = deal(basis, order, lax.axis_size("lon"), wide) if whole_rows else basis[order]
    moving, basis, land, conduct = tied((moving, basis, land, conduct))
    raw = lax.all_to_all(moving, axes, split_axis=0, concat_axis=0, tiled=True)
    if not whole_rows:
        raw = raw.reshape(tall, wide, width)
        left = from_before(raw[:, -HALO:], "lon", True)
        right = from_after(raw[:, :HALO], "lon", True)
        raw = circle(raw, right, left, 1)

    partial = lax.dot_general(
        basis, basis, (((0,), (0,)), ((), ())), preferred_element_type=f32
    )
    coef = conduct * (0.35 + 0.65 * land.astype(f32))
    edges = jnp.concatenate([coef[:HALO], coef[-HALO:]], axis=0)
    edges = jnp.pad(edges, ((0, 4), (0, width - wide)))
    partial, before, after = neighbours(partial, edges, "lat")
    partial = rest_of_ring(partial, "lat")
    before = jnp.where(top, 0.0, before[HALO : 2 * HALO, :wide])
    after = jnp.where(bottom, 0.0, after[:HALO, :wide])
    coef = jnp.concatenate([before, coef, after], axis=0)
    edges = jnp.concatenate([coef[:, :HALO], coef[:, -HALO:]], axis=1)
    edges = jnp.pad(edges, ((0, 4), (0, width - 2 * HALO)))
    partial, before, after = neighbours(partial, edges, "lon")
    rows = coef.shape[0]
    coef = circle(coef, after[:rows, :HALO], before[:rows, HALO : 2 * HALO], 1)
    gram = rest_of_ring(partial, "lon")
    inverse = factor_inverse(gram)
    across_down = weights(coef, width)
    ends = jnp.stack([top, bottom]).astype(i32)
    raw, inverse, across_down, ends = tied((raw, inverse, across_down, ends))

    north = from_before(raw[-HALO:], "lat", False)
    south = from_after(raw[:HALO], "lat", False)
    inner = inner_sweeps(raw, inverse, across_down)
    scale = cells / (width * SWEEPS)
    return outer_sweeps(scale, ends, north, south, inverse, inner, across_down, wide)


def solution(mesh):
    in_specs = (P(("lat", "lon"), None), P(("lat", "lon")), P("lat", "lon"), P("lat", "lon"))
    out_specs = P("lat", "lon")
    return jax.shard_map(
        per_device, mesh=mesh, in_specs=in_specs, out_specs=out_specs, check_vma=False
    )
```

```python
import functools

import jax
import jax.numpy as jnp
from jax import lax
from jax.experimental import pallas as pl
from jax.experimental.pallas import tpu as pltpu
from jax.sharding import PartitionSpec as P

SWEEPS = 10
HALO = SWEEPS
LANES = 128
SUB = 8
ONE_HOT = 1024
TILES = 4
BLOCK = 4
VMEM_BYTES = 56 * 1024 * 1024

bf16, f32, i32 = jnp.bfloat16, jnp.float32, jnp.int32


def iota(shape, dim):
    return lax.broadcasted_iota(i32, shape, dim)


def dot(a, b):
    return jnp.dot(a, b, preferred_element_type=f32)


def split3(x):
    high = x.astype(bf16)
    rest = x - high.astype(f32)
    mid = rest.astype(bf16)
    low = (rest - mid.astype(f32)).astype(bf16)
    return high, mid, low


def slots(wide):
    return -(-(wide + 2 * HALO) // SUB) * SUB


def circle(own, right, left, axis):
    wide = own.shape[axis]
    count = slots(wide)
    gap = list(own.shape)
    gap[axis] = count - wide - 2 * HALO
    around = jnp.concatenate([own, right, jnp.zeros(gap, own.dtype), left], axis=axis)
    shape = around.shape
    around = around.reshape(shape[:axis] + (SUB, count // SUB) + shape[axis + 1 :])
    return jnp.swapaxes(around, axis, axis + 1).reshape(shape)


def deal_kernel(tiles_lon, basis_ref, order_ref, out_ref, slot_ref, ready_ref, sems):
    rows, width = basis_ref.shape
    parts = rows // ONE_HOT
    tiles, places, _ = out_ref.shape
    wide = order_ref.shape[1]
    groups = places // SUB
    stacked = jnp.concatenate(
        [basis_ref[q * ONE_HOT : (q + 1) * ONE_HOT, :] for q in range(parts)], axis=1
    )

    order = order_ref[...]
    at = iota(order.shape, 0) % tiles_lon
    after = jnp.where(
        at == tiles_lon - 1, pltpu.roll(order, tiles_lon - 1, 0), pltpu.roll(order, tiles - 1, 0)
    )
    before = jnp.where(
        at == 0, pltpu.roll(order, tiles - tiles_lon + 1, 0), pltpu.roll(order, 1, 0)
    )
    padded = slot_ref.shape[1]
    column = iota((wide, padded), 0)
    slot = iota((wide, padded), 1)
    place = jnp.where(slot < places, (slot % SUB) * groups + slot // SUB, -1)
    sources, hits = [], []
    for source, hit in (
        (order, (place < wide) & (column == place)),
        (after, (place < wide + HALO) & (column == place - wide)),
        (before, (place >= places - HALO) & (column == place - places + wide)),
    ):
        hits.append(hit.astype(f32).astype(bf16))
        halves = jnp.concatenate([source & 63, source >> 6], axis=0)
        sources.append(halves.astype(f32).astype(bf16))
    halves = dot(jnp.concatenate(sources, axis=1), jnp.concatenate(hits, axis=0))
    slot_ref[...] = (halves[tiles:] * 64.0 + halves[:tiles]).astype(i32)

    take = TILES
    steps = tiles // take

    def leave(c):
        return pltpu.make_async_copy(
            ready_ref.at[pl.ds(c * take, take)],
            out_ref.at[pl.ds(c * take, take)],
            sems.at[c],
        )

    lane = iota((take * places, LANES), 1)

    for c in range(steps):
        wanted = []
        for h in range(take):
            order = slot_ref[c * take + h : c * take + h + 1, :]
            wanted.append(jnp.broadcast_to(order, (LANES, padded)).T[:places])
        wanted = jnp.concatenate(wanted, axis=0)
        within = wanted & (ONE_HOT - 1)
        part = wanted - within
        marks = [
            (within == lane + b * LANES).astype(f32).astype(bf16)
            for b in range(ONE_HOT // LANES)
        ]
        found = dot(jnp.concatenate(marks, axis=1), stacked)
        picked = found[:, :width]
        for q in range(1, parts):
            picked = jnp.where(
                part == q * ONE_HOT, found[:, q * width : (q + 1) * width], picked
            )
        for h in range(take):
            ready_ref[c * take + h] = picked[h * places : (h + 1) * places].astype(bf16)
        leave(c).start()
    for c in range(steps):
        leave(c).wait()


def deal(basis, order, tiles_lon, wide):
    rows, width = basis.shape
    tiles = rows // wide
    places = slots(wide)
    vmem = pl.BlockSpec(memory_space=pltpu.VMEM)
    return pl.pallas_call(
        functools.partial(deal_kernel, tiles_lon),
        out_shape=jax.ShapeDtypeStruct((tiles, places, width), bf16),
        in_specs=[vmem, vmem],
        out_specs=pl.BlockSpec(memory_space=pl.ANY),
        scratch_shapes=[
            pltpu.VMEM((tiles, -(-places // LANES) * LANES), i32),
            pltpu.VMEM((tiles, places, width), bf16),
            pltpu.SemaphoreType.DMA((tiles // TILES,)),
        ],
        compiler_params=pltpu.CompilerParams(vmem_limit_bytes=VMEM_BYTES),
        cost_estimate=pl.CostEstimate(
            flops=2 * tiles * places * rows * width,
            bytes_accessed=4 * rows * width,
            transcendentals=0,
        ),
        name="deal",
    )(basis, order.reshape(tiles, wide))


def inverse_kernel(gram_ref, out_ref):
    size = gram_ref.shape[0]
    count = size // SUB
    shape = (SUB, size)
    tiles = [gram_ref[t * SUB : (t + 1) * SUB, :] for t in range(count)]
    lane = iota(shape, 1)
    sub = iota(shape, 0)
    for top in range(count):
        first = top * SUB
        inside = (lane >= first) & (lane < first + SUB)
        columns = [
            [jnp.broadcast_to(tiles[t][:, first + c : first + c + 1], shape) for t in range(top, count)]
            for c in range(SUB)
        ]
        core = {
            (r, c): jnp.broadcast_to(columns[c][0][r : r + 1, :], shape)
            for r in range(SUB)
            for c in range(r, SUB)
        }
        lines = [
            jnp.where(
                inside,
                jnp.where(lane == first + c, 1.0, 0.0),
                jnp.broadcast_to(tiles[top][c : c + 1, :], shape),
            )
            for c in range(SUB)
        ]
        scales = []
        for c in range(SUB):
            inverse = 1.0 / core[c, c]
            scales.append(inverse)
            for d in range(c + 1, SUB):
                factor = core[c, d] * inverse
                for e in range(d, SUB):
                    core[d, e] = core[d, e] - factor * core[c, e]
                lines[d] = lines[d] - factor * lines[c]
                for t in range(1, count - top):
                    columns[d][t] = columns[d][t] - factor * columns[c][t]
        for t in range(1, count - top):
            rest = jnp.where(inside, 0.0, tiles[top + t])
            for c in range(SUB):
                rest = rest - columns[c][t] * (scales[c] * lines[c])
            tiles[top + t] = rest
        merged = lines[0]
        pivot = core[0, 0]
        for c in range(1, SUB):
            merged = jnp.where(sub == c, lines[c], merged)
            pivot = jnp.where(sub == c, core[c, c], pivot)
        kept = jnp.where(lane <= sub + first, merged, 0.0)
        out_ref[first : first + SUB, :] = kept * (1.0 / jnp.sqrt(pivot))


def factor_inverse(gram):
    size = gram.shape[0]
    return pl.pallas_call(
        inverse_kernel,
        out_shape=jax.ShapeDtypeStruct(gram.shape, f32),
        compiler_params=pltpu.CompilerParams(vmem_limit_bytes=VMEM_BYTES),
        cost_estimate=pl.CostEstimate(
            flops=40 * size**4, bytes_accessed=8 * size * size, transcendentals=0
        ),
        name="factor_inverse",
    )(gram)


def weight_kernel(coef_ref, across_hbm, down_hbm, spread, across_ref, down_ref, sems):
    rows, groups, _, lanes = spread.shape
    places = groups * SUB
    turned = coef_ref[...].T
    depth = turned.shape[1]
    pieces = jnp.concatenate(split3(turned[:places]), axis=1)
    per_step = rows // 4
    offset = iota((3 * depth, per_step * lanes), 0) & (depth - 1)
    offset = offset - (iota((3 * depth, per_step * lanes), 1) // lanes)

    def put(c, carry):
        values = dot(pieces, (offset == c * per_step).astype(f32).astype(bf16))
        for h in range(per_step):
            spread[c * per_step + h] = values[:, h * lanes : (h + 1) * lanes].reshape(
                groups, SUB, lanes
            )
        return carry

    lax.fori_loop(0, 4, put, 0)

    def weigh(r, carry):
        for g in range(groups):
            here = spread[r, g]
            east = spread[r, g + 1] if g + 1 < groups else pltpu.roll(spread[r, 0], SUB - 1, 0)
            across_ref[r, g] = 0.124 * (here + east)
            down_ref[r, g] = 0.124 * (here + spread[r + 1, g])
        return carry

    across_ref[rows - 1] = jnp.zeros((groups, SUB, lanes), f32)
    down_ref[rows - 1] = jnp.zeros((groups, SUB, lanes), f32)
    leaving = []
    for c in range(4):
        lax.fori_loop(c * per_step, min((c + 1) * per_step, rows - 1), weigh, 0)
        part = pl.ds(c * per_step, per_step)
        for k, (source, target) in enumerate(((across_ref, across_hbm), (down_ref, down_hbm))):
            leaving.append(
                pltpu.make_async_copy(source.at[part], target.at[part], sems.at[2 * c + k])
            )
            leaving[-1].start()
    for copy in leaving:
        copy.wait()


def weights(coef, lanes):
    rows, places = coef.shape
    coef = jnp.pad(coef, ((0, -rows % 64), (0, -places % LANES)))
    shape = (rows, places // SUB, SUB, lanes)
    return pl.pallas_call(
        weight_kernel,
        out_shape=(jax.ShapeDtypeStruct(shape, f32),) * 2,
        out_specs=(pl.BlockSpec(memory_space=pl.ANY),) * 2,
        scratch_shapes=[pltpu.VMEM(shape, f32)] * 3 + [pltpu.SemaphoreType.DMA((8,))],
        compiler_params=pltpu.CompilerParams(vmem_limit_bytes=VMEM_BYTES),
        cost_estimate=pl.CostEstimate(
            flops=rows * places * lanes * 100, bytes_accessed=8 * rows * places * lanes, transcendentals=0
        ),
        name="weights",
    )(coef)


def rotation(inverse):
    high, mid, low = split3(inverse.T)
    return jnp.concatenate(
        [jnp.concatenate([high, low], axis=1), jnp.concatenate([mid, jnp.zeros_like(mid)], axis=1)],
        axis=0,
    )


def rotated(raw, turn):
    lanes = raw.shape[1]
    parts = dot(jnp.concatenate([raw, raw], axis=1), turn)
    return (parts[:, :lanes] + parts[:, lanes:]).astype(bf16).astype(f32)


def update(src, dst, across, down, sums, row, take, counted):
    groups = src.shape[1]
    last = groups - 1
    span = range(take)
    start = [src[row + r, 0] for r in span]
    closing = [
        across[row + r, last] * (pltpu.roll(start[r], SUB - 1, 0) - src[row + r, last])
        for r in span
    ]
    wrapped = [pltpu.roll(flux, 1, 0) for flux in closing]

    def vertical(g, here):
        above = down[row - 1, g] * (here[0] - src[row - 1, g])
        change = []
        for r in span:
            below = here[r + 1] if r + 1 < take else src[row + take, g]
            under = down[row + r, g] * (below - here[r])
            change.append(under - above)
            above = under
        return change

    def finish(r, g, old, new):
        dst[row + r, g] = new
        if counted:
            sums[row + r, g] += old * old + new * new

    here = [src[row + r, 1] for r in span]
    west = [across[row + r, 0] * (here[r] - start[r]) for r in span]
    change = vertical(0, start)
    pending = [start[r] + (change[r] + west[r]) for r in span]
    for g in range(1, groups):
        if g < last:
            following = [src[row + r, g + 1] for r in span]
            flux = [across[row + r, g] * (following[r] - here[r]) for r in span]
        else:
            following, flux = None, closing
        change = vertical(g, here)
        for r in span:
            finish(r, g, here[r], here[r] + (change[r] + (flux[r] - west[r])))
        here, west = following, flux
    for r in span:
        finish(r, 0, start[r], pending[r] - wrapped[r])


def summed_lanes(sums, rows, totals):
    lane = iota(totals[0].shape, 1)
    for row, to in rows:
        for g in range(len(totals)):
            total = jnp.sum(sums[row, g], axis=1, keepdims=True)
            totals[g] = totals[g] + jnp.where(lane == to, total, 0.0)
    return totals


def inner_kernel(
    own_ref, inverse_ref, across_hbm, down_hbm, first_hbm, second_hbm, total_ref,
    first_ref, second_ref, across_ref, down_ref, sum_ref, sems,
):
    tall, groups, _, lanes = first_ref.shape
    inside = pl.ds(HALO, tall)
    fetches = [
        pltpu.make_async_copy(across_hbm.at[inside], across_ref, sems.at[0]),
        pltpu.make_async_copy(down_hbm.at[inside], down_ref, sems.at[1]),
    ]
    for fetch in fetches:
        fetch.start()
    turn = rotation(inverse_ref[...])
    take = 4
    cells = take * groups * SUB

    for c in range(tall // take):
        field = rotated(own_ref[c * cells : (c + 1) * cells, :], turn)
        first_ref[c * take : (c + 1) * take] = field.reshape(take, groups, SUB, lanes)
    sum_ref[...] = jnp.zeros_like(sum_ref)
    second_ref[0] = jnp.zeros(second_ref.shape[1:], f32)
    second_ref[tall - 1] = jnp.zeros(second_ref.shape[1:], f32)
    for fetch in fetches:
        fetch.wait()

    def sweep(s, src, dst, odd_pair, counted):
        count = tall - 2 - 2 * s

        def step(c, carry):
            row = s + 1 + c * BLOCK
            update(src, dst, across_ref, down_ref, sum_ref, row, BLOCK, counted)
            return carry

        lax.fori_loop(0, count // BLOCK, step, 0)
        if odd_pair:
            update(src, dst, across_ref, down_ref, sum_ref, s + count - 1, 2, counted)

    def two(t, carry):
        sweep(2 * t, first_ref, second_ref, (tall - 2) % BLOCK == 2, False)
        sweep(2 * t + 1, second_ref, first_ref, (tall - 4) % BLOCK == 2, True)
        return carry

    lax.fori_loop(0, SWEEPS // 2, two, 0)

    near = HALO + 1
    leaving = []
    for k, (source, target) in enumerate(((first_ref, first_hbm), (second_ref, second_hbm))):
        for side, row in enumerate((0, tall - near)):
            part = pl.ds(row, near)
            leaving.append(
                pltpu.make_async_copy(source.at[part], target.at[part], sems.at[2 + 2 * k + side])
            )
    for copy in leaving:
        copy.start()

    def gather(c, totals):
        rows = [(c * 4 + h, c * 4 + h) for h in range(4)]
        return tuple(summed_lanes(sum_ref, rows, list(totals)))

    zeros = tuple(jnp.zeros((SUB, lanes), f32) for _ in range(groups))
    totals = lax.fori_loop(0, tall // 4, gather, zeros)
    total_ref[...] = jnp.concatenate(totals, axis=0)
    for copy in leaving:
        copy.wait()


def inner_sweeps(own, inverse, across_down):
    tall, places, lanes = own.shape
    own = own.reshape(tall * places, lanes)
    vmem = pl.BlockSpec(memory_space=pltpu.VMEM)
    far = pl.BlockSpec(memory_space=pl.ANY)
    shape = (tall, places // SUB, SUB, lanes)
    return pl.pallas_call(
        inner_kernel,
        out_shape=(
            jax.ShapeDtypeStruct(shape, f32),
            jax.ShapeDtypeStruct(shape, f32),
            jax.ShapeDtypeStruct((places, lanes), f32),
        ),
        in_specs=[vmem, vmem, far, far],
        out_specs=(far, far, vmem),
        scratch_shapes=[pltpu.VMEM(shape, f32)] * 5 + [pltpu.SemaphoreType.DMA((6,))],
        compiler_params=pltpu.CompilerParams(vmem_limit_bytes=VMEM_BYTES),
        cost_estimate=pl.CostEstimate(
            flops=12 * 10**9, bytes_accessed=8 * own.size, transcendentals=0
        ),
        name="inner_sweeps",
    )(own, inverse, *across_down)


def outer_kernel(
    scale, ends_ref, inverse_ref, inner_ref, north_hbm, south_hbm, first_hbm, second_hbm,
    across_hbm, down_hbm, out_ref, first_ref, second_ref, across_ref, down_ref, sum_ref,
    north_ref, south_ref, sems,
):
    rows, groups, _, lanes = first_ref.shape
    tall = rows - 2 * HALO
    places = groups * SUB
    near = HALO + 1
    halos = [
        pltpu.make_async_copy(north_hbm, north_ref, sems.at[0]),
        pltpu.make_async_copy(south_hbm, south_ref, sems.at[1]),
    ]
    for halo in halos:
        halo.start()
    soon, late = [], []

    def fetch(wave, source, target, start, take, shift):
        wave.append(
            pltpu.make_async_copy(
                source.at[pl.ds(start, take)],
                target.at[pl.ds(start + shift, take)],
                sems.at[2 + len(soon) + len(late)],
            )
        )

    reach = HALO + 2
    wide_part = 2 * HALO + 1
    for source, target in ((across_hbm, across_ref), (down_hbm, down_ref)):
        fetch(soon, source, target, 0, reach, 0)
        fetch(soon, source, target, rows - reach, reach, 0)
    fetch(soon, first_hbm, first_ref, 0, 2, HALO)
    fetch(soon, first_hbm, first_ref, tall - 2, 2, HALO)
    fetch(late, second_hbm, second_ref, 1, near - 1, HALO)
    fetch(late, second_hbm, second_ref, tall - near, near - 1, HALO)
    for source, target in ((across_hbm, across_ref), (down_hbm, down_ref)):
        fetch(late, source, target, reach, wide_part - reach, 0)
        fetch(late, source, target, rows - wide_part, wide_part - reach, 0)
    fetch(late, first_hbm, first_ref, 2, near - 2, HALO)
    fetch(late, first_hbm, first_ref, tall - near, near - 2, HALO)
    for copy in soon + late:
        copy.start()
    sum_ref[...] = jnp.zeros_like(sum_ref)
    turn = rotation(inverse_ref[...])
    for halo in halos:
        halo.wait()
    take = 2
    cells = take * places

    for c in range(HALO // take):
        for source, offset in ((north_ref, 0), (south_ref, HALO + tall)):
            field = rotated(source[c * cells : (c + 1) * cells, :], turn)
            first_ref[offset + c * take : offset + (c + 1) * take] = field.reshape(
                take, groups, SUB, lanes
            )
    take = HALO // 2
    for copy in soon:
        copy.wait()

    def sweep(s, src, dst, counted):
        def step(c, carry):
            bottom = c // 2
            row = jnp.where(bottom == 0, s + 1, rows - 1 - HALO - s) + (c % 2) * take
            update(src, dst, across_ref, down_ref, sum_ref, row, take, counted)
            return carry

        lax.fori_loop(0, 4, step, 0)

        @pl.when(ends_ref[0] == 1)
        def _():
            dst[HALO - 1] = jnp.zeros(dst.shape[1:], f32)

        @pl.when(ends_ref[1] == 1)
        def _():
            dst[HALO + tall] = jnp.zeros(dst.shape[1:], f32)

    sweep(0, first_ref, second_ref, False)
    for copy in late:
        copy.wait()
    sweep(1, second_ref, first_ref, True)

    def two(t, carry):
        sweep(2 * t, first_ref, second_ref, False)
        sweep(2 * t + 1, second_ref, first_ref, True)
        return carry

    lax.fori_loop(1, SWEEPS // 2, two, 0)

    def gather(c, totals):
        pairs = []
        for row in (2 * c, 2 * c + 1):
            pairs += [(HALO + row, row), (tall + row, tall - HALO + row)]
        return tuple(summed_lanes(sum_ref, pairs, list(totals)))

    totals = tuple(inner_ref[g * SUB : (g + 1) * SUB, :] for g in range(groups))
    totals = lax.fori_loop(0, HALO // 2, gather, totals)
    totals = jnp.concatenate(totals, axis=0).T[:tall]
    slot = iota((places, out_ref.shape[1]), 0)
    column = iota((places, out_ref.shape[1]), 1)
    back = (column == (slot % SUB) * groups + slot // SUB).astype(f32).astype(bf16)
    high, mid, low = split3(totals)
    out_ref[...] = (dot(high, back) + (dot(mid, back) + dot(low, back))) * scale


def outer_sweeps(scale, ends, north, south, inverse, inner, across_down, wide):
    first, second, total = inner
    tall, groups, _, lanes = first.shape
    shape = (tall + 2 * HALO, groups, SUB, lanes)
    north, south = (x.reshape(-1, lanes) for x in (north, south))
    vmem = pl.BlockSpec(memory_space=pltpu.VMEM)
    far = pl.BlockSpec(memory_space=pl.ANY)
    return pl.pallas_call(
        functools.partial(outer_kernel, scale),
        out_shape=jax.ShapeDtypeStruct((tall, wide), f32),
        in_specs=[pl.BlockSpec(memory_space=pltpu.SMEM)] + [vmem] * 2 + [far] * 6,
        out_specs=vmem,
        scratch_shapes=[pltpu.VMEM(shape, f32)] * 5
        + [pltpu.VMEM(north.shape, bf16)] * 2
        + [pltpu.SemaphoreType.DMA((16,))],
        compiler_params=pltpu.CompilerParams(vmem_limit_bytes=VMEM_BYTES),
        name="outer_sweeps",
    )(ends, inverse, total, north, south, first, second, *across_down)


def from_before(x, axis, closed):
    count = lax.axis_size(axis)
    return lax.ppermute(
        x, axis, [(i, (i + 1) % count) for i in range(count if closed else count - 1)]
    )


def from_after(x, axis, closed):
    count = lax.axis_size(axis)
    return lax.ppermute(
        x, axis, [((i + 1) % count, i) for i in range(count if closed else count - 1)]
    )


def ahead(values, axis, step):
    count = lax.axis_size(axis)
    return lax.ppermute(values, axis, [((i + step) % count, i) for i in range(count)])


def neighbours(x, extra, axis):
    size = x.shape[0]
    sent = jnp.concatenate([x, extra], axis=0)
    after, before, second = ahead(sent, axis, 1), ahead(sent, axis, -1), ahead(x, axis, 2)
    x = (x + before[:size]) + (after[:size] + second)
    return x, before[size:], after[size:]


def rest_of_ring(x, axis):
    step = 4
    while step < lax.axis_size(axis):
        x = x + ahead(x, axis, step)
        step *= 2
    return x


def per_device(basis, order, land, conduct):
    axes = ("lat", "lon")
    rows_here, width = basis.shape
    tall, wide = land.shape
    count = lax.axis_size("lat") * lax.axis_size("lon")
    cells = rows_here * count
    tied = lax.optimization_barrier
    at = lax.axis_index("lat")
    top, bottom = at == 0, at == lax.axis_size("lat") - 1

    whole_rows = rows_here // count == wide
    moving = deal(basis, order, lax.axis_size("lon"), wide) if whole_rows else basis[order]
    moving, basis, land, conduct = tied((moving, basis, land, conduct))
    raw = lax.all_to_all(moving, axes, split_axis=0, concat_axis=0, tiled=True)
    if not whole_rows:
        raw = raw.reshape(tall, wide, width)
        left = from_before(raw[:, -HALO:], "lon", True)
        right = from_after(raw[:, :HALO], "lon", True)
        raw = circle(raw, right, left, 1)

    partial = lax.dot_general(
        basis, basis, (((0,), (0,)), ((), ())), preferred_element_type=f32
    )
    coef = conduct * (0.35 + 0.65 * land.astype(f32))
    edges = jnp.concatenate([coef[:HALO], coef[-HALO:]], axis=0)
    edges = jnp.pad(edges, ((0, 4), (0, width - wide)))
    partial, before, after = neighbours(partial, edges, "lat")
    partial = rest_of_ring(partial, "lat")
    before = jnp.where(top, 0.0, before[HALO : 2 * HALO, :wide])
    after = jnp.where(bottom, 0.0, after[:HALO, :wide])
    coef = jnp.concatenate([before, coef, after], axis=0)
    edges = jnp.concatenate([coef[:, :HALO], coef[:, -HALO:]], axis=1)
    edges = jnp.pad(edges, ((0, 4), (0, width - 2 * HALO)))
    partial, before, after = neighbours(partial, edges, "lon")
    rows = coef.shape[0]
    coef = circle(coef, after[:rows, :HALO], before[:rows, HALO : 2 * HALO], 1)
    gram = rest_of_ring(partial, "lon")
    inverse = factor_inverse(gram)
    across_down = weights(coef, width)
    ends = jnp.stack([top, bottom]).astype(i32)
    raw, inverse, across_down, ends = tied((raw, inverse, across_down, ends))

    north = from_before(raw[-HALO:], "lat", False)
    south = from_after(raw[:HALO], "lat", False)
    inner = inner_sweeps(raw, inverse, across_down)
    scale = cells / (width * SWEEPS)
    return outer_sweeps(scale, ends, north, south, inverse, inner, across_down, wide)


def solution(mesh):
    in_specs = (P(("lat", "lon"), None), P(("lat", "lon")), P("lat", "lon"), P("lat", "lon"))
    out_specs = P("lat", "lon")
    return jax.shard_map(
        per_device, mesh=mesh, in_specs=in_specs, out_specs=out_specs, check_vma=False
    )
```

```python
import functools

import jax
import jax.numpy as jnp
from jax import lax
from jax.experimental import pallas as pl
from jax.experimental.pallas import tpu as pltpu
from jax.sharding import PartitionSpec as P

SWEEPS = 10
HALO = SWEEPS
LANES = 128
SUB = 8
ONE_HOT = 1024
TILES = 4
BLOCK = 8
VMEM_BYTES = 56 * 1024 * 1024

bf16, f32, i32 = jnp.bfloat16, jnp.float32, jnp.int32


def iota(shape, dim):
    return lax.broadcasted_iota(i32, shape, dim)


def dot(a, b):
    return jnp.dot(a, b, preferred_element_type=f32)


def split3(x):
    high = x.astype(bf16)
    rest = x - high.astype(f32)
    mid = rest.astype(bf16)
    low = (rest - mid.astype(f32)).astype(bf16)
    return high, mid, low


def slots(wide):
    return -(-(wide + 2 * HALO) // SUB) * SUB


def circle(own, right, left, axis):
    wide = own.shape[axis]
    count = slots(wide)
    gap = list(own.shape)
    gap[axis] = count - wide - 2 * HALO
    around = jnp.concatenate([own, right, jnp.zeros(gap, own.dtype), left], axis=axis)
    shape = around.shape
    around = around.reshape(shape[:axis] + (SUB, count // SUB) + shape[axis + 1 :])
    return jnp.swapaxes(around, axis, axis + 1).reshape(shape)


def deal_kernel(tiles_lon, basis_ref, order_ref, out_ref, slot_ref, ready_ref, sems):
    rows, width = basis_ref.shape
    parts = rows // ONE_HOT
    tiles, places, _ = out_ref.shape
    wide = order_ref.shape[1]
    groups = places // SUB
    stacked = jnp.concatenate(
        [basis_ref[q * ONE_HOT : (q + 1) * ONE_HOT, :] for q in range(parts)], axis=1
    )

    order = order_ref[...]
    at = iota(order.shape, 0) % tiles_lon
    after = jnp.where(
        at == tiles_lon - 1, pltpu.roll(order, tiles_lon - 1, 0), pltpu.roll(order, tiles - 1, 0)
    )
    before = jnp.where(
        at == 0, pltpu.roll(order, tiles - tiles_lon + 1, 0), pltpu.roll(order, 1, 0)
    )
    padded = slot_ref.shape[1]
    column = iota((wide, padded), 0)
    slot = iota((wide, padded), 1)
    place = jnp.where(slot < places, (slot % SUB) * groups + slot // SUB, -1)
    sources, hits = [], []
    for source, hit in (
        (order, (place < wide) & (column == place)),
        (after, (place < wide + HALO) & (column == place - wide)),
        (before, (place >= places - HALO) & (column == place - places + wide)),
    ):
        hits.append(hit.astype(f32).astype(bf16))
        halves = jnp.concatenate([source & 63, source >> 6], axis=0)
        sources.append(halves.astype(f32).astype(bf16))
    halves = dot(jnp.concatenate(sources, axis=1), jnp.concatenate(hits, axis=0))
    slot_ref[...] = (halves[tiles:] * 64.0 + halves[:tiles]).astype(i32)

    take = TILES
    steps = tiles // take

    def leave(c):
        return pltpu.make_async_copy(
            ready_ref.at[pl.ds(c * take, take)],
            out_ref.at[pl.ds(c * take, take)],
            sems.at[c],
        )

    lane = iota((take * places, LANES), 1)

    for c in range(steps):
        wanted = []
        for h in range(take):
            order = slot_ref[c * take + h : c * take + h + 1, :]
            wanted.append(jnp.broadcast_to(order, (LANES, padded)).T[:places])
        wanted = jnp.concatenate(wanted, axis=0)
        within = wanted & (ONE_HOT - 1)
        part = wanted - within
        marks = [
            (within == lane + b * LANES).astype(f32).astype(bf16)
            for b in range(ONE_HOT // LANES)
        ]
        found = dot(jnp.concatenate(marks, axis=1), stacked)
        picked = found[:, :width]
        for q in range(1, parts):
            picked = jnp.where(
                part == q * ONE_HOT, found[:, q * width : (q + 1) * width], picked
            )
        for h in range(take):
            ready_ref[c * take + h] = picked[h * places : (h + 1) * places].astype(bf16)
        leave(c).start()
    for c in range(steps):
        leave(c).wait()


def deal(basis, order, tiles_lon, wide):
    rows, width = basis.shape
    tiles = rows // wide
    places = slots(wide)
    vmem = pl.BlockSpec(memory_space=pltpu.VMEM)
    return pl.pallas_call(
        functools.partial(deal_kernel, tiles_lon),
        out_shape=jax.ShapeDtypeStruct((tiles, places, width), bf16),
        in_specs=[vmem, vmem],
        out_specs=pl.BlockSpec(memory_space=pl.ANY),
        scratch_shapes=[
            pltpu.VMEM((tiles, -(-places // LANES) * LANES), i32),
            pltpu.VMEM((tiles, places, width), bf16),
            pltpu.SemaphoreType.DMA((tiles // TILES,)),
        ],
        compiler_params=pltpu.CompilerParams(vmem_limit_bytes=VMEM_BYTES),
        cost_estimate=pl.CostEstimate(
            flops=2 * tiles * places * rows * width,
            bytes_accessed=4 * rows * width,
            transcendentals=0,
        ),
        name="deal",
    )(basis, order.reshape(tiles, wide))


def inverse_kernel(gram_ref, out_ref):
    size = gram_ref.shape[0]
    count = size // SUB
    shape = (SUB, size)
    tiles = [gram_ref[t * SUB : (t + 1) * SUB, :] for t in range(count)]
    lane = iota(shape, 1)
    sub = iota(shape, 0)
    for top in range(count):
        first = top * SUB
        inside = (lane >= first) & (lane < first + SUB)
        columns = [
            [jnp.broadcast_to(tiles[t][:, first + c : first + c + 1], shape) for t in range(top, count)]
            for c in range(SUB)
        ]
        core = {
            (r, c): jnp.broadcast_to(columns[c][0][r : r + 1, :], shape)
            for r in range(SUB)
            for c in range(r, SUB)
        }
        lines = [
            jnp.where(
                inside,
                jnp.where(lane == first + c, 1.0, 0.0),
                jnp.broadcast_to(tiles[top][c : c + 1, :], shape),
            )
            for c in range(SUB)
        ]
        scales = []
        for c in range(SUB):
            inverse = 1.0 / core[c, c]
            scales.append(inverse)
            for d in range(c + 1, SUB):
                factor = core[c, d] * inverse
                for e in range(d, SUB):
                    core[d, e] = core[d, e] - factor * core[c, e]
                lines[d] = lines[d] - factor * lines[c]
                for t in range(1, count - top):
                    columns[d][t] = columns[d][t] - factor * columns[c][t]
        for t in range(1, count - top):
            rest = jnp.where(inside, 0.0, tiles[top + t])
            for c in range(SUB):
                rest = rest - columns[c][t] * (scales[c] * lines[c])
            tiles[top + t] = rest
        merged = lines[0]
        pivot = core[0, 0]
        for c in range(1, SUB):
            merged = jnp.where(sub == c, lines[c], merged)
            pivot = jnp.where(sub == c, core[c, c], pivot)
        kept = jnp.where(lane <= sub + first, merged, 0.0)
        out_ref[first : first + SUB, :] = kept * (1.0 / jnp.sqrt(pivot))


def factor_inverse(gram):
    size = gram.shape[0]
    return pl.pallas_call(
        inverse_kernel,
        out_shape=jax.ShapeDtypeStruct(gram.shape, f32),
        compiler_params=pltpu.CompilerParams(vmem_limit_bytes=VMEM_BYTES),
        cost_estimate=pl.CostEstimate(
            flops=40 * size**4, bytes_accessed=8 * size * size, transcendentals=0
        ),
        name="factor_inverse",
    )(gram)


def weight_kernel(coef_ref, across_hbm, down_hbm, spread, across_ref, down_ref, sems):
    rows, groups, _, lanes = spread.shape
    places = groups * SUB
    turned = coef_ref[...].T
    depth = turned.shape[1]
    pieces = jnp.concatenate(split3(turned[:places]), axis=1)
    per_step = rows // 4
    offset = iota((3 * depth, per_step * lanes), 0) & (depth - 1)
    offset = offset - (iota((3 * depth, per_step * lanes), 1) // lanes)

    def put(c, carry):
        values = dot(pieces, (offset == c * per_step).astype(f32).astype(bf16))
        for h in range(per_step):
            spread[c * per_step + h] = values[:, h * lanes : (h + 1) * lanes].reshape(
                groups, SUB, lanes
            )
        return carry

    lax.fori_loop(0, 4, put, 0)

    def weigh(r, carry):
        for g in range(groups):
            here = spread[r, g]
            east = spread[r, g + 1] if g + 1 < groups else pltpu.roll(spread[r, 0], SUB - 1, 0)
            across_ref[r, g] = 0.124 * (here + east)
            down_ref[r, g] = 0.124 * (here + spread[r + 1, g])
        return carry

    across_ref[rows - 1] = jnp.zeros((groups, SUB, lanes), f32)
    down_ref[rows - 1] = jnp.zeros((groups, SUB, lanes), f32)
    leaving = []
    for c in range(4):
        lax.fori_loop(c * per_step, min((c + 1) * per_step, rows - 1), weigh, 0)
        part = pl.ds(c * per_step, per_step)
        for k, (source, target) in enumerate(((across_ref, across_hbm), (down_ref, down_hbm))):
            leaving.append(
                pltpu.make_async_copy(source.at[part], target.at[part], sems.at[2 * c + k])
            )
            leaving[-1].start()
    for copy in leaving:
        copy.wait()


def weights(coef, lanes):
    rows, places = coef.shape
    coef = jnp.pad(coef, ((0, -rows % 64), (0, -places % LANES)))
    shape = (rows, places // SUB, SUB, lanes)
    return pl.pallas_call(
        weight_kernel,
        out_shape=(jax.ShapeDtypeStruct(shape, f32),) * 2,
        out_specs=(pl.BlockSpec(memory_space=pl.ANY),) * 2,
        scratch_shapes=[pltpu.VMEM(shape, f32)] * 3 + [pltpu.SemaphoreType.DMA((8,))],
        compiler_params=pltpu.CompilerParams(vmem_limit_bytes=VMEM_BYTES),
        cost_estimate=pl.CostEstimate(
            flops=rows * places * lanes * 100, bytes_accessed=8 * rows * places * lanes, transcendentals=0
        ),
        name="weights",
    )(coef)


def rotation(inverse):
    high, mid, low = split3(inverse.T)
    return jnp.concatenate(
        [jnp.concatenate([high, low], axis=1), jnp.concatenate([mid, jnp.zeros_like(mid)], axis=1)],
        axis=0,
    )


def rotated(raw, turn):
    lanes = raw.shape[1]
    parts = dot(jnp.concatenate([raw, raw], axis=1), turn)
    return (parts[:, :lanes] + parts[:, lanes:]).astype(bf16).astype(f32)


def update(src, dst, across, down, sums, row, take, counted, kept=True):
    groups = src.shape[1]
    last = groups - 1
    span = range(take)
    start = [src[row + r, 0] for r in span]
    closing = [
        across[row + r, last] * (pltpu.roll(start[r], SUB - 1, 0) - src[row + r, last])
        for r in span
    ]
    wrapped = [pltpu.roll(flux, 1, 0) for flux in closing]

    def vertical(g, here):
        above = down[row - 1, g] * (here[0] - src[row - 1, g])
        change = []
        for r in span:
            below = here[r + 1] if r + 1 < take else src[row + take, g]
            under = down[row + r, g] * (below - here[r])
            change.append(under - above)
            above = under
        return change

    def finish(r, g, old, new):
        if kept:
            dst[row + r, g] = new
        if counted:
            sums[row + r, g] += old * old + new * new

    here = [src[row + r, 1] for r in span]
    west = [across[row + r, 0] * (here[r] - start[r]) for r in span]
    change = vertical(0, start)
    pending = [start[r] + (change[r] + west[r]) for r in span]
    for g in range(1, groups):
        if g < last:
            following = [src[row + r, g + 1] for r in span]
            flux = [across[row + r, g] * (following[r] - here[r]) for r in span]
        else:
            following, flux = None, closing
        change = vertical(g, here)
        for r in span:
            finish(r, g, here[r], here[r] + (change[r] + (flux[r] - west[r])))
        here, west = following, flux
    for r in span:
        finish(r, 0, start[r], pending[r] - wrapped[r])


def summed_lanes(sums, rows, totals):
    lane = iota(totals[0].shape, 1)
    for row, to in rows:
        for g in range(len(totals)):
            total = jnp.sum(sums[row, g], axis=1, keepdims=True)
            totals[g] = totals[g] + jnp.where(lane == to, total, 0.0)
    return totals


def inner_kernel(
    own_ref, inverse_ref, across_hbm, down_hbm, first_hbm, second_hbm, total_ref,
    first_ref, second_ref, across_ref, down_ref, sum_ref, sems,
):
    tall, groups, _, lanes = first_ref.shape
    inside = pl.ds(HALO, tall)
    fetches = [
        pltpu.make_async_copy(across_hbm.at[inside], across_ref, sems.at[0]),
        pltpu.make_async_copy(down_hbm.at[inside], down_ref, sems.at[1]),
    ]
    for fetch in fetches:
        fetch.start()
    turn = rotation(inverse_ref[...])
    take = 4
    cells = take * groups * SUB

    for c in range(tall // take):
        field = rotated(own_ref[c * cells : (c + 1) * cells, :], turn)
        first_ref[c * take : (c + 1) * take] = field.reshape(take, groups, SUB, lanes)
    sum_ref[...] = jnp.zeros_like(sum_ref)
    second_ref[0] = jnp.zeros(second_ref.shape[1:], f32)
    second_ref[tall - 1] = jnp.zeros(second_ref.shape[1:], f32)
    for fetch in fetches:
        fetch.wait()

    for s in range(SWEEPS):
        src, dst = (first_ref, second_ref) if s % 2 == 0 else (second_ref, first_ref)
        count = tall - 2 - 2 * s
        size = -(-count // -(-count // BLOCK))
        run = functools.partial(update, src, dst, across_ref, down_ref, sum_ref)
        flags = (s % 2 == 1, s < SWEEPS - 1)

        def step(c, carry):
            run(s + 1 + c * size, size, *flags)
            return carry

        lax.fori_loop(0, count // size, step, 0)
        if count % size:
            run(s + 1 + count - count % size, count % size, *flags)

    near = HALO + 1
    leaving = []
    for k, (source, target) in enumerate(((first_ref, first_hbm), (second_ref, second_hbm))):
        for side, row in enumerate((0, tall - near)):
            part = pl.ds(row, near)
            leaving.append(
                pltpu.make_async_copy(source.at[part], target.at[part], sems.at[2 + 2 * k + side])
            )
    for copy in leaving:
        copy.start()

    def gather(c, totals):
        rows = [(c * 4 + h, c * 4 + h) for h in range(4)]
        return tuple(summed_lanes(sum_ref, rows, list(totals)))

    zeros = tuple(jnp.zeros((SUB, lanes), f32) for _ in range(groups))
    totals = lax.fori_loop(0, tall // 4, gather, zeros)
    total_ref[...] = jnp.concatenate(totals, axis=0)
    for copy in leaving:
        copy.wait()


def inner_sweeps(own, inverse, across_down):
    tall, places, lanes = own.shape
    own = own.reshape(tall * places, lanes)
    vmem = pl.BlockSpec(memory_space=pltpu.VMEM)
    far = pl.BlockSpec(memory_space=pl.ANY)
    shape = (tall, places // SUB, SUB, lanes)
    return pl.pallas_call(
        inner_kernel,
        out_shape=(
            jax.ShapeDtypeStruct(shape, f32),
            jax.ShapeDtypeStruct(shape, f32),
            jax.ShapeDtypeStruct((places, lanes), f32),
        ),
        in_specs=[vmem, vmem, far, far],
        out_specs=(far, far, vmem),
        scratch_shapes=[pltpu.VMEM(shape, f32)] * 5 + [pltpu.SemaphoreType.DMA((6,))],
        compiler_params=pltpu.CompilerParams(vmem_limit_bytes=VMEM_BYTES),
        cost_estimate=pl.CostEstimate(
            flops=12 * 10**9, bytes_accessed=8 * own.size, transcendentals=0
        ),
        name="inner_sweeps",
    )(own, inverse, *across_down)


def outer_kernel(
    scale, ends_ref, inverse_ref, inner_ref, north_hbm, south_hbm, first_hbm, second_hbm,
    across_hbm, down_hbm, out_ref, first_ref, second_ref, across_ref, down_ref, sum_ref,
    north_ref, south_ref, sems,
):
    rows, groups, _, lanes = first_ref.shape
    tall = rows - 2 * HALO
    places = groups * SUB
    near = HALO + 1
    halos = [
        pltpu.make_async_copy(north_hbm, north_ref, sems.at[0]),
        pltpu.make_async_copy(south_hbm, south_ref, sems.at[1]),
    ]
    for halo in halos:
        halo.start()
    soon, late = [], []

    def fetch(wave, source, target, start, take, shift):
        wave.append(
            pltpu.make_async_copy(
                source.at[pl.ds(start, take)],
                target.at[pl.ds(start + shift, take)],
                sems.at[2 + len(soon) + len(late)],
            )
        )

    reach = HALO + 2
    wide_part = 2 * HALO + 1
    for source, target in ((across_hbm, across_ref), (down_hbm, down_ref)):
        fetch(soon, source, target, 0, reach, 0)
        fetch(soon, source, target, rows - reach, reach, 0)
    fetch(soon, first_hbm, first_ref, 0, 2, HALO)
    fetch(soon, first_hbm, first_ref, tall - 2, 2, HALO)
    fetch(late, second_hbm, second_ref, 1, near - 1, HALO)
    fetch(late, second_hbm, second_ref, tall - near, near - 1, HALO)
    for source, target in ((across_hbm, across_ref), (down_hbm, down_ref)):
        fetch(late, source, target, reach, wide_part - reach, 0)
        fetch(late, source, target, rows - wide_part, wide_part - reach, 0)
    fetch(late, first_hbm, first_ref, 2, near - 2, HALO)
    fetch(late, first_hbm, first_ref, tall - near, near - 2, HALO)
    for copy in soon + late:
        copy.start()
    sum_ref[...] = jnp.zeros_like(sum_ref)
    turn = rotation(inverse_ref[...])
    for halo in halos:
        halo.wait()
    take = 2
    cells = take * places

    for c in range(HALO // take):
        for source, offset in ((north_ref, 0), (south_ref, HALO + tall)):
            field = rotated(source[c * cells : (c + 1) * cells, :], turn)
            first_ref[offset + c * take : offset + (c + 1) * take] = field.reshape(
                take, groups, SUB, lanes
            )
    take = HALO // 2
    for copy in soon:
        copy.wait()

    for s in range(SWEEPS):
        src, dst = (first_ref, second_ref) if s % 2 == 0 else (second_ref, first_ref)
        run = functools.partial(update, src, dst, across_ref, down_ref, sum_ref)
        if s == 1:
            for copy in late:
                copy.wait()

        def both(side, carry):
            halo = HALO - 1 - s
            if s % 2 == 0:
                start = jnp.where(side == 0, s + 1, rows - 1 - HALO - s)
                run(start, take, False)
                run(start + take, take, False)
                return carry
            if halo > 0:
                run(jnp.where(side == 0, s + 1, HALO + tall), halo, False)
            start = jnp.where(side == 0, HALO, rows - 1 - HALO - s)
            done = 0
            while done < s + 1:
                size = min(s + 1 - done, 2 * take if s + 1 < 2 * take else take)
                run(start + done, size, True, s < SWEEPS - 1)
                done += size
            return carry

        lax.fori_loop(0, 2, both, 0)
        if s < SWEEPS - 1:

            @pl.when(ends_ref[0] == 1)
            def _():
                dst[HALO - 1] = jnp.zeros(dst.shape[1:], f32)

            @pl.when(ends_ref[1] == 1)
            def _():
                dst[HALO + tall] = jnp.zeros(dst.shape[1:], f32)

    def gather(c, totals):
        pairs = []
        for row in (2 * c, 2 * c + 1):
            pairs += [(HALO + row, row), (tall + row, tall - HALO + row)]
        return tuple(summed_lanes(sum_ref, pairs, list(totals)))

    totals = tuple(inner_ref[g * SUB : (g + 1) * SUB, :] for g in range(groups))
    totals = lax.fori_loop(0, HALO // 2, gather, totals)
    totals = jnp.concatenate(totals, axis=0).T[:tall]
    slot = iota((places, out_ref.shape[1]), 0)
    column = iota((places, out_ref.shape[1]), 1)
    back = (column == (slot % SUB) * groups + slot // SUB).astype(f32).astype(bf16)
    high, mid, low = split3(totals)
    out_ref[...] = (dot(high, back) + (dot(mid, back) + dot(low, back))) * scale


def outer_sweeps(scale, ends, north, south, inverse, inner, across_down, wide):
    first, second, total = inner
    tall, groups, _, lanes = first.shape
    shape = (tall + 2 * HALO, groups, SUB, lanes)
    north, south = (x.reshape(-1, lanes) for x in (north, south))
    vmem = pl.BlockSpec(memory_space=pltpu.VMEM)
    far = pl.BlockSpec(memory_space=pl.ANY)
    return pl.pallas_call(
        functools.partial(outer_kernel, scale),
        out_shape=jax.ShapeDtypeStruct((tall, wide), f32),
        in_specs=[pl.BlockSpec(memory_space=pltpu.SMEM)] + [vmem] * 2 + [far] * 6,
        out_specs=vmem,
        scratch_shapes=[pltpu.VMEM(shape, f32)] * 5
        + [pltpu.VMEM(north.shape, bf16)] * 2
        + [pltpu.SemaphoreType.DMA((16,))],
        compiler_params=pltpu.CompilerParams(vmem_limit_bytes=VMEM_BYTES),
        name="outer_sweeps",
    )(ends, inverse, total, north, south, first, second, *across_down)


def from_before(x, axis, closed):
    count = lax.axis_size(axis)
    return lax.ppermute(
        x, axis, [(i, (i + 1) % count) for i in range(count if closed else count - 1)]
    )


def from_after(x, axis, closed):
    count = lax.axis_size(axis)
    return lax.ppermute(
        x, axis, [((i + 1) % count, i) for i in range(count if closed else count - 1)]
    )


def ahead(values, axis, step):
    count = lax.axis_size(axis)
    return lax.ppermute(values, axis, [((i + step) % count, i) for i in range(count)])


def neighbours(x, extra, axis):
    size = x.shape[0]
    sent = jnp.concatenate([x, extra], axis=0)
    after, before, second = ahead(sent, axis, 1), ahead(sent, axis, -1), ahead(x, axis, 2)
    x = (x + before[:size]) + (after[:size] + second)
    return x, before[size:], after[size:]


def rest_of_ring(x, axis):
    step = 4
    while step < lax.axis_size(axis):
        x = x + ahead(x, axis, step)
        step *= 2
    return x


def per_device(basis, order, land, conduct):
    axes = ("lat", "lon")
    rows_here, width = basis.shape
    tall, wide = land.shape
    count = lax.axis_size("lat") * lax.axis_size("lon")
    cells = rows_here * count
    tied = lax.optimization_barrier
    at = lax.axis_index("lat")
    top, bottom = at == 0, at == lax.axis_size("lat") - 1

    whole_rows = rows_here // count == wide
    moving = deal(basis, order, lax.axis_size("lon"), wide) if whole_rows else basis[order]
    moving, basis, land, conduct = tied((moving, basis, land, conduct))
    raw = lax.all_to_all(moving, axes, split_axis=0, concat_axis=0, tiled=True)
    if not whole_rows:
        raw = raw.reshape(tall, wide, width)
        left = from_before(raw[:, -HALO:], "lon", True)
        right = from_after(raw[:, :HALO], "lon", True)
        raw = circle(raw, right, left, 1)

    partial = lax.dot_general(
        basis, basis, (((0,), (0,)), ((), ())), preferred_element_type=f32
    )
    coef = conduct * (0.35 + 0.65 * land.astype(f32))
    edges = jnp.concatenate([coef[:HALO], coef[-HALO:]], axis=0)
    edges = jnp.pad(edges, ((0, 4), (0, width - wide)))
    partial, before, after = neighbours(partial, edges, "lat")
    partial = rest_of_ring(partial, "lat")
    before = jnp.where(top, 0.0, before[HALO : 2 * HALO, :wide])
    after = jnp.where(bottom, 0.0, after[:HALO, :wide])
    coef = jnp.concatenate([before, coef, after], axis=0)
    edges = jnp.concatenate([coef[:, :HALO], coef[:, -HALO:]], axis=1)
    edges = jnp.pad(edges, ((0, 4), (0, width - 2 * HALO)))
    partial, before, after = neighbours(partial, edges, "lon")
    rows = coef.shape[0]
    coef = circle(coef, after[:rows, :HALO], before[:rows, HALO : 2 * HALO], 1)
    gram = rest_of_ring(partial, "lon")
    inverse = factor_inverse(gram)
    across_down = weights(coef, width)
    ends = jnp.stack([top, bottom]).astype(i32)
    raw, inverse, across_down, ends = tied((raw, inverse, across_down, ends))

    north = from_before(raw[-HALO:], "lat", False)
    south = from_after(raw[:HALO], "lat", False)
    inner = inner_sweeps(raw, inverse, across_down)
    scale = cells / (width * SWEEPS)
    return outer_sweeps(scale, ends, north, south, inverse, inner, across_down, wide)


def solution(mesh):
    in_specs = (P(("lat", "lon"), None), P(("lat", "lon")), P("lat", "lon"), P("lat", "lon"))
    out_specs = P("lat", "lon")
    return jax.shard_map(
        per_device, mesh=mesh, in_specs=in_specs, out_specs=out_specs, check_vma=False
    )
```

```python
import functools

import jax
import jax.numpy as jnp
from jax import lax
from jax.experimental import pallas as pl
from jax.experimental.pallas import tpu as pltpu
from jax.sharding import PartitionSpec as P

SWEEPS = 10
HALO = SWEEPS
LANES = 128
SUB = 8
ONE_HOT = 1024
TILES = 4
BLOCK = 8
VMEM_BYTES = 56 * 1024 * 1024
OUTER_BYTES = 52 * 1024 * 1024

bf16, f32, i32 = jnp.bfloat16, jnp.float32, jnp.int32


def iota(shape, dim):
    return lax.broadcasted_iota(i32, shape, dim)


def dot(a, b):
    return jnp.dot(a, b, preferred_element_type=f32)


def split3(x):
    high = x.astype(bf16)
    rest = x - high.astype(f32)
    mid = rest.astype(bf16)
    low = (rest - mid.astype(f32)).astype(bf16)
    return high, mid, low


def slots(wide):
    return -(-(wide + 2 * HALO) // SUB) * SUB


def circle(own, right, left, axis):
    wide = own.shape[axis]
    count = slots(wide)
    gap = list(own.shape)
    gap[axis] = count - wide - 2 * HALO
    around = jnp.concatenate([own, right, jnp.zeros(gap, own.dtype), left], axis=axis)
    shape = around.shape
    around = around.reshape(shape[:axis] + (SUB, count // SUB) + shape[axis + 1 :])
    return jnp.swapaxes(around, axis, axis + 1).reshape(shape)


def deal_kernel(tiles_lon, basis_ref, order_ref, out_ref, slot_ref, ready_ref, sems):
    rows, width = basis_ref.shape
    parts = rows // ONE_HOT
    tiles, places, _ = out_ref.shape
    wide = order_ref.shape[1]
    groups = places // SUB
    stacked = jnp.concatenate(
        [basis_ref[q * ONE_HOT : (q + 1) * ONE_HOT, :] for q in range(parts)], axis=1
    )

    order = order_ref[...]
    at = iota(order.shape, 0) % tiles_lon
    after = jnp.where(
        at == tiles_lon - 1, pltpu.roll(order, tiles_lon - 1, 0), pltpu.roll(order, tiles - 1, 0)
    )
    before = jnp.where(
        at == 0, pltpu.roll(order, tiles - tiles_lon + 1, 0), pltpu.roll(order, 1, 0)
    )
    padded = slot_ref.shape[1]
    column = iota((wide, padded), 0)
    slot = iota((wide, padded), 1)
    place = jnp.where(slot < places, (slot % SUB) * groups + slot // SUB, -1)
    sources, hits = [], []
    for source, hit in (
        (order, (place < wide) & (column == place)),
        (after, (place < wide + HALO) & (column == place - wide)),
        (before, (place >= places - HALO) & (column == place - places + wide)),
    ):
        hits.append(hit.astype(f32).astype(bf16))
        halves = jnp.concatenate([source & 63, source >> 6], axis=0)
        sources.append(halves.astype(f32).astype(bf16))
    halves = dot(jnp.concatenate(sources, axis=1), jnp.concatenate(hits, axis=0))
    slot_ref[...] = (halves[tiles:] * 64.0 + halves[:tiles]).astype(i32)

    take = TILES
    steps = tiles // take

    def leave(c):
        return pltpu.make_async_copy(
            ready_ref.at[pl.ds(c * take, take)],
            out_ref.at[pl.ds(c * take, take)],
            sems.at[c],
        )

    lane = iota((take * places, LANES), 1)

    for c in range(steps):
        wanted = []
        for h in range(take):
            order = slot_ref[c * take + h : c * take + h + 1, :]
            wanted.append(jnp.broadcast_to(order, (LANES, padded)).T[:places])
        wanted = jnp.concatenate(wanted, axis=0)
        within = wanted & (ONE_HOT - 1)
        part = wanted - within
        marks = [
            (within == lane + b * LANES).astype(f32).astype(bf16)
            for b in range(ONE_HOT // LANES)
        ]
        found = dot(jnp.concatenate(marks, axis=1), stacked)
        picked = found[:, :width]
        for q in range(1, parts):
            picked = jnp.where(
                part == q * ONE_HOT, found[:, q * width : (q + 1) * width], picked
            )
        for h in range(take):
            ready_ref[c * take + h] = picked[h * places : (h + 1) * places].astype(bf16)
        leave(c).start()
    for c in range(steps):
        leave(c).wait()


def deal(basis, order, tiles_lon, wide):
    rows, width = basis.shape
    tiles = rows // wide
    places = slots(wide)
    vmem = pl.BlockSpec(memory_space=pltpu.VMEM)
    return pl.pallas_call(
        functools.partial(deal_kernel, tiles_lon),
        out_shape=jax.ShapeDtypeStruct((tiles, places, width), bf16),
        in_specs=[vmem, vmem],
        out_specs=pl.BlockSpec(memory_space=pl.ANY),
        scratch_shapes=[
            pltpu.VMEM((tiles, -(-places // LANES) * LANES), i32),
            pltpu.VMEM((tiles, places, width), bf16),
            pltpu.SemaphoreType.DMA((tiles // TILES,)),
        ],
        compiler_params=pltpu.CompilerParams(vmem_limit_bytes=VMEM_BYTES),
        cost_estimate=pl.CostEstimate(
            flops=2 * tiles * places * rows * width,
            bytes_accessed=4 * rows * width,
            transcendentals=0,
        ),
        name="deal",
    )(basis, order.reshape(tiles, wide))


def inverse_kernel(gram_ref, turn_ref, out_ref):
    size = gram_ref.shape[0]
    count = size // SUB
    shape = (SUB, size)
    tiles = [gram_ref[t * SUB : (t + 1) * SUB, :] for t in range(count)]
    lane = iota(shape, 1)
    sub = iota(shape, 0)
    for top in range(count):
        first = top * SUB
        inside = (lane >= first) & (lane < first + SUB)
        columns = [
            [jnp.broadcast_to(tiles[t][:, first + c : first + c + 1], shape) for t in range(top, count)]
            for c in range(SUB)
        ]
        core = {
            (r, c): jnp.broadcast_to(columns[c][0][r : r + 1, :], shape)
            for r in range(SUB)
            for c in range(r, SUB)
        }
        lines = [
            jnp.where(
                inside,
                jnp.where(lane == first + c, 1.0, 0.0),
                jnp.broadcast_to(tiles[top][c : c + 1, :], shape),
            )
            for c in range(SUB)
        ]
        scales = []
        for c in range(SUB):
            inverse = 1.0 / core[c, c]
            scales.append(inverse)
            for d in range(c + 1, SUB):
                factor = core[c, d] * inverse
                for e in range(d, SUB):
                    core[d, e] = core[d, e] - factor * core[c, e]
                lines[d] = lines[d] - factor * lines[c]
                for t in range(1, count - top):
                    columns[d][t] = columns[d][t] - factor * columns[c][t]
        for t in range(1, count - top):
            rest = jnp.where(inside, 0.0, tiles[top + t])
            for c in range(SUB):
                rest = rest - columns[c][t] * (scales[c] * lines[c])
            tiles[top + t] = rest
        merged = lines[0]
        pivot = core[0, 0]
        for c in range(1, SUB):
            merged = jnp.where(sub == c, lines[c], merged)
            pivot = jnp.where(sub == c, core[c, c], pivot)
        kept = jnp.where(lane <= sub + first, merged, 0.0)
        out_ref[first : first + SUB, :] = kept * (1.0 / jnp.sqrt(pivot))
    turn_ref[...] = rotation(out_ref[...])


def factor_inverse(gram):
    size = gram.shape[0]
    return pl.pallas_call(
        inverse_kernel,
        out_shape=jax.ShapeDtypeStruct((2 * size, 2 * size), bf16),
        scratch_shapes=[pltpu.VMEM(gram.shape, f32)],
        compiler_params=pltpu.CompilerParams(vmem_limit_bytes=VMEM_BYTES),
        cost_estimate=pl.CostEstimate(
            flops=40 * size**4, bytes_accessed=8 * size * size, transcendentals=0
        ),
        name="factor_inverse",
    )(gram)


def weight_kernel(coef_ref, across_hbm, down_hbm, spread, across_ref, down_ref, sems):
    rows, groups, _, lanes = spread.shape
    places = groups * SUB
    turned = coef_ref[...].T
    depth = turned.shape[1]
    pieces = jnp.concatenate(split3(turned[:places]), axis=1)
    per_step = rows // 4
    offset = iota((3 * depth, per_step * lanes), 0) & (depth - 1)
    offset = offset - (iota((3 * depth, per_step * lanes), 1) // lanes)

    def put(c, carry):
        values = dot(pieces, (offset == c * per_step).astype(f32).astype(bf16))
        for h in range(per_step):
            spread[c * per_step + h] = values[:, h * lanes : (h + 1) * lanes].reshape(
                groups, SUB, lanes
            )
        return carry

    lax.fori_loop(0, 4, put, 0)

    def weigh(r, carry):
        for g in range(groups):
            here = spread[r, g]
            east = spread[r, g + 1] if g + 1 < groups else pltpu.roll(spread[r, 0], SUB - 1, 0)
            across_ref[r, g] = 0.124 * (here + east)
            down_ref[r, g] = 0.124 * (here + spread[r + 1, g])
        return carry

    across_ref[rows - 1] = jnp.zeros((groups, SUB, lanes), f32)
    down_ref[rows - 1] = jnp.zeros((groups, SUB, lanes), f32)
    leaving = []
    for c in range(4):
        lax.fori_loop(c * per_step, min((c + 1) * per_step, rows - 1), weigh, 0)
        part = pl.ds(c * per_step, per_step)
        for k, (source, target) in enumerate(((across_ref, across_hbm), (down_ref, down_hbm))):
            leaving.append(
                pltpu.make_async_copy(source.at[part], target.at[part], sems.at[2 * c + k])
            )
            leaving[-1].start()
    for copy in leaving:
        copy.wait()


def weights(coef, lanes):
    rows, places = coef.shape
    coef = jnp.pad(coef, ((0, -rows % 64), (0, -places % LANES)))
    shape = (rows, places // SUB, SUB, lanes)
    return pl.pallas_call(
        weight_kernel,
        out_shape=(jax.ShapeDtypeStruct(shape, f32),) * 2,
        out_specs=(pl.BlockSpec(memory_space=pl.ANY),) * 2,
        scratch_shapes=[pltpu.VMEM(shape, f32)] * 3 + [pltpu.SemaphoreType.DMA((8,))],
        compiler_params=pltpu.CompilerParams(vmem_limit_bytes=VMEM_BYTES),
        cost_estimate=pl.CostEstimate(
            flops=rows * places * lanes * 100, bytes_accessed=8 * rows * places * lanes, transcendentals=0
        ),
        name="weights",
    )(coef)


def rotation(inverse):
    high, mid, low = split3(inverse.T)
    return jnp.concatenate(
        [jnp.concatenate([high, low], axis=1), jnp.concatenate([mid, jnp.zeros_like(mid)], axis=1)],
        axis=0,
    )


def rotated(raw, turn):
    lanes = raw.shape[1]
    parts = dot(jnp.concatenate([raw, raw], axis=1), turn)
    return (parts[:, :lanes] + parts[:, lanes:]).astype(bf16).astype(f32)


def update(src, dst, across, down, sums, row, take, counted, kept=True):
    groups = src.shape[1]
    last = groups - 1
    span = range(take)
    start = [src[row + r, 0] for r in span]
    closing = [
        across[row + r, last] * (pltpu.roll(start[r], SUB - 1, 0) - src[row + r, last])
        for r in span
    ]
    wrapped = [pltpu.roll(flux, 1, 0) for flux in closing]

    def vertical(g, here):
        above = down[row - 1, g] * (here[0] - src[row - 1, g])
        change = []
        for r in span:
            below = here[r + 1] if r + 1 < take else src[row + take, g]
            under = down[row + r, g] * (below - here[r])
            change.append(under - above)
            above = under
        return change

    def finish(r, g, old, new):
        if kept:
            dst[row + r, g] = new
        if counted:
            sums[row + r, g] += old * old + new * new

    here = [src[row + r, 1] for r in span]
    west = [across[row + r, 0] * (here[r] - start[r]) for r in span]
    change = vertical(0, start)
    pending = [start[r] + (change[r] + west[r]) for r in span]
    for g in range(1, groups):
        if g < last:
            following = [src[row + r, g + 1] for r in span]
            flux = [across[row + r, g] * (following[r] - here[r]) for r in span]
        else:
            following, flux = None, closing
        change = vertical(g, here)
        for r in span:
            finish(r, g, here[r], here[r] + (change[r] + (flux[r] - west[r])))
        here, west = following, flux
    for r in span:
        finish(r, 0, start[r], pending[r] - wrapped[r])


def summed_lanes(sums, rows, totals):
    lane = iota(totals[0].shape, 1)
    for row, to in rows:
        for g in range(len(totals)):
            total = jnp.sum(sums[row, g], axis=1, keepdims=True)
            totals[g] = totals[g] + jnp.where(lane == to, total, 0.0)
    return totals


def inner_kernel(
    own_ref, turn_ref, across_hbm, down_hbm, first_hbm, second_hbm,
    first_ref, second_ref, across_ref, down_ref, sum_ref, sems,
):
    tall, groups, _, lanes = second_ref.shape
    inside = pl.ds(HALO, tall)
    fetches = [
        pltpu.make_async_copy(across_hbm.at[inside], across_ref, sems.at[0]),
        pltpu.make_async_copy(down_hbm.at[inside], down_ref, sems.at[1]),
    ]
    for fetch in fetches:
        fetch.start()
    turn = turn_ref[...]
    take = 4
    cells = take * groups * SUB

    for c in range(tall // take):
        field = rotated(own_ref[c * cells : (c + 1) * cells, :], turn)
        first_ref[c * take : (c + 1) * take] = field.reshape(take, groups, SUB, lanes)
    sum_ref[...] = jnp.zeros_like(sum_ref)
    second_ref[0] = jnp.zeros(second_ref.shape[1:], f32)
    second_ref[tall - 1] = jnp.zeros(second_ref.shape[1:], f32)
    for fetch in fetches:
        fetch.wait()

    for s in range(SWEEPS):
        src, dst = (first_ref, second_ref) if s % 2 == 0 else (second_ref, first_ref)
        count = tall - 2 - 2 * s
        size = -(-count // -(-count // BLOCK))
        run = functools.partial(update, src, dst, across_ref, down_ref, sum_ref)
        flags = (s % 2 == 1, s < SWEEPS - 1)

        def step(c, carry):
            run(s + 1 + c * size, size, *flags)
            return carry

        lax.fori_loop(0, count // size, step, 0)
        if count % size:
            run(s + 1 + count - count % size, count % size, *flags)

    near = HALO + 1
    leaving = []
    for k, (source, target) in enumerate(((first_ref, first_hbm), (second_ref, second_hbm))):
        for side, row in enumerate((0, tall - near)):
            part = pl.ds(row, near)
            leaving.append(
                pltpu.make_async_copy(source.at[part], target.at[part], sems.at[2 + 2 * k + side])
            )
    for copy in leaving:
        copy.start()

    def gather(c, totals):
        rows = [(c * 4 + h, c * 4 + h) for h in range(4)]
        return tuple(summed_lanes(sum_ref, rows, list(totals)))

    zeros = tuple(jnp.zeros((SUB, lanes), f32) for _ in range(groups))
    totals = lax.fori_loop(0, tall // 4, gather, zeros)
    for g in range(groups):
        first_ref[tall, g] = totals[g]
    part = pl.ds(tall, 1)
    leaving.append(pltpu.make_async_copy(first_ref.at[part], first_hbm.at[part], sems.at[6]))
    leaving[-1].start()
    for copy in leaving:
        copy.wait()


def inner_sweeps(own, inverse, across_down):
    tall, places, lanes = own.shape
    own = own.reshape(tall * places, lanes)
    vmem = pl.BlockSpec(memory_space=pltpu.VMEM)
    far = pl.BlockSpec(memory_space=pl.ANY)
    shape = (tall, places // SUB, SUB, lanes)
    longer = (tall + 1,) + shape[1:]
    return pl.pallas_call(
        inner_kernel,
        out_shape=(jax.ShapeDtypeStruct(longer, f32), jax.ShapeDtypeStruct(shape, f32)),
        in_specs=[vmem, vmem, far, far],
        out_specs=(far, far),
        scratch_shapes=[pltpu.VMEM(longer, f32)]
        + [pltpu.VMEM(shape, f32)] * 4
        + [pltpu.SemaphoreType.DMA((7,))],
        compiler_params=pltpu.CompilerParams(vmem_limit_bytes=VMEM_BYTES),
        cost_estimate=pl.CostEstimate(
            flops=12 * 10**9, bytes_accessed=8 * own.size, transcendentals=0
        ),
        name="inner_sweeps",
    )(own, inverse, *across_down)


def outer_kernel(
    scale, ends_ref, turn_ref, north_hbm, south_hbm, first_hbm, second_hbm,
    across_hbm, down_hbm, out_ref, first_ref, second_ref, across_ref, down_ref, sum_ref,
    north_ref, south_ref, inner_ref, sems,
):
    rows, groups, _, lanes = first_ref.shape
    tall = rows - 2 * HALO
    places = groups * SUB
    near = HALO + 1
    halos = [
        pltpu.make_async_copy(north_hbm, north_ref, sems.at[0]),
        pltpu.make_async_copy(south_hbm, south_ref, sems.at[1]),
    ]
    for halo in halos:
        halo.start()
    soon, late = [], []

    def fetch(wave, source, target, start, take, shift):
        wave.append(
            pltpu.make_async_copy(
                source.at[pl.ds(start, take)],
                target.at[pl.ds(start + shift, take)],
                sems.at[2 + len(soon) + len(late)],
            )
        )

    reach = HALO + 2
    wide_part = 2 * HALO + 1
    for source, target in ((across_hbm, across_ref), (down_hbm, down_ref)):
        fetch(soon, source, target, 0, reach, 0)
        fetch(soon, source, target, rows - reach, reach, 0)
    fetch(soon, first_hbm, first_ref, 0, 2, HALO)
    fetch(soon, first_hbm, first_ref, tall - 2, 2, HALO)
    fetch(late, second_hbm, second_ref, 1, near - 1, HALO)
    fetch(late, second_hbm, second_ref, tall - near, near - 1, HALO)
    for source, target in ((across_hbm, across_ref), (down_hbm, down_ref)):
        fetch(late, source, target, reach, wide_part - reach, 0)
        fetch(late, source, target, rows - wide_part, wide_part - reach, 0)
    fetch(late, first_hbm, first_ref, 2, near - 2, HALO)
    fetch(late, first_hbm, first_ref, tall - near, near - 2, HALO)
    fetch(late, first_hbm, inner_ref, tall, 1, -tall)
    for copy in soon + late:
        copy.start()
    sum_ref[...] = jnp.zeros_like(sum_ref)
    turn = turn_ref[...]
    for halo in halos:
        halo.wait()
    take = 2
    cells = take * places

    for c in range(HALO // take):
        for source, offset in ((north_ref, 0), (south_ref, HALO + tall)):
            field = rotated(source[c * cells : (c + 1) * cells, :], turn)
            first_ref[offset + c * take : offset + (c + 1) * take] = field.reshape(
                take, groups, SUB, lanes
            )
    take = HALO // 2
    for copy in soon:
        copy.wait()

    for s in range(SWEEPS):
        src, dst = (first_ref, second_ref) if s % 2 == 0 else (second_ref, first_ref)
        run = functools.partial(update, src, dst, across_ref, down_ref, sum_ref)
        if s == 1:
            for copy in late:
                copy.wait()

        def both(side, carry):
            halo = HALO - 1 - s
            if s % 2 == 0:
                start = jnp.where(side == 0, s + 1, rows - 1 - HALO - s)
                run(start, take, False)
                run(start + take, take, False)
                return carry
            if halo > 0:
                run(jnp.where(side == 0, s + 1, HALO + tall), halo, False)
            start = jnp.where(side == 0, HALO, rows - 1 - HALO - s)
            done = 0
            while done < s + 1:
                size = min(s + 1 - done, 2 * take if s + 1 < 2 * take else take)
                run(start + done, size, True, s < SWEEPS - 1)
                done += size
            return carry

        lax.fori_loop(0, 2, both, 0)
        if s < SWEEPS - 1:

            @pl.when(ends_ref[0] == 1)
            def _():
                dst[HALO - 1] = jnp.zeros(dst.shape[1:], f32)

            @pl.when(ends_ref[1] == 1)
            def _():
                dst[HALO + tall] = jnp.zeros(dst.shape[1:], f32)

    def gather(c, totals):
        pairs = []
        for row in (2 * c, 2 * c + 1):
            pairs += [(HALO + row, row), (tall + row, tall - HALO + row)]
        return tuple(summed_lanes(sum_ref, pairs, list(totals)))

    totals = tuple(inner_ref[0, g] for g in range(groups))
    totals = lax.fori_loop(0, HALO // 2, gather, totals)
    totals = jnp.concatenate(totals, axis=0).T[:tall]
    slot = iota((places, out_ref.shape[1]), 0)
    column = iota((places, out_ref.shape[1]), 1)
    back = (column == (slot % SUB) * groups + slot // SUB).astype(f32).astype(bf16)
    high, mid, low = split3(totals)
    out_ref[...] = (dot(high, back) + (dot(mid, back) + dot(low, back))) * scale


def outer_sweeps(scale, ends, north, south, inverse, inner, across_down, wide):
    first, second = inner
    tall, groups, _, lanes = second.shape
    shape = (tall + 2 * HALO, groups, SUB, lanes)
    north, south = (x.reshape(-1, lanes) for x in (north, south))
    vmem = pl.BlockSpec(memory_space=pltpu.VMEM)
    far = pl.BlockSpec(memory_space=pl.ANY)
    return pl.pallas_call(
        functools.partial(outer_kernel, scale),
        out_shape=jax.ShapeDtypeStruct((tall, wide), f32),
        in_specs=[pl.BlockSpec(memory_space=pltpu.SMEM), vmem] + [far] * 6,
        out_specs=vmem,
        scratch_shapes=[pltpu.VMEM(shape, f32)] * 5
        + [pltpu.VMEM(north.shape, bf16)] * 2
        + [pltpu.VMEM((1,) + shape[1:], f32), pltpu.SemaphoreType.DMA((17,))],
        compiler_params=pltpu.CompilerParams(vmem_limit_bytes=OUTER_BYTES),
        name="outer_sweeps",
    )(ends, inverse, north, south, first, second, *across_down)


def from_before(x, axis, closed):
    count = lax.axis_size(axis)
    return lax.ppermute(
        x, axis, [(i, (i + 1) % count) for i in range(count if closed else count - 1)]
    )


def from_after(x, axis, closed):
    count = lax.axis_size(axis)
    return lax.ppermute(
        x, axis, [((i + 1) % count, i) for i in range(count if closed else count - 1)]
    )


def ahead(values, axis, step):
    count = lax.axis_size(axis)
    return lax.ppermute(values, axis, [((i + step) % count, i) for i in range(count)])


def neighbours(x, extra, axis):
    size = x.shape[0]
    sent = jnp.concatenate([x, extra], axis=0)
    after, before, second = ahead(sent, axis, 1), ahead(sent, axis, -1), ahead(x, axis, 2)
    x = (x + before[:size]) + (after[:size] + second)
    return x, before[size:], after[size:]


def rest_of_ring(x, axis):
    step = 4
    while step < lax.axis_size(axis):
        x = x + ahead(x, axis, step)
        step *= 2
    return x


def per_device(basis, order, land, conduct):
    axes = ("lat", "lon")
    rows_here, width = basis.shape
    tall, wide = land.shape
    count = lax.axis_size("lat") * lax.axis_size("lon")
    cells = rows_here * count
    tied = lax.optimization_barrier
    at = lax.axis_index("lat")
    top, bottom = at == 0, at == lax.axis_size("lat") - 1

    whole_rows = rows_here // count == wide
    moving = deal(basis, order, lax.axis_size("lon"), wide) if whole_rows else basis[order]
    moving, basis, land, conduct = tied((moving, basis, land, conduct))
    raw = lax.all_to_all(moving, axes, split_axis=0, concat_axis=0, tiled=True)
    if not whole_rows:
        raw = raw.reshape(tall, wide, width)
        left = from_before(raw[:, -HALO:], "lon", True)
        right = from_after(raw[:, :HALO], "lon", True)
        raw = circle(raw, right, left, 1)

    partial = lax.dot_general(
        basis, basis, (((0,), (0,)), ((), ())), preferred_element_type=f32
    )
    coef = conduct * (0.35 + 0.65 * land.astype(f32))
    edges = jnp.concatenate([coef[:HALO], coef[-HALO:]], axis=0)
    edges = jnp.pad(edges, ((0, 4), (0, width - wide)))
    partial, before, after = neighbours(partial, edges, "lat")
    partial = rest_of_ring(partial, "lat")
    before = jnp.where(top, 0.0, before[HALO : 2 * HALO, :wide])
    after = jnp.where(bottom, 0.0, after[:HALO, :wide])
    coef = jnp.concatenate([before, coef, after], axis=0)
    edges = jnp.concatenate([coef[:, :HALO], coef[:, -HALO:]], axis=1)
    edges = jnp.pad(edges, ((0, 4), (0, width - 2 * HALO)))
    partial, before, after = neighbours(partial, edges, "lon")
    rows = coef.shape[0]
    coef = circle(coef, after[:rows, :HALO], before[:rows, HALO : 2 * HALO], 1)
    gram = rest_of_ring(partial, "lon")
    inverse = factor_inverse(gram)
    across_down = weights(coef, width)
    ends = jnp.stack([top, bottom]).astype(i32)
    raw, inverse, across_down, ends = tied((raw, inverse, across_down, ends))

    north = from_before(raw[-HALO:], "lat", False)
    south = from_after(raw[:HALO], "lat", False)
    inner = inner_sweeps(raw, inverse, across_down)
    scale = cells / (width * SWEEPS)
    return outer_sweeps(scale, ends, north, south, inverse, inner, across_down, wide)


def solution(mesh):
    in_specs = (P(("lat", "lon"), None), P(("lat", "lon")), P("lat", "lon"), P("lat", "lon"))
    out_specs = P("lat", "lon")
    return jax.shard_map(
        per_device, mesh=mesh, in_specs=in_specs, out_specs=out_specs, check_vma=False
    )
```

```python
import functools

import jax
import jax.numpy as jnp
from jax import lax
from jax.experimental import pallas as pl
from jax.experimental.pallas import tpu as pltpu
from jax.sharding import PartitionSpec as P

SWEEPS = 10
HALO = SWEEPS
LANES = 128
SUB = 8
ONE_HOT = 1024
TILES = 2
BLOCK = 8
VMEM_BYTES = 56 * 1024 * 1024
OUTER_BYTES = 52 * 1024 * 1024

bf16, f32, i32 = jnp.bfloat16, jnp.float32, jnp.int32


def iota(shape, dim):
    return lax.broadcasted_iota(i32, shape, dim)


def dot(a, b):
    return jnp.dot(a, b, preferred_element_type=f32)


def split3(x):
    high = x.astype(bf16)
    rest = x - high.astype(f32)
    mid = rest.astype(bf16)
    low = (rest - mid.astype(f32)).astype(bf16)
    return high, mid, low


def slots(wide):
    return -(-(wide + 2 * HALO) // SUB) * SUB


def circle(own, right, left, axis):
    wide = own.shape[axis]
    count = slots(wide)
    gap = list(own.shape)
    gap[axis] = count - wide - 2 * HALO
    around = jnp.concatenate([own, right, jnp.zeros(gap, own.dtype), left], axis=axis)
    shape = around.shape
    around = around.reshape(shape[:axis] + (SUB, count // SUB) + shape[axis + 1 :])
    return jnp.swapaxes(around, axis, axis + 1).reshape(shape)


def deal_kernel(tiles_lon, basis_ref, order_ref, out_ref, slot_ref, ready_ref, sems):
    rows, width = basis_ref.shape
    parts = rows // ONE_HOT
    tiles, places, _ = out_ref.shape
    wide = order_ref.shape[1]
    groups = places // SUB
    stacked = jnp.concatenate(
        [basis_ref[q * ONE_HOT : (q + 1) * ONE_HOT, :] for q in range(parts)], axis=1
    )

    order = order_ref[...]
    at = iota(order.shape, 0) % tiles_lon
    after = jnp.where(
        at == tiles_lon - 1, pltpu.roll(order, tiles_lon - 1, 0), pltpu.roll(order, tiles - 1, 0)
    )
    before = jnp.where(
        at == 0, pltpu.roll(order, tiles - tiles_lon + 1, 0), pltpu.roll(order, 1, 0)
    )
    padded = slot_ref.shape[1]
    column = iota((wide, padded), 0)
    slot = iota((wide, padded), 1)
    place = jnp.where(slot < places, (slot % SUB) * groups + slot // SUB, -1)
    sources, hits = [], []
    for source, hit in (
        (order, (place < wide) & (column == place)),
        (after, (place < wide + HALO) & (column == place - wide)),
        (before, (place >= places - HALO) & (column == place - places + wide)),
    ):
        hits.append(hit.astype(f32).astype(bf16))
        halves = jnp.concatenate([source & 63, source >> 6], axis=0)
        sources.append(halves.astype(f32).astype(bf16))
    halves = dot(jnp.concatenate(sources, axis=1), jnp.concatenate(hits, axis=0))
    slot_ref[...] = (halves[tiles:] * 64.0 + halves[:tiles]).astype(i32)

    take = TILES
    steps = tiles // take

    def leave(c):
        return pltpu.make_async_copy(
            ready_ref.at[pl.ds(c * take, take)],
            out_ref.at[pl.ds(c * take, take)],
            sems.at[c],
        )

    lane = iota((take * places, LANES), 1)

    for c in range(steps):
        wanted = []
        for h in range(take):
            order = slot_ref[c * take + h : c * take + h + 1, :]
            wanted.append(jnp.broadcast_to(order, (LANES, padded)).T[:places])
        wanted = jnp.concatenate(wanted, axis=0)
        within = wanted & (ONE_HOT - 1)
        part = wanted - within
        marks = [
            (within == lane + b * LANES).astype(f32).astype(bf16)
            for b in range(ONE_HOT // LANES)
        ]
        found = dot(jnp.concatenate(marks, axis=1), stacked)
        picked = found[:, :width]
        for q in range(1, parts):
            picked = jnp.where(
                part == q * ONE_HOT, found[:, q * width : (q + 1) * width], picked
            )
        for h in range(take):
            ready_ref[c * take + h] = picked[h * places : (h + 1) * places].astype(bf16)
        leave(c).start()
    for c in range(steps):
        leave(c).wait()


def deal(basis, order, tiles_lon, wide):
    rows, width = basis.shape
    tiles = rows // wide
    places = slots(wide)
    vmem = pl.BlockSpec(memory_space=pltpu.VMEM)
    return pl.pallas_call(
        functools.partial(deal_kernel, tiles_lon),
        out_shape=jax.ShapeDtypeStruct((tiles, places, width), bf16),
        in_specs=[vmem, vmem],
        out_specs=pl.BlockSpec(memory_space=pl.ANY),
        scratch_shapes=[
            pltpu.VMEM((tiles, -(-places // LANES) * LANES), i32),
            pltpu.VMEM((tiles, places, width), bf16),
            pltpu.SemaphoreType.DMA((tiles // TILES,)),
        ],
        compiler_params=pltpu.CompilerParams(vmem_limit_bytes=VMEM_BYTES),
        cost_estimate=pl.CostEstimate(
            flops=2 * tiles * places * rows * width,
            bytes_accessed=4 * rows * width,
            transcendentals=0,
        ),
        name="deal",
    )(basis, order.reshape(tiles, wide))


def inverse_kernel(gram_ref, turn_ref, out_ref):
    size = gram_ref.shape[0]
    count = size // SUB
    shape = (SUB, size)
    tiles = [gram_ref[t * SUB : (t + 1) * SUB, :] for t in range(count)]
    lane = iota(shape, 1)
    sub = iota(shape, 0)
    for top in range(count):
        first = top * SUB
        inside = (lane >= first) & (lane < first + SUB)
        columns = [
            [jnp.broadcast_to(tiles[t][:, first + c : first + c + 1], shape) for t in range(top, count)]
            for c in range(SUB)
        ]
        core = {
            (r, c): jnp.broadcast_to(columns[c][0][r : r + 1, :], shape)
            for r in range(SUB)
            for c in range(r, SUB)
        }
        lines = [
            jnp.where(
                inside,
                jnp.where(lane == first + c, 1.0, 0.0),
                jnp.broadcast_to(tiles[top][c : c + 1, :], shape),
            )
            for c in range(SUB)
        ]
        scales = []
        for c in range(SUB):
            inverse = 1.0 / core[c, c]
            scales.append(inverse)
            for d in range(c + 1, SUB):
                factor = core[c, d] * inverse
                for e in range(d, SUB):
                    core[d, e] = core[d, e] - factor * core[c, e]
                lines[d] = lines[d] - factor * lines[c]
                for t in range(1, count - top):
                    columns[d][t] = columns[d][t] - factor * columns[c][t]
        for t in range(1, count - top):
            rest = jnp.where(inside, 0.0, tiles[top + t])
            for c in range(SUB):
                rest = rest - columns[c][t] * (scales[c] * lines[c])
            tiles[top + t] = rest
        merged = lines[0]
        pivot = core[0, 0]
        for c in range(1, SUB):
            merged = jnp.where(sub == c, lines[c], merged)
            pivot = jnp.where(sub == c, core[c, c], pivot)
        kept = jnp.where(lane <= sub + first, merged, 0.0)
        out_ref[first : first + SUB, :] = kept * (1.0 / jnp.sqrt(pivot))
    turn_ref[...] = rotation(out_ref[...])


def factor_inverse(gram):
    size = gram.shape[0]
    return pl.pallas_call(
        inverse_kernel,
        out_shape=jax.ShapeDtypeStruct((2 * size, 2 * size), bf16),
        scratch_shapes=[pltpu.VMEM(gram.shape, f32)],
        compiler_params=pltpu.CompilerParams(vmem_limit_bytes=VMEM_BYTES),
        cost_estimate=pl.CostEstimate(
            flops=40 * size**4, bytes_accessed=8 * size * size, transcendentals=0
        ),
        name="factor_inverse",
    )(gram)


def weight_kernel(coef_ref, across_hbm, down_hbm, spread, across_ref, down_ref, sems):
    rows, groups, _, lanes = spread.shape
    places = groups * SUB
    turned = coef_ref[...].T
    depth = turned.shape[1]
    pieces = jnp.concatenate(split3(turned[:places]), axis=1)
    per_step = rows // 4
    offset = iota((3 * depth, per_step * lanes), 0) & (depth - 1)
    offset = offset - (iota((3 * depth, per_step * lanes), 1) // lanes)

    def put(c, carry):
        values = dot(pieces, (offset == c * per_step).astype(f32).astype(bf16))
        for h in range(per_step):
            spread[c * per_step + h] = values[:, h * lanes : (h + 1) * lanes].reshape(
                groups, SUB, lanes
            )
        return carry

    lax.fori_loop(0, 4, put, 0)

    def weigh(r, carry):
        for g in range(groups):
            here = spread[r, g]
            east = spread[r, g + 1] if g + 1 < groups else pltpu.roll(spread[r, 0], SUB - 1, 0)
            across_ref[r, g] = 0.124 * (here + east)
            down_ref[r, g] = 0.124 * (here + spread[r + 1, g])
        return carry

    across_ref[rows - 1] = jnp.zeros((groups, SUB, lanes), f32)
    down_ref[rows - 1] = jnp.zeros((groups, SUB, lanes), f32)
    leaving = []
    for c in range(4):
        lax.fori_loop(c * per_step, min((c + 1) * per_step, rows - 1), weigh, 0)
        part = pl.ds(c * per_step, per_step)
        for k, (source, target) in enumerate(((across_ref, across_hbm), (down_ref, down_hbm))):
            leaving.append(
                pltpu.make_async_copy(source.at[part], target.at[part], sems.at[2 * c + k])
            )
            leaving[-1].start()
    for copy in leaving:
        copy.wait()


def weights(coef, lanes):
    rows, places = coef.shape
    coef = jnp.pad(coef, ((0, -rows % 64), (0, -places % LANES)))
    shape = (rows, places // SUB, SUB, lanes)
    return pl.pallas_call(
        weight_kernel,
        out_shape=(jax.ShapeDtypeStruct(shape, f32),) * 2,
        out_specs=(pl.BlockSpec(memory_space=pl.ANY),) * 2,
        scratch_shapes=[pltpu.VMEM(shape, f32)] * 3 + [pltpu.SemaphoreType.DMA((8,))],
        compiler_params=pltpu.CompilerParams(vmem_limit_bytes=VMEM_BYTES),
        cost_estimate=pl.CostEstimate(
            flops=rows * places * lanes * 100, bytes_accessed=8 * rows * places * lanes, transcendentals=0
        ),
        name="weights",
    )(coef)


def rotation(inverse):
    high, mid, low = split3(inverse.T)
    return jnp.concatenate(
        [jnp.concatenate([high, low], axis=1), jnp.concatenate([mid, jnp.zeros_like(mid)], axis=1)],
        axis=0,
    )


def rotated(raw, turn):
    lanes = raw.shape[1]
    parts = dot(jnp.concatenate([raw, raw], axis=1), turn)
    return (parts[:, :lanes] + parts[:, lanes:]).astype(bf16).astype(f32)


def update(src, dst, across, down, sums, row, take, counted, kept=True):
    groups = src.shape[1]
    last = groups - 1
    span = range(take)
    start = [src[row + r, 0] for r in span]
    closing = [
        across[row + r, last] * (pltpu.roll(start[r], SUB - 1, 0) - src[row + r, last])
        for r in span
    ]
    wrapped = [pltpu.roll(flux, 1, 0) for flux in closing]

    def vertical(g, here):
        above = down[row - 1, g] * (here[0] - src[row - 1, g])
        change = []
        for r in span:
            below = here[r + 1] if r + 1 < take else src[row + take, g]
            under = down[row + r, g] * (below - here[r])
            change.append(under - above)
            above = under
        return change

    def finish(r, g, old, new):
        if kept:
            dst[row + r, g] = new
        if counted:
            sums[row + r, g] += old * old + new * new

    here = [src[row + r, 1] for r in span]
    west = [across[row + r, 0] * (here[r] - start[r]) for r in span]
    change = vertical(0, start)
    pending = [start[r] + (change[r] + west[r]) for r in span]
    for g in range(1, groups):
        if g < last:
            following = [src[row + r, g + 1] for r in span]
            flux = [across[row + r, g] * (following[r] - here[r]) for r in span]
        else:
            following, flux = None, closing
        change = vertical(g, here)
        for r in span:
            finish(r, g, here[r], here[r] + (change[r] + (flux[r] - west[r])))
        here, west = following, flux
    for r in span:
        finish(r, 0, start[r], pending[r] - wrapped[r])


def summed_lanes(sums, rows, totals):
    lane = iota(totals[0].shape, 1)
    for row, to in rows:
        for g in range(len(totals)):
            total = jnp.sum(sums[row, g], axis=1, keepdims=True)
            totals[g] = totals[g] + jnp.where(lane == to, total, 0.0)
    return totals


def inner_kernel(
    own_ref, turn_ref, across_hbm, down_hbm, first_hbm, second_hbm,
    first_ref, second_ref, across_ref, down_ref, sum_ref, sems,
):
    tall, groups, _, lanes = second_ref.shape
    inside = pl.ds(HALO, tall)
    fetches = [
        pltpu.make_async_copy(across_hbm.at[inside], across_ref, sems.at[0]),
        pltpu.make_async_copy(down_hbm.at[inside], down_ref, sems.at[1]),
    ]
    for fetch in fetches:
        fetch.start()
    turn = turn_ref[...]
    take = 4
    cells = take * groups * SUB

    for c in range(tall // take):
        field = rotated(own_ref[c * cells : (c + 1) * cells, :], turn)
        first_ref[c * take : (c + 1) * take] = field.reshape(take, groups, SUB, lanes)
    sum_ref[...] = jnp.zeros_like(sum_ref)
    second_ref[0] = jnp.zeros(second_ref.shape[1:], f32)
    second_ref[tall - 1] = jnp.zeros(second_ref.shape[1:], f32)
    for fetch in fetches:
        fetch.wait()

    for s in range(SWEEPS):
        src, dst = (first_ref, second_ref) if s % 2 == 0 else (second_ref, first_ref)
        count = tall - 2 - 2 * s
        size = -(-count // -(-count // BLOCK))
        run = functools.partial(update, src, dst, across_ref, down_ref, sum_ref)
        flags = (s % 2 == 1, s < SWEEPS - 1)

        def step(c, carry):
            run(s + 1 + c * size, size, *flags)
            return carry

        lax.fori_loop(0, count // size, step, 0)
        if count % size:
            run(s + 1 + count - count % size, count % size, *flags)

    near = HALO + 1
    leaving = []
    for k, (source, target) in enumerate(((first_ref, first_hbm), (second_ref, second_hbm))):
        for side, row in enumerate((0, tall - near)):
            part = pl.ds(row, near)
            leaving.append(
                pltpu.make_async_copy(source.at[part], target.at[part], sems.at[2 + 2 * k + side])
            )
    for copy in leaving:
        copy.start()

    def gather(c, totals):
        rows = [(c * 4 + h, c * 4 + h) for h in range(4)]
        return tuple(summed_lanes(sum_ref, rows, list(totals)))

    zeros = tuple(jnp.zeros((SUB, lanes), f32) for _ in range(groups))
    totals = lax.fori_loop(0, tall // 4, gather, zeros)
    for g in range(groups):
        first_ref[tall, g] = totals[g]
    part = pl.ds(tall, 1)
    leaving.append(pltpu.make_async_copy(first_ref.at[part], first_hbm.at[part], sems.at[6]))
    leaving[-1].start()
    for copy in leaving:
        copy.wait()


def inner_sweeps(own, inverse, across_down):
    tall, places, lanes = own.shape
    own = own.reshape(tall * places, lanes)
    vmem = pl.BlockSpec(memory_space=pltpu.VMEM)
    far = pl.BlockSpec(memory_space=pl.ANY)
    shape = (tall, places // SUB, SUB, lanes)
    longer = (tall + 1,) + shape[1:]
    return pl.pallas_call(
        inner_kernel,
        out_shape=(jax.ShapeDtypeStruct(longer, f32), jax.ShapeDtypeStruct(shape, f32)),
        in_specs=[vmem, vmem, far, far],
        out_specs=(far, far),
        scratch_shapes=[pltpu.VMEM(longer, f32)]
        + [pltpu.VMEM(shape, f32)] * 4
        + [pltpu.SemaphoreType.DMA((7,))],
        compiler_params=pltpu.CompilerParams(vmem_limit_bytes=VMEM_BYTES),
        cost_estimate=pl.CostEstimate(
            flops=12 * 10**9, bytes_accessed=8 * own.size, transcendentals=0
        ),
        name="inner_sweeps",
    )(own, inverse, *across_down)


def outer_kernel(
    scale, ends_ref, turn_ref, north_hbm, south_hbm, first_hbm, second_hbm,
    across_hbm, down_hbm, out_ref, first_ref, second_ref, across_ref, down_ref, sum_ref,
    north_ref, south_ref, inner_ref, sems,
):
    rows, groups, _, lanes = first_ref.shape
    tall = rows - 2 * HALO
    places = groups * SUB
    near = HALO + 1
    halos = [
        pltpu.make_async_copy(north_hbm, north_ref, sems.at[0]),
        pltpu.make_async_copy(south_hbm, south_ref, sems.at[1]),
    ]
    for halo in halos:
        halo.start()
    soon, late = [], []

    def fetch(wave, source, target, start, take, shift):
        wave.append(
            pltpu.make_async_copy(
                source.at[pl.ds(start, take)],
                target.at[pl.ds(start + shift, take)],
                sems.at[2 + len(soon) + len(late)],
            )
        )

    reach = HALO + 2
    wide_part = 2 * HALO + 1
    for source, target in ((across_hbm, across_ref), (down_hbm, down_ref)):
        fetch(soon, source, target, 0, reach, 0)
        fetch(soon, source, target, rows - reach, reach, 0)
    fetch(soon, first_hbm, first_ref, 0, 2, HALO)
    fetch(soon, first_hbm, first_ref, tall - 2, 2, HALO)
    fetch(late, second_hbm, second_ref, 1, near - 1, HALO)
    fetch(late, second_hbm, second_ref, tall - near, near - 1, HALO)
    for source, target in ((across_hbm, across_ref), (down_hbm, down_ref)):
        fetch(late, source, target, reach, wide_part - reach, 0)
        fetch(late, source, target, rows - wide_part, wide_part - reach, 0)
    fetch(late, first_hbm, first_ref, 2, near - 2, HALO)
    fetch(late, first_hbm, first_ref, tall - near, near - 2, HALO)
    fetch(late, first_hbm, inner_ref, tall, 1, -tall)
    for copy in soon + late:
        copy.start()
    sum_ref[...] = jnp.zeros_like(sum_ref)
    turn = turn_ref[...]
    for halo in halos:
        halo.wait()
    take = 2
    cells = take * places

    for c in range(HALO // take):
        for source, offset in ((north_ref, 0), (south_ref, HALO + tall)):
            field = rotated(source[c * cells : (c + 1) * cells, :], turn)
            first_ref[offset + c * take : offset + (c + 1) * take] = field.reshape(
                take, groups, SUB, lanes
            )
    take = HALO // 2
    for copy in soon:
        copy.wait()

    for s in range(SWEEPS):
        src, dst = (first_ref, second_ref) if s % 2 == 0 else (second_ref, first_ref)
        run = functools.partial(update, src, dst, across_ref, down_ref, sum_ref)
        if s == 1:
            for copy in late:
                copy.wait()

        def both(side, carry):
            halo = HALO - 1 - s
            if s % 2 == 0:
                start = jnp.where(side == 0, s + 1, rows - 1 - HALO - s)
                run(start, take, False)
                run(start + take, take, False)
                return carry
            if halo > 0:
                run(jnp.where(side == 0, s + 1, HALO + tall), halo, False)
            start = jnp.where(side == 0, HALO, rows - 1 - HALO - s)
            done = 0
            while done < s + 1:
                size = min(s + 1 - done, 2 * take if s + 1 < 2 * take else take)
                run(start + done, size, True, s < SWEEPS - 1)
                done += size
            return carry

        lax.fori_loop(0, 2, both, 0)
        if s < SWEEPS - 1:

            @pl.when(ends_ref[0] == 1)
            def _():
                dst[HALO - 1] = jnp.zeros(dst.shape[1:], f32)

            @pl.when(ends_ref[1] == 1)
            def _():
                dst[HALO + tall] = jnp.zeros(dst.shape[1:], f32)

    def gather(c, totals):
        pairs = []
        for row in (2 * c, 2 * c + 1):
            pairs += [(HALO + row, row), (tall + row, tall - HALO + row)]
        return tuple(summed_lanes(sum_ref, pairs, list(totals)))

    totals = tuple(inner_ref[0, g] for g in range(groups))
    totals = lax.fori_loop(0, HALO // 2, gather, totals)
    totals = jnp.concatenate(totals, axis=0).T[:tall]
    slot = iota((places, out_ref.shape[1]), 0)
    column = iota((places, out_ref.shape[1]), 1)
    back = (column == (slot % SUB) * groups + slot // SUB).astype(f32).astype(bf16)
    high, mid, low = split3(totals)
    out_ref[...] = (dot(high, back) + (dot(mid, back) + dot(low, back))) * scale


def outer_sweeps(scale, ends, north, south, inverse, inner, across_down, wide):
    first, second = inner
    tall, groups, _, lanes = second.shape
    shape = (tall + 2 * HALO, groups, SUB, lanes)
    north, south = (x.reshape(-1, lanes) for x in (north, south))
    vmem = pl.BlockSpec(memory_space=pltpu.VMEM)
    far = pl.BlockSpec(memory_space=pl.ANY)
    return pl.pallas_call(
        functools.partial(outer_kernel, scale),
        out_shape=jax.ShapeDtypeStruct((tall, wide), f32),
        in_specs=[pl.BlockSpec(memory_space=pltpu.SMEM), vmem] + [far] * 6,
        out_specs=vmem,
        scratch_shapes=[pltpu.VMEM(shape, f32)] * 5
        + [pltpu.VMEM(north.shape, bf16)] * 2
        + [pltpu.VMEM((1,) + shape[1:], f32), pltpu.SemaphoreType.DMA((17,))],
        compiler_params=pltpu.CompilerParams(vmem_limit_bytes=OUTER_BYTES),
        name="outer_sweeps",
    )(ends, inverse, north, south, first, second, *across_down)


def from_before(x, axis, closed):
    count = lax.axis_size(axis)
    return lax.ppermute(
        x, axis, [(i, (i + 1) % count) for i in range(count if closed else count - 1)]
    )


def from_after(x, axis, closed):
    count = lax.axis_size(axis)
    return lax.ppermute(
        x, axis, [((i + 1) % count, i) for i in range(count if closed else count - 1)]
    )


def ahead(values, axis, step):
    count = lax.axis_size(axis)
    return lax.ppermute(values, axis, [((i + step) % count, i) for i in range(count)])


def neighbours(x, extra, axis):
    size = x.shape[0]
    sent = jnp.concatenate([x, extra], axis=0)
    after, before, second = ahead(sent, axis, 1), ahead(sent, axis, -1), ahead(x, axis, 2)
    x = (x + before[:size]) + (after[:size] + second)
    return x, before[size:], after[size:]


def rest_of_ring(x, axis):
    step = 4
    while step < lax.axis_size(axis):
        x = x + ahead(x, axis, step)
        step *= 2
    return x


def per_device(basis, order, land, conduct):
    axes = ("lat", "lon")
    rows_here, width = basis.shape
    tall, wide = land.shape
    count = lax.axis_size("lat") * lax.axis_size("lon")
    cells = rows_here * count
    tied = lax.optimization_barrier
    at = lax.axis_index("lat")
    top, bottom = at == 0, at == lax.axis_size("lat") - 1

    whole_rows = rows_here // count == wide
    moving = deal(basis, order, lax.axis_size("lon"), wide) if whole_rows else basis[order]
    moving, basis, land, conduct = tied((moving, basis, land, conduct))
    raw = lax.all_to_all(moving, axes, split_axis=0, concat_axis=0, tiled=True)
    if not whole_rows:
        raw = raw.reshape(tall, wide, width)
        left = from_before(raw[:, -HALO:], "lon", True)
        right = from_after(raw[:, :HALO], "lon", True)
        raw = circle(raw, right, left, 1)

    partial = lax.dot_general(
        basis, basis, (((0,), (0,)), ((), ())), preferred_element_type=f32
    )
    coef = conduct * (0.35 + 0.65 * land.astype(f32))
    edges = jnp.concatenate([coef[:HALO], coef[-HALO:]], axis=0)
    edges = jnp.pad(edges, ((0, 4), (0, width - wide)))
    partial, before, after = neighbours(partial, edges, "lat")
    partial = rest_of_ring(partial, "lat")
    before = jnp.where(top, 0.0, before[HALO : 2 * HALO, :wide])
    after = jnp.where(bottom, 0.0, after[:HALO, :wide])
    coef = jnp.concatenate([before, coef, after], axis=0)
    edges = jnp.concatenate([coef[:, :HALO], coef[:, -HALO:]], axis=1)
    edges = jnp.pad(edges, ((0, 4), (0, width - 2 * HALO)))
    partial, before, after = neighbours(partial, edges, "lon")
    rows = coef.shape[0]
    coef = circle(coef, after[:rows, :HALO], before[:rows, HALO : 2 * HALO], 1)
    gram = rest_of_ring(partial, "lon")
    inverse = factor_inverse(gram)
    across_down = weights(coef, width)
    ends = jnp.stack([top, bottom]).astype(i32)
    raw, inverse, across_down, ends = tied((raw, inverse, across_down, ends))

    north = from_before(raw[-HALO:], "lat", False)
    south = from_after(raw[:HALO], "lat", False)
    inner = inner_sweeps(raw, inverse, across_down)
    scale = cells / (width * SWEEPS)
    return outer_sweeps(scale, ends, north, south, inverse, inner, across_down, wide)


def solution(mesh):
    in_specs = (P(("lat", "lon"), None), P(("lat", "lon")), P("lat", "lon"), P("lat", "lon"))
    out_specs = P("lat", "lon")
    return jax.shard_map(
        per_device, mesh=mesh, in_specs=in_specs, out_specs=out_specs, check_vma=False
    )
```
